32 devices in a mesh: groups: 2 (over x), labels: 16 (over z, y, core).
Axes of the slice: x: 2, y: 2, z: 4, core: 2. Of those that a mesh axis runs over, the one named last changes fastest.
Arguments:
- embeddings: bfloat16 [32768, 768], P('labels'), may hold values from -6 to 6
- edge_tiles: bfloat16 [64, 2, 512, 512], P('labels'), may hold values from -0.1875 to 0.1875
- neighbour: int32 [64, 2], replicated, may hold values from 0 to 3, as said below
- propensity: float32 [32768], P('labels'), may hold values from 0.05 to 0.5
- queries: bfloat16 [512, 768], P('groups'), parts along dimension 0, may hold values from -6 to 6
- positives: int32 [512, 8], P('groups'), parts along dimension 0, may hold values from 0 to 32767
Outputs:
- grad_embed: bfloat16 [65536, 768], P(('groups', 'labels')), parts along dimension 0
- grad_queries: float32 [512, 768], P('groups'), parts along dimension 0
The draws below stay inside these ranges and needn't reach their ends.
There are 2 independent parts, one for each index of `groups`. The reference program is written for one: setup_inputs(seed, part) draws one part's arguments, and reference() takes and returns one part's arrays. A program takes and returns all parts, laid end to end along the dimension named above; an argument that names none is the same for every part. Nothing has to cross between parts.
Inputs may be any that keep to these rules, and one draw needn't show every extreme that they name: `neighbour`: on each side, the 4 blocks of one shard name exactly 2 distinct blocks of the neighbouring shard.
All inputs are finite; a program needn't handle non-finite values.
Results may differ from the reference program's by a relative error of at most 0.0059.
Values may be sent and summed in bfloat16 or wider, within the bound.
No kernel may reach another device: no remote copies, remote signals or barrier semaphores. Data moves between devices by JAX's collectives and lax.ppermute only.
A program may use at most 128 MiB of HBM per device.

```python
import math
import jax
import jax.numpy as jnp
import numpy as np
from jax import lax

D = 768
BLOCK = 512
BLOCKS_DEV = 4
NAMED = 2
QUERIES = 256
POSITIVES = 8
BLOCKS = 64
LABELS = 32768
N_LABELS = 16


def draw_neighbour(key, part):
    key = jax.random.fold_in(key, 11)
    keys = jax.random.split(key, 3)
    count = N_LABELS * 2
    named = jax.vmap(lambda k: jax.random.permutation(k, BLOCKS_DEV)[:NAMED])(jax.random.split(keys[0], count))
    ranks = jax.vmap(lambda k: jax.random.permutation(k, BLOCKS_DEV))(jax.random.split(keys[1], count))
    picks = jax.random.randint(keys[2], (count, BLOCKS_DEV), 0, NAMED)
    picks = jnp.where(ranks < NAMED, ranks, picks)
    chosen = jnp.take_along_axis(named, picks, axis=1)
    chosen = chosen.reshape(N_LABELS, 2, BLOCKS_DEV).transpose(0, 2, 1).reshape(BLOCKS, 2)
    return chosen.astype(jnp.int32)


def with_ends(drawn, rng, least, high):
    longest = drawn.shape.index(max(drawn.shape))
    spots = []
    for shift in (0, 1):
        where = [jax.random.randint(jax.random.fold_in(rng, axis), (), 0, length) for axis, length in enumerate(drawn.shape)]
        where[longest] = (where[longest] + shift) % drawn.shape[longest]
        spots.append(tuple(where))
    return drawn.at[spots[0]].set(least).at[spots[1]].set(high)


def steps_of(rng, dims, cuts, least, high):
    level = 1.0
    for position, blocks in cuts:
        draws = jax.random.uniform(jax.random.fold_in(jax.random.fold_in(rng, 6), position), (blocks,), jnp.float32, least / len(cuts), high / len(cuts))
        level = level * jnp.repeat(jnp.exp(draws), dims[position] // blocks).reshape((-1,) + (1,) * (len(dims) - 1 - position))
    return level


def rank_table(count, slope):
    loads = [(1 << 20) // math.isqrt(grade ** slope) + 1 for grade in range(1, count + 1)]
    deviation = 1 + sum(loads) // (1 << 30)
    return np.cumsum(np.array([max(1, weight // deviation) for weight in loads]))


def ranked_ids(stream_key, shape, count, slope):
    listing = rank_table(count, slope)
    lot = jax.random.randint(jax.random.fold_in(stream_key, 1), shape, 0, int(listing[count - 1]))
    grade = jnp.searchsorted(jnp.asarray(listing, jnp.int32), lot, side="right")
    return jax.random.permutation(jax.random.fold_in(stream_key, 2), count)[grade].astype(jnp.int32)


def centred(stream_key, shape, deviation, most, cuts=(), kind=jnp.bfloat16):
    drawn = jax.random.normal(stream_key, shape, jnp.float32) * deviation
    if len(cuts) > 0:
        drawn = steps_of(stream_key, shape, cuts, -0.22, 0.18) * drawn
    return jnp.clip(drawn, min=-most, max=most).astype(kind)


def setup_inputs(seed: int = 0, part: int = 0) -> dict:
    streams_of = jax.random.split(jax.random.key(seed), 7)
    part_splits = jax.random.split(jax.random.fold_in(streams_of[6], part), 7)
    return {
        "embeddings": centred(streams_of[0], (LABELS, D), 1.0, 6.0, ((0, 16),)),
        "edge_tiles": centred(streams_of[1], (BLOCKS, 2, BLOCK, BLOCK), (2 * BLOCK) ** -0.5, 0.1875, ((0, 16),)),
        "neighbour": draw_neighbour(jax.random.fold_in(streams_of[6], 71), part),
        "propensity": jnp.clip(jnp.exp(math.log(0.5) - 2.3025851 * jax.random.uniform(streams_of[3], (LABELS,), jnp.float32) ** steps_of(streams_of[3], (LABELS,), ((0, 16),), -0.2, 0.2)), 0.05, 0.5),
        "queries": centred(part_splits[4], (QUERIES, D), 1.0, 6.0),
        "positives": with_ends(ranked_ids(part_splits[5], (QUERIES, POSITIVES), LABELS, 2), jax.random.fold_in(part_splits[5], 3), 0, LABELS - 1).astype(jnp.int32),
    }


def reference(embeddings, edge_tiles, neighbour, propensity, queries, positives):
    blocks = embeddings.reshape(BLOCKS, BLOCK, D)
    owner = jnp.arange(BLOCKS, dtype=jnp.int32) // BLOCKS_DEV
    next_ids = (owner + 1) % N_LABELS * BLOCKS_DEV + neighbour[:, 0]
    prev_ids = (owner + N_LABELS - 1) % N_LABELS * BLOCKS_DEV + neighbour[:, 1]

    def hop(index):
        own = blocks[index].astype(jnp.float32)
        ahead = jnp.dot(edge_tiles[index, 0], blocks[next_ids[index]], preferred_element_type=jnp.float32)
        behind = jnp.dot(edge_tiles[index, 1], blocks[prev_ids[index]], preferred_element_type=jnp.float32)
        return (own + ahead + behind).astype(jnp.bfloat16)
    mixed = lax.map(hop, jnp.arange(BLOCKS, dtype=jnp.int32))
    weights = propensity.reshape(BLOCKS, BLOCK)

    def score(total, index):
        rows = mixed[index]
        scores = jnp.dot(queries, rows.T, preferred_element_type=jnp.float32) / math.sqrt(D)
        label_ids = index * BLOCK + jnp.arange(BLOCK, dtype=jnp.int32)
        hits = jnp.any(positives[:, :, None] == label_ids[None, None, :], axis=1).astype(jnp.float32)
        signal = (jax.nn.sigmoid(scores) - hits / weights[index][None, :]).astype(jnp.bfloat16)
        total = total + jnp.dot(signal, rows, preferred_element_type=jnp.float32)
        back = (jnp.dot(signal.T, queries, preferred_element_type=jnp.float32) / math.sqrt(QUERIES)).astype(jnp.bfloat16)
        return (total, back)
    start = jnp.zeros((QUERIES, D), jnp.float32)
    query_total, back = lax.scan(score, start, jnp.arange(BLOCKS, dtype=jnp.int32))
    grad_queries = query_total / math.sqrt(LABELS)
    marks = jnp.arange(BLOCKS_DEV, dtype=jnp.int32)

    def per_shard(shard):
        first = (shard * BLOCKS_DEV).astype(jnp.int32)
        rows = lax.dynamic_slice_in_dim(back, first, BLOCKS_DEV, 0).astype(jnp.float32)
        tiles = lax.dynamic_slice_in_dim(edge_tiles, first, BLOCKS_DEV, 0).astype(jnp.float32)
        lists = lax.dynamic_slice_in_dim(neighbour, first, BLOCKS_DEV, 0)
        push_next = jnp.einsum('bji,bjd->bid', tiles[:, 0], rows, precision=lax.Precision.HIGHEST)
        push_prev = jnp.einsum('bji,bjd->bid', tiles[:, 1], rows, precision=lax.Precision.HIGHEST)
        pick_next = (lists[:, 0][:, None] == marks[None, :]).astype(jnp.float32)
        pick_prev = (lists[:, 1][:, None] == marks[None, :]).astype(jnp.float32)
        to_next = jnp.einsum('bj,brd->jrd', pick_next, push_next, precision=lax.Precision.HIGHEST)
        to_prev = jnp.einsum('bj,brd->jrd', pick_prev, push_prev, precision=lax.Precision.HIGHEST)
        return (to_next.astype(jnp.bfloat16), to_prev.astype(jnp.bfloat16))
    to_next_all, to_prev_all = lax.map(per_shard, jnp.arange(N_LABELS, dtype=jnp.int32))
    carried_zero = jnp.roll(to_next_all, 1, axis=0).reshape(LABELS, D)
    carried_one = jnp.roll(to_prev_all, -1, axis=0).reshape(LABELS, D)
    grad_embed = (back.reshape(LABELS, D).astype(jnp.float32) + carried_zero.astype(jnp.float32) + carried_one.astype(jnp.float32)).astype(jnp.bfloat16)
    return (grad_embed, grad_queries)
```

```python
import functools
import math

import jax
import jax.numpy as jnp
from jax import lax
from jax.experimental import pallas as pl
from jax.experimental.pallas import tpu as pltpu
from jax.sharding import PartitionSpec as P

BF16 = jnp.bfloat16
F32 = jnp.float32
NT = (((1,), (1,)), ((), ()))
NN = (((1,), (0,)), ((), ()))
TN = (((0,), (0,)), ((), ()))
VMEM_BYTES = 48 * 1024 * 1024

NEXT_SLOT, PREV_SLOT, FOR_PREV, FOR_NEXT, CORE = 0, 4, 8, 10, 12


def dot(a, b, dims):
    return lax.dot_general(a, b, dims, preferred_element_type=F32)


def index_table(neighbour, device, count, blocks_dev):
    def lists(shard, side):
        column = neighbour[:, side]
        return lax.dynamic_slice_in_dim(column, shard * blocks_dev, blocks_dev, 0)

    own_next = lists(device, 0)
    own_prev = lists(device, 1)
    by_prev = lists((device + count - 1) % count, 0)
    by_next = lists((device + 1) % count, 1)
    return jnp.concatenate(
        [
            (own_next != jnp.min(own_next)).astype(jnp.int32),
            (own_prev != jnp.min(own_prev)).astype(jnp.int32),
            jnp.stack(
                [
                    jnp.min(by_prev),
                    jnp.max(by_prev),
                    jnp.min(by_next),
                    jnp.max(by_next),
                    device % 2,
                ]
            ),
        ]
    )


def project_kernel(table, queries, embeddings, own, for_prev, for_next, *, scale):
    c = pl.program_id(0)
    scores = dot(queries[...], embeddings[...], NT) * scale
    own[...] = scores
    rounded = scores.astype(BF16)
    for slot in range(2):

        @pl.when(table[FOR_PREV + slot] == c)
        def _():
            for_prev[slot] = rounded

        @pl.when(table[FOR_NEXT + slot] == c)
        def _():
            for_next[slot] = rounded


def signal_kernel(
    table, own, from_next, from_prev, tiles, positives, propensity, signal, to_next, to_prev, sum_next, sum_prev
):
    g = pl.program_id(0)
    block = own.shape[1]

    @pl.when(g == 0)
    def _():
        sum_next[...] = jnp.zeros_like(sum_next)
        sum_prev[...] = jnp.zeros_like(sum_prev)

    slot0 = table[NEXT_SLOT + g]
    slot1 = table[PREV_SLOT + g]
    scores = own[...] + dot(from_next[slot0], tiles[0, 0], NT) + dot(from_prev[slot1], tiles[0, 1], NT)
    first = table[CORE + 1] + g * block
    ids = lax.broadcasted_iota(jnp.int32, own.shape, 1)
    hits = jnp.zeros(own.shape, jnp.bool_)
    for column in range(positives.shape[1]):
        hits = jnp.logical_or(hits, ids == positives[:, column : column + 1] - first)
    inverse = 1.0 / propensity[...]
    value = jax.nn.sigmoid(scores) - jnp.where(hits, inverse, 0.0)
    value = value.astype(BF16)
    signal[...] = value
    sum_next[slot0] += dot(value, tiles[0, 0], NN)
    sum_prev[slot1] += dot(value, tiles[0, 1], NN)

    @pl.when(g == pl.num_programs(0) - 1)
    def _():
        to_next[...] = sum_next[...].astype(BF16)
        to_prev[...] = sum_prev[...].astype(BF16)


def gather_kernel(table, signal, before, after, embeddings, weight, kept, sent, total):
    c = pl.program_id(0)

    def carried(received, place):
        slot = (table[place + 1] == c).astype(jnp.int32)
        named = jnp.logical_or(table[place] == c, table[place + 1] == c)
        return jnp.where(named, received[slot].astype(F32), 0.0)

    value = signal[...].astype(F32) + carried(before, FOR_PREV) + carried(after, FOR_NEXT)
    value = value.astype(BF16)
    weight[...] = value
    part = dot(value, embeddings[...], NN)

    @pl.when(c == 0)
    def _():
        total[...] = part

    @pl.when(c != 0)
    def _():
        total[...] += part

    @pl.when(c == pl.num_programs(0) - 1)
    def _():
        rows = kept.shape[0]
        core = table[CORE]
        kept[...] = total[pl.ds(pl.multiple_of(core * rows, rows), rows), :]
        sent[...] = total[pl.ds(pl.multiple_of((1 - core) * rows, rows), rows), :]


def embed_kernel(weight, queries, out, *, scale):
    out[...] = (dot(weight[...], queries[...], TN) * scale).astype(BF16)


def whole(shape):
    return pl.BlockSpec(shape, lambda *_: (0,) * len(shape))


def call(kernel, name, grid, in_specs, out_specs, out_shape, scratch, prefetch, cost):
    return pl.pallas_call(
        kernel,
        grid_spec=pltpu.PrefetchScalarGridSpec(
            num_scalar_prefetch=prefetch,
            grid=grid,
            in_specs=in_specs,
            out_specs=out_specs,
            scratch_shapes=scratch,
        ),
        out_shape=out_shape,
        name=name,
        cost_estimate=pl.CostEstimate(flops=cost[0], bytes_accessed=cost[1], transcendentals=0),
        compiler_params=pltpu.CompilerParams(vmem_limit_bytes=VMEM_BYTES),
    )


def reduce_rows(kept, sent, scale):
    count = lax.axis_size("labels")
    chips = count // 2
    core = lax.axis_index("labels") % 2
    swap = [(i, i ^ 1) for i in range(count)]
    groups = [list(range(0, count, 2)), list(range(1, count, 2))]
    rows, width = kept.shape
    half = (kept + lax.ppermute(sent, "labels", swap)).astype(BF16)
    pieces = half.reshape(chips, rows // chips, width)
    pieces = lax.all_to_all(pieces, "labels", 0, 0, axis_index_groups=groups)
    total = (jnp.sum(pieces.astype(F32), axis=0) * scale).astype(BF16)
    spread = jnp.broadcast_to(total[None], pieces.shape)
    spread = lax.all_to_all(spread, "labels", 0, 0, axis_index_groups=groups)
    mine = spread.reshape(rows, width)
    other = lax.ppermute(mine, "labels", swap)
    first = jnp.where(core == 0, mine, other)
    second = jnp.where(core == 0, other, mine)
    return jnp.concatenate([first, second], axis=0).astype(F32)


def per_device(embeddings, edge_tiles, neighbour, propensity, queries, positives):
    count = lax.axis_size("labels")
    device = lax.axis_index("labels")
    blocks_dev, _, block, _ = edge_tiles.shape
    labels_dev, width = embeddings.shape
    rows = queries.shape[0]
    ahead = [(i, (i + 1) % count) for i in range(count)]
    behind = [((i + 1) % count, i) for i in range(count)]
    table = index_table(neighbour, device, count, blocks_dev)
    table = jnp.concatenate([table, (device * labels_dev).astype(jnp.int32)[None]])
    pair = jax.ShapeDtypeStruct((2, rows, block), BF16)
    by_columns = pl.BlockSpec((rows, block), lambda g, *_: (0, g))
    by_rows = pl.BlockSpec((block, width), lambda g, *_: (g, 0))
    product = 2 * rows * labels_dev * width
    mixing = 2 * rows * labels_dev * block

    own, for_prev, for_next = call(
        functools.partial(project_kernel, scale=1.0 / math.sqrt(width)),
        "project",
        (blocks_dev,),
        [whole((rows, width)), by_rows],
        [by_columns, whole(pair.shape), whole(pair.shape)],
        [jax.ShapeDtypeStruct((rows, labels_dev), F32), pair, pair],
        [],
        1,
        (product, 2 * labels_dev * width + 4 * rows * labels_dev),
    )(table, queries, embeddings)

    from_next = lax.ppermute(for_prev, "labels", behind)
    from_prev = lax.ppermute(for_next, "labels", ahead)

    signal, to_next, to_prev = call(
        signal_kernel,
        "signal",
        (blocks_dev,),
        [
            by_columns,
            whole(pair.shape),
            whole(pair.shape),
            pl.BlockSpec((1, 2, block, block), lambda g, *_: (g, 0, 0, 0)),
            whole(positives.shape),
            pl.BlockSpec((1, block), lambda g, *_: (0, g)),
        ],
        [by_columns, whole(pair.shape), whole(pair.shape)],
        [jax.ShapeDtypeStruct((rows, labels_dev), BF16), pair, pair],
        [pltpu.VMEM((2, rows, block), F32), pltpu.VMEM((2, rows, block), F32)],
        1,
        (4 * mixing, 4 * labels_dev * block + 6 * rows * labels_dev),
    )(table, own, from_next, from_prev, edge_tiles, positives, propensity.reshape(1, labels_dev))

    before = lax.ppermute(to_next, "labels", ahead)
    after = lax.ppermute(to_prev, "labels", behind)

    weight, kept, sent = call(
        gather_kernel,
        "gather",
        (blocks_dev,),
        [by_columns, whole(pair.shape), whole(pair.shape), by_rows],
        [by_columns, whole((rows // 2, width)), whole((rows // 2, width))],
        [jax.ShapeDtypeStruct((rows, labels_dev), BF16)]
        + [jax.ShapeDtypeStruct((rows // 2, width), F32)] * 2,
        [pltpu.VMEM((rows, width), F32)],
        1,
        (product, 2 * labels_dev * width + 4 * rows * labels_dev),
    )(table, signal, before, after, embeddings)

    grad_queries = reduce_rows(kept, sent, 1.0 / math.sqrt(labels_dev * count))

    grad_embed = call(
        functools.partial(embed_kernel, scale=1.0 / math.sqrt(rows)),
        "embed",
        (blocks_dev,),
        [by_columns, whole((rows, width))],
        by_rows,
        jax.ShapeDtypeStruct((labels_dev, width), BF16),
        [],
        0,
        (product, 2 * labels_dev * width + 2 * rows * labels_dev),
    )(weight, queries)
    return (grad_embed, grad_queries)


def solution(mesh):
    placed = (
        P("labels", None),
        P("labels", None, None, None),
        P(),
        P("labels"),
        P("groups", None),
        P("groups", None),
    )
    return jax.shard_map(
        per_device,
        mesh=mesh,
        in_specs=placed,
        out_specs=(P(("groups", "labels"), None), P("groups", None)),
        check_vma=False,
    )
```

```python
import functools
import math

import jax
import jax.numpy as jnp
from jax import lax
from jax.experimental import pallas as pl
from jax.experimental.pallas import tpu as pltpu
from jax.sharding import PartitionSpec as P

AXIS = "labels"
BF16 = jnp.bfloat16
F32 = jnp.float32
NT = (((1,), (1,)), ((), ()))
NN = (((1,), (0,)), ((), ()))
TN = (((0,), (0,)), ((), ()))
VMEM_BYTES = 16 * 1024 * 1024

OFF, ON = True, False


def dot(a, b, dims):
    return lax.dot_general(a, b, dims, preferred_element_type=F32)


def own_side(device, off):
    odd = device % 2
    return 1 - odd if off else odd


def partner_of(device, count, off):
    ahead = jnp.where(device == count - 1, 0, device + 1)
    behind = jnp.where(device == 0, count - 1, device - 1)
    return jnp.where(own_side(device, off) == 0, ahead, behind)


def own_list(lists, blocks, off):
    device = lax.axis_index(AXIS)
    side = own_side(device, off)
    return [lists[side, device * blocks + g] for g in range(blocks)]


def slots_of(lists, blocks, off):
    named = own_list(lists, blocks, off)
    least = functools.reduce(jnp.minimum, named)
    return [(value != least).astype(jnp.int32) for value in named]


def named_by_partner(lists, blocks, off):
    device = lax.axis_index(AXIS)
    partner = partner_of(device, lax.axis_size(AXIS), off)
    side = 1 - own_side(device, off)
    named = [lists[side, partner * blocks + g] for g in range(blocks)]
    return functools.reduce(jnp.minimum, named), functools.reduce(jnp.maximum, named)


def tile_side(off):
    return own_side(lax.axis_index(AXIS), off)


def block_rows(ref, index, block):
    return ref[pl.ds(pl.multiple_of(index * block, block), block), :]


def project_kernel(lists, queries, embeddings, *rest, off, scale):
    out, table, left, right, sem = rest[-5:]
    block = out.shape[2]
    blocks = embeddings.shape[0] // block
    fetches = [pltpu.make_async_copy(lists, table, sem.at[0]), pltpu.make_async_copy(queries, left, sem.at[1])]
    for g in range(blocks):
        fetches.append(pltpu.make_async_copy(embeddings.at[pl.ds(g * block, block), :], right.at[g], sem.at[2 + g]))
    for fetch in fetches:
        fetch.start()
    for fetch in fetches:
        fetch.wait()
    for slot, index in enumerate(named_by_partner(table, blocks, off)):
        out[slot] = (dot(left[...], right[index], NT) * scale).astype(BF16)


def hits_kernel(positives, propensity, out):
    blocks, rows, block = out.shape
    first = lax.axis_index(AXIS) * blocks * block
    ids = lax.broadcasted_iota(jnp.int32, (rows, block), 1)
    inverse = 1.0 / propensity[...]
    for g in range(blocks):
        hits = jnp.zeros((rows, block), jnp.bool_)
        for column in range(positives.shape[1]):
            hits = jnp.logical_or(hits, ids == positives[:, column : column + 1] - (first + g * block))
        out[g] = jnp.where(hits, inverse[:, g * block : (g + 1) * block], 0.0)


def base_kernel(lists, queries, embeddings, received, tiles, out, *, scale):
    blocks, _, block = out.shape
    side = tile_side(ON)
    for g, slot in enumerate(slots_of(lists, blocks, ON)):
        own = dot(queries[...], embeddings[g * block : (g + 1) * block, :], NT) * scale
        out[g] = own + dot(received[slot], tiles[g, side], NT)


def signal_kernel(lists, base, hits, received, tiles, signal, push, total):
    blocks = base.shape[0]
    side = tile_side(OFF)
    total[...] = jnp.zeros_like(total)
    for g, slot in enumerate(slots_of(lists, blocks, OFF)):
        scores = base[g] + dot(received[slot], tiles[g, side], NT)
        value = (jax.nn.sigmoid(scores) - hits[g]).astype(BF16)
        signal[g] = value
        total[slot] += dot(value, tiles[g, side], NN)
    push[...] = total[...].astype(BF16)


def push_kernel(lists, signal, tiles, push, total):
    blocks = signal.shape[0]
    side = tile_side(ON)
    total[...] = jnp.zeros_like(total)
    for g, slot in enumerate(slots_of(lists, blocks, ON)):
        total[slot] += dot(signal[g], tiles[g, side], NN)
    push[...] = total[...].astype(BF16)


def query_kernel(lists, signal, received, embeddings, out):
    blocks, _, block = signal.shape
    total = dot(signal[0], embeddings[0:block, :], NN)
    for g in range(1, blocks):
        total += dot(signal[g], embeddings[g * block : (g + 1) * block, :], NN)
    for slot, index in enumerate(named_by_partner(lists, blocks, ON)):
        total += dot(received[slot], block_rows(embeddings, index, block), NN)
    out[...] = total


def query_end_kernel(lists, part, received, embeddings, after, kept, sent, total, *, blocks):
    del after
    block = received.shape[2]
    first, second = named_by_partner(lists, blocks, OFF)
    total[...] = (
        part[...]
        + dot(received[0], block_rows(embeddings, first, block), NN)
        + dot(received[1], block_rows(embeddings, second, block), NN)
    )
    rows = kept.shape[0]
    core = lax.axis_index(AXIS) % 2
    kept[...] = total[pl.ds(pl.multiple_of(core * rows, rows), rows), :]
    sent[...] = total[pl.ds(pl.multiple_of((1 - core) * rows, rows), rows), :]


def embed_kernel(lists, signal, received, queries, out, held, total, ready, sem, *, scale):
    blocks, _, block = signal.shape
    for g in range(blocks):
        total[g] = dot(signal[g], queries[...], TN)
    for slot, index in enumerate(named_by_partner(lists, blocks, ON)):
        total[index] += dot(received[slot], queries[...], TN)
    copies = []
    for g in range(blocks):
        ready[g] = (total[g] * scale).astype(BF16)
        copies.append(pltpu.make_async_copy(ready.at[g], out.at[pl.ds(g * block, block), :], sem.at[g]))
        copies[-1].start()
    for slot, index in enumerate(named_by_partner(lists, blocks, OFF)):
        held[slot] = total[index]
    for copy in copies:
        copy.wait()


def embed_end_kernel(lists, held, received, queries, old, out, ready, sem, *, blocks, scale):
    del old
    block = ready.shape[1]
    copies = []
    for slot, index in enumerate(named_by_partner(lists, blocks, OFF)):
        ready[slot] = ((held[slot] + dot(received[slot], queries[...], TN)) * scale).astype(BF16)
        place = out.at[pl.ds(pl.multiple_of(index * block, block), block), :]
        copies.append(pltpu.make_async_copy(ready.at[slot], place, sem.at[slot]))
        copies[-1].start()
    for copy in copies:
        copy.wait()


VMEM = pl.BlockSpec(memory_space=pltpu.VMEM)
SMEM = pl.BlockSpec(memory_space=pltpu.SMEM)
ANY = pl.BlockSpec(memory_space=pl.ANY)
HBM = pl.BlockSpec(memory_space=pltpu.HBM)


def call(kernel, name, in_specs, out_shape, out_specs=None, scratch=(), aliases=None):
    if out_specs is None:
        out_specs = jax.tree.map(lambda _: VMEM, out_shape)
    return pl.pallas_call(
        kernel,
        in_specs=in_specs,
        out_specs=out_specs,
        out_shape=out_shape,
        scratch_shapes=scratch,
        input_output_aliases=aliases or {},
        name=name,
        cost_estimate=pl.CostEstimate(flops=0, bytes_accessed=0, transcendentals=0),
        compiler_params=pltpu.CompilerParams(vmem_limit_bytes=VMEM_BYTES),
    )


def digit_of(stride, radix):
    return (lax.axis_index(AXIS) // stride) % radix


def moved(i, stride, radix, step):
    digit = (i // stride) % radix
    return i + ((digit + step) % radix - digit) * stride


def exchange(value, stride, radix, step):
    count = lax.axis_size(AXIS)
    return lax.ppermute(value, AXIS, [(i, moved(i, stride, radix, step)) for i in range(count)])


def split_kernel(*refs, stride, radix, arrived):
    held, got = refs[0], refs[1 : 1 + arrived]
    kept, sent = refs[1 + arrived], refs[2 + arrived : 1 + arrived + radix]
    total = refs[-1]
    value = held[...]
    for ref in got:
        value = value + ref[...].astype(F32)
    total[...] = value
    rows = kept.shape[0]
    digit = digit_of(stride, radix)
    kept[...] = total[pl.ds(pl.multiple_of(digit * rows, rows), rows), :]
    for step, ref in enumerate(sent, 1):
        place = (digit + step) % radix
        ref[...] = total[pl.ds(pl.multiple_of(place * rows, rows), rows), :].astype(BF16)


def finish_kernel(*refs, scale):
    value = refs[0][...]
    for ref in refs[1:-1]:
        value = value + ref[...].astype(F32)
    refs[-1][...] = (value * scale).astype(BF16)


def join_kernel(*refs, stride, radix):
    pieces, out = refs[:-1], refs[-1]
    rows = pieces[0].shape[0]
    digit = digit_of(stride, radix)
    for step, ref in enumerate(pieces):
        place = (digit + radix - step) % radix
        out[pl.ds(pl.multiple_of(place * rows, rows), rows), :] = ref[...].astype(out.dtype)


def stages_of(count, rows):
    stages = []
    stride, radix = 2, 2
    while stride < count and count // stride % radix == 0 and rows % (16 * radix) == 0:
        stages.append((stride, radix))
        stride *= radix
        rows //= radix
        radix = 4 if radix == 2 else 2
    return stages


def sum_queries(kept, sent, scale):
    count = lax.axis_size(AXIS)
    rows, width = kept.shape
    stages = stages_of(count, rows)
    got = [exchange(sent, 1, 2, 1)]
    held = kept
    for stride, radix in stages:
        rows //= radix
        piece = jax.ShapeDtypeStruct((rows, width), F32)
        small = jax.ShapeDtypeStruct((rows, width), BF16)
        held, *parts = call(
            functools.partial(split_kernel, stride=stride, radix=radix, arrived=len(got)),
            "split",
            [VMEM] * (1 + len(got)),
            [piece] + [small] * (radix - 1),
            scratch=[pltpu.VMEM((rows * radix, width), F32)],
        )(held, *got)
        got = [exchange(part, stride, radix, step) for step, part in enumerate(parts, 1)]
    done = math.prod(radix for _, radix in stages) * 2
    if done < count:
        for ref in got:
            held = held + ref.astype(F32)
        groups = [list(range(first, count, done)) for first in range(done)]
        held, got = lax.psum(held, AXIS, axis_index_groups=groups), []
    value = call(
        functools.partial(finish_kernel, scale=scale),
        "finish",
        [VMEM] * (1 + len(got)),
        jax.ShapeDtypeStruct((rows, width), BF16),
    )(held, *got)
    for stride, radix in stages[::-1] + [(1, 2)]:
        pieces = [value] + [exchange(value, stride, radix, step) for step in range(1, radix)]
        rows *= radix
        value = call(
            functools.partial(join_kernel, stride=stride, radix=radix),
            "join",
            [VMEM] * radix,
            jax.ShapeDtypeStruct((rows, width), F32 if stride == 1 else BF16),
        )(*pieces)
    return value


def per_device(embeddings, edge_tiles, neighbour, propensity, queries, positives):
    count = lax.axis_size(AXIS)
    blocks, _, block, _ = edge_tiles.shape
    labels_dev, width = embeddings.shape
    rows = queries.shape[0]
    lists = neighbour.T
    odd = range(1, count, 2)
    off_route = [(i, (i + 1) % count) for i in odd] + [((i + 1) % count, i) for i in odd]

    def off_swap(value):
        return lax.ppermute(value, AXIS, off_route)

    def on_swap(value):
        return exchange(value, 1, 2, 1)

    pair = jax.ShapeDtypeStruct((2, rows, block), BF16)
    pair_sum = pltpu.VMEM((2, rows, block), F32)
    full = jax.ShapeDtypeStruct((blocks, rows, block), F32)
    scale = 1.0 / math.sqrt(width)

    def project(off, *after):
        return call(
            functools.partial(project_kernel, off=off, scale=scale),
            "project_off" if off else "project_on",
            [HBM] * 3 + [ANY] * len(after),
            pair,
            scratch=[
                pltpu.SMEM(lists.shape, jnp.int32),
                pltpu.VMEM((rows, width), BF16),
                pltpu.VMEM((blocks, block, width), BF16),
                pltpu.SemaphoreType.DMA((2 + blocks,)),
            ],
        )(*(pltpu.with_memory_space_constraint(x, pltpu.HBM) for x in (lists, queries, embeddings)), *after)

    for_off = project(OFF)
    from_off = off_swap(for_off)
    from_on = on_swap(project(ON, for_off))
    hits = call(
        hits_kernel, "hits", [VMEM, VMEM], full
    )(positives, propensity.reshape(1, labels_dev))
    base = call(
        functools.partial(base_kernel, scale=scale),
        "base",
        [SMEM] + [VMEM] * 4,
        full,
    )(lists, queries, embeddings, from_on, edge_tiles)
    signal, push_off = call(
        signal_kernel,
        "signal",
        [SMEM] + [VMEM] * 4,
        [jax.ShapeDtypeStruct(full.shape, BF16), pair],
        scratch=[pair_sum],
    )(lists, base, hits, from_off, edge_tiles)

    back_off = off_swap(push_off)
    push_on = call(
        push_kernel, "push", [SMEM, VMEM, VMEM], pair, scratch=[pair_sum]
    )(lists, signal, edge_tiles)
    back_on = on_swap(push_on)
    part = call(
        query_kernel,
        "query",
        [SMEM] + [VMEM] * 3,
        jax.ShapeDtypeStruct((rows, width), F32),
    )(lists, signal, back_on, embeddings)
    out, held = call(
        functools.partial(embed_kernel, scale=1.0 / math.sqrt(rows)),
        "embed",
        [SMEM] + [VMEM] * 3,
        [
            jax.ShapeDtypeStruct((labels_dev, width), BF16),
            jax.ShapeDtypeStruct((2, block, width), F32),
        ],
        out_specs=[ANY, VMEM],
        scratch=[
            pltpu.VMEM((blocks, block, width), F32),
            pltpu.VMEM((blocks, block, width), BF16),
            pltpu.SemaphoreType.DMA((blocks,)),
        ],
    )(lists, signal, back_on, queries)

    half = jax.ShapeDtypeStruct((rows // 2, width), F32)
    kept, sent = call(
        functools.partial(query_end_kernel, blocks=blocks),
        "query_end",
        [SMEM] + [VMEM] * 3 + [ANY],
        [half, half],
        scratch=[pltpu.VMEM((rows, width), F32)],
    )(lists, part, back_off, embeddings, held)
    grad_embed = call(
        functools.partial(embed_end_kernel, blocks=blocks, scale=1.0 / math.sqrt(rows)),
        "embed_end",
        [SMEM] + [VMEM] * 3 + [ANY],
        jax.ShapeDtypeStruct((labels_dev, width), BF16),
        out_specs=ANY,
        scratch=[pltpu.VMEM((2, block, width), BF16), pltpu.SemaphoreType.DMA((2,))],
        aliases={4: 0},
    )(lists, held, back_off, queries, out)
    grad_queries = sum_queries(kept, sent, 1.0 / math.sqrt(labels_dev * count))
    return (grad_embed, grad_queries)


def solution(mesh):
    placed = (
        P("labels", None),
        P("labels", None, None, None),
        P(),
        P("labels"),
        P("groups", None),
        P("groups", None),
    )
    return jax.shard_map(
        per_device,
        mesh=mesh,
        in_specs=placed,
        out_specs=(P(("groups", "labels"), None), P("groups", None)),
        check_vma=False,
    )
```

```python
import functools
import math

import jax
import jax.numpy as jnp
from jax import lax
from jax.experimental import pallas as pl
from jax.experimental.pallas import tpu as pltpu
from jax.sharding import PartitionSpec as P

AXIS = "labels"
BF16 = jnp.bfloat16
F32 = jnp.float32
NT = (((1,), (1,)), ((), ()))
NN = (((1,), (0,)), ((), ()))
TN = (((0,), (0,)), ((), ()))
VMEM_BYTES = 16 * 1024 * 1024

OFF, ON = True, False


def dot(a, b, dims):
    return lax.dot_general(a, b, dims, preferred_element_type=F32)


def own_side(device, off):
    odd = device % 2
    return 1 - odd if off else odd


def partner_of(device, count, off):
    ahead = jnp.where(device == count - 1, 0, device + 1)
    behind = jnp.where(device == 0, count - 1, device - 1)
    return jnp.where(own_side(device, off) == 0, ahead, behind)


def own_list(lists, blocks, off):
    device = lax.axis_index(AXIS)
    side = own_side(device, off)
    return [lists[side, device * blocks + g] for g in range(blocks)]


def slots_of(lists, blocks, off):
    named = own_list(lists, blocks, off)
    least = functools.reduce(jnp.minimum, named)
    return [(value != least).astype(jnp.int32) for value in named]


def named_by_partner(lists, blocks, off):
    device = lax.axis_index(AXIS)
    partner = partner_of(device, lax.axis_size(AXIS), off)
    side = 1 - own_side(device, off)
    named = [lists[side, partner * blocks + g] for g in range(blocks)]
    return functools.reduce(jnp.minimum, named), functools.reduce(jnp.maximum, named)


def tile_side(off):
    return own_side(lax.axis_index(AXIS), off)


def block_rows(ref, index, block):
    return ref[pl.ds(pl.multiple_of(index * block, block), block), :]


def project_kernel(lists, queries, embeddings, own, for_off, for_on, table, left, right, sem, *, scale):
    blocks, _, block = own.shape
    fetches = [pltpu.make_async_copy(lists, table, sem.at[0]), pltpu.make_async_copy(queries, left, sem.at[1])]
    for g in range(blocks):
        fetches.append(pltpu.make_async_copy(embeddings.at[pl.ds(g * block, block), :], right.at[g], sem.at[2 + g]))
    for fetch in fetches:
        fetch.start()
    for fetch in fetches[:2]:
        fetch.wait()
    for g in range(blocks):
        fetches[2 + g].wait()
        own[g] = dot(left[...], right[g], NT) * scale
    for out, off in ((for_off, OFF), (for_on, ON)):
        for slot, index in enumerate(named_by_partner(table, blocks, off)):
            out[slot] = own[index].astype(BF16)


def hits_kernel(positives, propensity, out):
    blocks, rows, block = out.shape
    first = lax.axis_index(AXIS) * blocks * block
    ids = lax.broadcasted_iota(jnp.int32, (rows, block), 1)
    inverse = 1.0 / propensity[...]
    for g in range(blocks):
        hits = jnp.zeros((rows, block), jnp.bool_)
        for column in range(positives.shape[1]):
            hits = jnp.logical_or(hits, ids == positives[:, column : column + 1] - (first + g * block))
        out[g] = jnp.where(hits, inverse[:, g * block : (g + 1) * block], 0.0)


def base_kernel(lists, own, received, tiles, out):
    blocks = out.shape[0]
    side = tile_side(ON)
    for g, slot in enumerate(slots_of(lists, blocks, ON)):
        out[g] = own[g] + dot(received[slot], tiles[g, side], NT)


def signal_kernel(lists, base, hits, received, tiles, signal, push, total):
    blocks = base.shape[0]
    side = tile_side(OFF)
    total[...] = jnp.zeros_like(total)
    for g, slot in enumerate(slots_of(lists, blocks, OFF)):
        scores = base[g] + dot(received[slot], tiles[g, side], NT)
        value = (jax.nn.sigmoid(scores) - hits[g]).astype(BF16)
        signal[g] = value
        total[slot] += dot(value, tiles[g, side], NN)
    push[...] = total[...].astype(BF16)


def push_kernel(lists, signal, tiles, push, total):
    blocks = signal.shape[0]
    other = lax.axis_index(AXIS) ^ 1
    side = own_side(other, ON)
    named = [lists[side, other * blocks + g] for g in range(blocks)]
    least = functools.reduce(jnp.minimum, named)
    total[...] = jnp.zeros_like(total)
    for g, value in enumerate(named):
        total[(value != least).astype(jnp.int32)] += dot(signal[g], tiles[g, side], NN)
    push[...] = total[...].astype(BF16)


def query_kernel(lists, signal, received, embeddings, out):
    blocks, _, block = signal.shape
    total = dot(signal[0], embeddings[0:block, :], NN)
    for g in range(1, blocks):
        total += dot(signal[g], embeddings[g * block : (g + 1) * block, :], NN)
    for slot, index in enumerate(named_by_partner(lists, blocks, ON)):
        total += dot(received[slot], block_rows(embeddings, index, block), NN)
    out[...] = total


def query_end_kernel(lists, part, received, embeddings, after, kept, sent, total, *, blocks, rows):
    del after
    block = received.shape[2]
    first, second = named_by_partner(lists, blocks, OFF)
    total[...] = (
        part[...]
        + dot(received[0], block_rows(embeddings, first, block), NN)
        + dot(received[1], block_rows(embeddings, second, block), NN)
    )
    core = lax.axis_index(AXIS) % 2
    for piece in range(kept.shape[0] // rows):
        place = pl.ds(piece * rows, rows)
        kept[place, :] = total[pl.ds(pl.multiple_of((2 * piece + core) * rows, rows), rows), :]
        sent[place, :] = total[pl.ds(pl.multiple_of((2 * piece + 1 - core) * rows, rows), rows), :]


def embed_kernel(lists, signal, received, queries, out, held, total, ready, sem, *, scale):
    blocks, _, block = signal.shape
    for g in range(blocks):
        total[g] = dot(signal[g], queries[...], TN)
    for slot, index in enumerate(named_by_partner(lists, blocks, ON)):
        total[index] += dot(received[slot], queries[...], TN)
    copies = []
    for g in range(blocks):
        ready[g] = (total[g] * scale).astype(BF16)
        copies.append(pltpu.make_async_copy(ready.at[g], out.at[pl.ds(g * block, block), :], sem.at[g]))
        copies[-1].start()
    for slot, index in enumerate(named_by_partner(lists, blocks, OFF)):
        held[slot] = total[index]
    for copy in copies:
        copy.wait()


def embed_end_kernel(lists, held, received, queries, old, out, ready, sem, *, blocks, scale):
    del old
    block = ready.shape[1]
    copies = []
    for slot, index in enumerate(named_by_partner(lists, blocks, OFF)):
        ready[slot] = ((held[slot] + dot(received[slot], queries[...], TN)) * scale).astype(BF16)
        place = out.at[pl.ds(pl.multiple_of(index * block, block), block), :]
        copies.append(pltpu.make_async_copy(ready.at[slot], place, sem.at[slot]))
        copies[-1].start()
    for copy in copies:
        copy.wait()


VMEM = pl.BlockSpec(memory_space=pltpu.VMEM)
SMEM = pl.BlockSpec(memory_space=pltpu.SMEM)
ANY = pl.BlockSpec(memory_space=pl.ANY)
HBM = pl.BlockSpec(memory_space=pltpu.HBM)


def call(kernel, name, in_specs, out_shape, out_specs=None, scratch=(), aliases=None):
    if out_specs is None:
        out_specs = jax.tree.map(lambda _: VMEM, out_shape)
    return pl.pallas_call(
        kernel,
        in_specs=in_specs,
        out_specs=out_specs,
        out_shape=out_shape,
        scratch_shapes=scratch,
        input_output_aliases=aliases or {},
        name=name,
        cost_estimate=pl.CostEstimate(flops=0, bytes_accessed=0, transcendentals=0),
        compiler_params=pltpu.CompilerParams(vmem_limit_bytes=VMEM_BYTES),
    )


def exchange(value, mask):
    count = lax.axis_size(AXIS)
    return lax.ppermute(value, AXIS, [(i, i ^ mask) for i in range(count)])


def finish_kernel(pieces, out, *, scale):
    value = pieces[0].astype(F32)
    for i in range(1, pieces.shape[0]):
        value = value + pieces[i].astype(F32)
    out[...] = (value * scale).astype(BF16)


def piece_rows(count, rows):
    return rows // count if rows % (16 * count) == 0 else 16


def sum_queries(kept, sent, scale):
    count = lax.axis_size(AXIS)
    rows, width = kept.shape
    chips = count // 2
    groups = [list(range(core, count, 2)) for core in range(2)]
    half = kept + exchange(sent, 1)
    step = piece_rows(count, 2 * rows)
    if step * chips != rows:
        half = lax.psum(half, AXIS, axis_index_groups=groups) * scale
        both = jnp.stack([half, exchange(half, 1)]).reshape(2, rows // step, step, width)
        both = jnp.where(lax.axis_index(AXIS) % 2 == 0, both, both[::-1])
        return both.swapaxes(0, 1).reshape(2 * rows, width)
    half = half.astype(BF16).reshape(chips, step, width)
    pieces = lax.all_to_all(half, AXIS, 0, 0, axis_index_groups=groups)
    piece = call(
        functools.partial(finish_kernel, scale=scale),
        "finish",
        [VMEM],
        jax.ShapeDtypeStruct((step, width), BF16),
    )(pieces)
    return lax.all_gather(piece, AXIS, axis=0, tiled=True).astype(F32)


def per_device(embeddings, edge_tiles, neighbour, propensity, queries, positives):
    count = lax.axis_size(AXIS)
    blocks, _, block, _ = edge_tiles.shape
    labels_dev, width = embeddings.shape
    rows = queries.shape[0]
    lists = neighbour.T
    odd = range(1, count, 2)
    off_route = [(i, (i + 1) % count) for i in odd] + [((i + 1) % count, i) for i in odd]

    def off_swap(value):
        return lax.ppermute(value, AXIS, off_route)

    def on_swap(value):
        return exchange(value, 1)

    pair = jax.ShapeDtypeStruct((2, rows, block), BF16)
    pair_sum = pltpu.VMEM((2, rows, block), F32)
    full = jax.ShapeDtypeStruct((blocks, rows, block), F32)
    scale = 1.0 / math.sqrt(width)

    own, for_off, for_on = call(
        functools.partial(project_kernel, scale=scale),
        "project",
        [HBM] * 3,
        [full, pair, pair],
        scratch=[
            pltpu.SMEM(lists.shape, jnp.int32),
            pltpu.VMEM((rows, width), BF16),
            pltpu.VMEM((blocks, block, width), BF16),
            pltpu.SemaphoreType.DMA((2 + blocks,)),
        ],
    )(*(pltpu.with_memory_space_constraint(x, pltpu.HBM) for x in (lists, queries, embeddings)))
    from_off = off_swap(for_off)
    from_on = on_swap(for_on)
    other_tiles = on_swap(edge_tiles)
    hits = call(
        hits_kernel, "hits", [VMEM, VMEM], full
    )(positives, propensity.reshape(1, labels_dev))
    base = call(base_kernel, "base", [SMEM] + [VMEM] * 3, full)(lists, own, from_on, edge_tiles)
    signal, push_off = call(
        signal_kernel,
        "signal",
        [SMEM] + [VMEM] * 4,
        [jax.ShapeDtypeStruct(full.shape, BF16), pair],
        scratch=[pair_sum],
    )(lists, base, hits, from_off, edge_tiles)

    back_off = off_swap(push_off)
    other_signal = on_swap(signal)
    back_on = call(push_kernel, "push", [SMEM, VMEM, VMEM], pair, scratch=[pair_sum])(
        lists, other_signal, other_tiles
    )
    part = call(
        query_kernel,
        "query",
        [SMEM] + [VMEM] * 3,
        jax.ShapeDtypeStruct((rows, width), F32),
    )(lists, signal, back_on, embeddings)
    out, held = call(
        functools.partial(embed_kernel, scale=1.0 / math.sqrt(rows)),
        "embed",
        [SMEM] + [VMEM] * 3,
        [
            jax.ShapeDtypeStruct((labels_dev, width), BF16),
            jax.ShapeDtypeStruct((2, block, width), F32),
        ],
        out_specs=[ANY, VMEM],
        scratch=[
            pltpu.VMEM((blocks, block, width), F32),
            pltpu.VMEM((blocks, block, width), BF16),
            pltpu.SemaphoreType.DMA((blocks,)),
        ],
    )(lists, signal, back_on, queries)

    half = jax.ShapeDtypeStruct((rows // 2, width), F32)
    kept, sent = call(
        functools.partial(query_end_kernel, blocks=blocks, rows=piece_rows(count, rows)),
        "query_end",
        [SMEM] + [VMEM] * 3 + [ANY],
        [half, half],
        scratch=[pltpu.VMEM((rows, width), F32)],
    )(lists, part, back_off, embeddings, held)
    grad_embed = call(
        functools.partial(embed_end_kernel, blocks=blocks, scale=1.0 / math.sqrt(rows)),
        "embed_end",
        [SMEM] + [VMEM] * 3 + [ANY],
        jax.ShapeDtypeStruct((labels_dev, width), BF16),
        out_specs=ANY,
        scratch=[pltpu.VMEM((2, block, width), BF16), pltpu.SemaphoreType.DMA((2,))],
        aliases={4: 0},
    )(lists, held, back_off, queries, out)
    grad_queries = sum_queries(kept, sent, 1.0 / math.sqrt(labels_dev * count))
    return (grad_embed, grad_queries)


def solution(mesh):
    placed = (
        P("labels", None),
        P("labels", None, None, None),
        P(),
        P("labels"),
        P("groups", None),
        P("groups", None),
    )
    return jax.shard_map(
        per_device,
        mesh=mesh,
        in_specs=placed,
        out_specs=(P(("groups", "labels"), None), P("groups", None)),
        check_vma=False,
    )
```

```python
import functools
import math

import jax
import jax.numpy as jnp
from jax import lax
from jax.experimental import pallas as pl
from jax.experimental.pallas import tpu as pltpu
from jax.sharding import PartitionSpec as P

AXIS = "labels"
BF16 = jnp.bfloat16
F32 = jnp.float32
NT = (((1,), (1,)), ((), ()))
NN = (((1,), (0,)), ((), ()))
TN = (((0,), (0,)), ((), ()))
MIB = 1024 * 1024

OFF, ON = True, False


def dot(a, b, dims):
    return lax.dot_general(a, b, dims, preferred_element_type=F32)


def own_side(device, off):
    odd = device % 2
    return 1 - odd if off else odd


def partner_of(device, count, off):
    ahead = jnp.where(device == count - 1, 0, device + 1)
    behind = jnp.where(device == 0, count - 1, device - 1)
    return jnp.where(own_side(device, off) == 0, ahead, behind)


def own_list(lists, blocks, off):
    device = lax.axis_index(AXIS)
    side = own_side(device, off)
    return [lists[side, device * blocks + g] for g in range(blocks)]


def slots_of(lists, blocks, off):
    named = own_list(lists, blocks, off)
    least = functools.reduce(jnp.minimum, named)
    return [(value != least).astype(jnp.int32) for value in named]


def named_by_partner(lists, blocks, off):
    device = lax.axis_index(AXIS)
    partner = partner_of(device, lax.axis_size(AXIS), off)
    side = 1 - own_side(device, off)
    named = [lists[side, partner * blocks + g] for g in range(blocks)]
    return functools.reduce(jnp.minimum, named), functools.reduce(jnp.maximum, named)


def tile_side(off):
    return own_side(lax.axis_index(AXIS), off)


def block_rows(ref, index, block):
    return ref[pl.ds(pl.multiple_of(index * block, block), block), :]


def project_kernel(lists, queries, embeddings, own, for_off_a, for_off_b, for_on, table, left, right, sem, *, scale):
    blocks, _, block = own.shape
    half = for_off_a.shape[1]
    fetches = [pltpu.make_async_copy(lists, table, sem.at[0]), pltpu.make_async_copy(queries, left, sem.at[1])]
    for g in range(blocks):
        fetches.append(pltpu.make_async_copy(embeddings.at[pl.ds(g * block, block), :], right.at[g], sem.at[2 + g]))
    for fetch in fetches:
        fetch.start()
    for fetch in fetches[:2]:
        fetch.wait()
    for g in range(blocks):
        fetches[2 + g].wait()
        own[g] = dot(left[...], right[g], NT) * scale
    for slot, index in enumerate(named_by_partner(table, blocks, OFF)):
        for_off_a[slot] = own[index, :half].astype(BF16)
        for_off_b[slot] = own[index, half:].astype(BF16)
    for slot, index in enumerate(named_by_partner(table, blocks, ON)):
        for_on[slot] = own[index].astype(BF16)


def hits_kernel(positives, propensity, out):
    blocks, rows, block = out.shape
    first = lax.axis_index(AXIS) * blocks * block
    ids = lax.broadcasted_iota(jnp.int32, (rows, block), 1)
    inverse = 1.0 / propensity[...]
    for g in range(blocks):
        hits = jnp.zeros((rows, block), jnp.bool_)
        for column in range(positives.shape[1]):
            hits = jnp.logical_or(hits, ids == positives[:, column : column + 1] - (first + g * block))
        out[g] = jnp.where(hits, inverse[:, g * block : (g + 1) * block], 0.0)


def base_kernel(lists, own, received, tiles, out):
    blocks = out.shape[0]
    side = tile_side(ON)
    for g, slot in enumerate(slots_of(lists, blocks, ON)):
        out[g] = own[g] + dot(received[slot], tiles[g, side], NT)


def signal_kernel(lists, base, hits, received, tiles, *rest, first):
    signal, push_off, push_on, total_off, total_on = rest[-5:]
    blocks = base.shape[0]
    rows = slice(first, first + received.shape[1])
    side_off, side_on = tile_side(OFF), tile_side(ON)
    slots_on = slots_of(lists, blocks, ON)
    total_off[...] = jnp.zeros_like(total_off)
    total_on[...] = jnp.zeros_like(total_on)
    for g, slot in enumerate(slots_of(lists, blocks, OFF)):
        scores = base[g, rows] + dot(received[slot], tiles[g, side_off], NT)
        value = (jax.nn.sigmoid(scores) - hits[g, rows]).astype(BF16)
        signal[g, rows] = value
        total_off[slot] += dot(value, tiles[g, side_off], NN)
        total_on[slots_on[g]] += dot(value, tiles[g, side_on], NN)
    push_off[...] = total_off[...].astype(BF16)
    push_on[...] = total_on[...].astype(BF16)


def query_kernel(signal, embeddings, out):
    blocks, _, block = signal.shape
    total = dot(signal[0], embeddings[0:block, :], NN)
    for g in range(1, blocks):
        total += dot(signal[g], embeddings[g * block : (g + 1) * block, :], NN)
    out[...] = total


def query_on_kernel(lists, received_a, received_b, embeddings, after, out, *, blocks):
    del after
    half, block = received_a.shape[1:]
    first, second = named_by_partner(lists, blocks, ON)
    left, right = block_rows(embeddings, first, block), block_rows(embeddings, second, block)
    for rows, received in ((slice(0, half), received_a), (slice(half, 2 * half), received_b)):
        out[rows, :] = dot(received[0], left, NN) + dot(received[1], right, NN)


def query_half_kernel(lists, part, received, embeddings, after, out, *, blocks):
    del after
    half, block = received.shape[1:]
    first, second = named_by_partner(lists, blocks, OFF)
    left, right = block_rows(embeddings, first, block), block_rows(embeddings, second, block)
    out[...] = part[:half, :] + dot(received[0], left, NN) + dot(received[1], right, NN)


def query_end_kernel(lists, part, part_on, received, embeddings, other, kept, sent, *, blocks):
    half, block = received.shape[1:]
    first, second = named_by_partner(lists, blocks, OFF)
    left, right = block_rows(embeddings, first, block), block_rows(embeddings, second, block)
    value = part[half:, :] + part_on[half:, :] + dot(received[0], left, NN) + dot(received[1], right, NN)
    above = other[...] + part_on[:half, :]
    upper = lax.axis_index(AXIS) % 2 == 0
    kept[...] = jnp.where(upper, above, value)
    sent[...] = jnp.where(upper, value, above)


def embed_kernel(signal, queries, out):
    for g in range(signal.shape[0]):
        out[g] = dot(signal[g], queries[...], TN)


def embed_end_kernel(lists, part, on_a, on_b, off_a, off_b, queries, *rest, blocks, first, last, scale):
    out, token, total, ready, sem = rest[-5:]
    block = part.shape[1]
    half = off_a.shape[1]
    token[...] = jnp.zeros_like(token)
    for g in range(first, last):
        total[g - first] = part[g]
    for slot, index in enumerate(named_by_partner(lists, blocks, ON)):

        @pl.when(jnp.logical_and(index >= first, index < last))
        def _():
            total[index - first] += dot(on_a[slot], queries[:half, :], TN) + dot(on_b[slot], queries[half:, :], TN)

    for slot, index in enumerate(named_by_partner(lists, blocks, OFF)):

        @pl.when(jnp.logical_and(index >= first, index < last))
        def _():
            total[index - first] += dot(off_a[slot], queries[:half, :], TN) + dot(off_b[slot], queries[half:, :], TN)

    copies = []
    for g in range(first, last):
        ready[g - first] = (total[g - first] * scale).astype(BF16)
        place = out.at[pl.ds(g * block, block), :]
        copies.append(pltpu.make_async_copy(ready.at[g - first], place, sem.at[g - first]))
        copies[-1].start()
    for copy in copies:
        copy.wait()


VMEM = pl.BlockSpec(memory_space=pltpu.VMEM)
SMEM = pl.BlockSpec(memory_space=pltpu.SMEM)
ANY = pl.BlockSpec(memory_space=pl.ANY)
HBM = pl.BlockSpec(memory_space=pltpu.HBM)


def call(kernel, name, in_specs, out_shape, out_specs=None, scratch=(), aliases=None, vmem=12, flops=0):
    if out_specs is None:
        out_specs = jax.tree.map(lambda _: VMEM, out_shape)
    return pl.pallas_call(
        kernel,
        in_specs=in_specs,
        out_specs=out_specs,
        out_shape=out_shape,
        scratch_shapes=scratch,
        input_output_aliases=aliases or {},
        name=name,
        cost_estimate=pl.CostEstimate(flops=flops, bytes_accessed=0, transcendentals=0),
        compiler_params=pltpu.CompilerParams(vmem_limit_bytes=vmem * MIB),
    )


def exchange(value, mask):
    count = lax.axis_size(AXIS)
    return lax.ppermute(value, AXIS, [(i, i ^ mask) for i in range(count)])


def halve_kernel(held, got, kept, sent, *, bit):
    rows = kept.shape[0]
    digit = (lax.axis_index(AXIS) // bit) % 2
    here = pl.ds(pl.multiple_of(digit * rows, rows), rows)
    there = pl.ds(pl.multiple_of((1 - digit) * rows, rows), rows)
    kept[...] = held[here, :] + got[here, :]
    sent[...] = (held[there, :] + got[there, :]).astype(BF16)


def add_kernel(held, got, *rest, scale):
    rest[-1][...] = ((held[...].astype(F32) + got[...].astype(F32)) * scale).astype(BF16)


def join_kernel(held, got, out, *, bit):
    rows = held.shape[0]
    digit = (lax.axis_index(AXIS) // bit) % 2
    out[pl.ds(pl.multiple_of(digit * rows, rows), rows), :] = held[...].astype(out.dtype)
    out[pl.ds(pl.multiple_of((1 - digit) * rows, rows), rows), :] = got[...].astype(out.dtype)


def sum_queries(kept, sent, beside, scale):
    count = lax.axis_size(AXIS)
    rows, width = kept.shape
    got = exchange(sent, 1)
    if count & (count - 1) or count < 4:
        half = lax.psum(kept + got, AXIS, axis_index_groups=[list(range(c, count, 2)) for c in range(2)])
        both = jnp.stack([half, exchange(half, 1)])
        both = jnp.where(lax.axis_index(AXIS) % 2 == 0, both, both[::-1])
        return both.reshape(2 * rows, width) * scale
    piece = jax.ShapeDtypeStruct((rows // 2, width), BF16)
    held, sent = call(
        functools.partial(halve_kernel, bit=2),
        "halve",
        [VMEM] * 2,
        [jax.ShapeDtypeStruct(piece.shape, F32), piece],
    )(kept, got)
    got = exchange(sent, 2)
    bits = [1 << k for k in range(2, count.bit_length() - 1)]
    for k in range(len(bits) + 1):
        last = k == len(bits)
        after = beside[k : k + 1]
        held = call(
            functools.partial(add_kernel, scale=scale if last else 1.0),
            "add",
            [VMEM] * 2 + [ANY] * len(after),
            piece,
        )(held, got, *after)
        if not last:
            got = exchange(held, bits[k])
    for bit in (2, 1):
        rows_out = held.shape[0] * 2
        held = call(
            functools.partial(join_kernel, bit=bit),
            "join",
            [VMEM] * 2,
            jax.ShapeDtypeStruct((rows_out, width), F32 if bit == 1 else BF16),
        )(held, exchange(held, bit))
    return held


def per_device(embeddings, edge_tiles, neighbour, propensity, queries, positives):
    count = lax.axis_size(AXIS)
    blocks, _, block, _ = edge_tiles.shape
    labels_dev, width = embeddings.shape
    rows = queries.shape[0]
    lists = neighbour.T
    odd = range(1, count, 2)
    off_route = [(i, (i + 1) % count) for i in odd] + [((i + 1) % count, i) for i in odd]

    def off_swap(value):
        return lax.ppermute(value, AXIS, off_route)

    def on_swap(value):
        return exchange(value, 1)

    pair = jax.ShapeDtypeStruct((2, rows, block), BF16)
    pair_sum = pltpu.VMEM((2, rows, block), F32)
    full = jax.ShapeDtypeStruct((blocks, rows, block), F32)
    scale = 1.0 / math.sqrt(width)

    half = jax.ShapeDtypeStruct((2, rows // 2, block), BF16)
    own, for_off_a, for_off_b, for_on = call(
        functools.partial(project_kernel, scale=scale),
        "project",
        [HBM] * 3,
        [full, half, half, pair],
        scratch=[
            pltpu.SMEM(lists.shape, jnp.int32),
            pltpu.VMEM((rows, width), BF16),
            pltpu.VMEM((blocks, block, width), BF16),
            pltpu.SemaphoreType.DMA((2 + blocks,)),
        ],
        vmem=12,
    )(*(pltpu.with_memory_space_constraint(x, pltpu.HBM) for x in (lists, queries, embeddings)))
    from_off_a = off_swap(for_off_a)
    from_off_b = off_swap(for_off_b)
    from_on = on_swap(for_on)
    hits = call(hits_kernel, "hits", [VMEM, VMEM], full)(positives, propensity.reshape(1, labels_dev))
    base = call(base_kernel, "base", [SMEM] + [VMEM] * 3, full)(lists, own, from_on, edge_tiles)

    def signal_of(received, first, *begun):
        return call(
            functools.partial(signal_kernel, first=first),
            "signal",
            [SMEM] + [VMEM] * 4 + [ANY] * len(begun),
            [jax.ShapeDtypeStruct(full.shape, BF16), half, half],
            scratch=[pltpu.VMEM(half.shape, F32)] * 2,
            aliases={5: 0} if begun else None,
        )(lists, base, hits, received, edge_tiles, *begun)

    signal, push_a, push_on_a = signal_of(from_off_a, 0)
    back_a = off_swap(push_a)
    signal, push_b, push_on_b = signal_of(from_off_b, rows // 2, signal)
    back_b = off_swap(push_b)
    on_a, on_b = on_swap(push_on_a), on_swap(push_on_b)
    part = call(query_kernel, "query", [VMEM] * 2, jax.ShapeDtypeStruct((rows, width), F32))(signal, embeddings)
    embed = call(embed_kernel, "embed", [VMEM] * 2, jax.ShapeDtypeStruct((blocks, block, width), F32))(
        signal, queries
    )
    piece = jax.ShapeDtypeStruct((rows // 2, width), F32)
    upper = call(
        functools.partial(query_half_kernel, blocks=blocks), "query_half", [SMEM] + [VMEM] * 3 + [ANY], piece, flops=10**9
    )(lists, part, back_a, embeddings, embed)
    part_on = call(
        functools.partial(query_on_kernel, blocks=blocks),
        "query_on",
        [SMEM] + [VMEM] * 3 + [ANY],
        jax.ShapeDtypeStruct((rows, width), F32),
    )(lists, on_a, on_b, embeddings, upper)
    kept, sent = call(
        functools.partial(query_end_kernel, blocks=blocks), "query_end", [SMEM] + [VMEM] * 5, [piece, piece]
    )(lists, part, part_on, back_b, embeddings, upper)

    def embed_end(first, last, *begun):
        return call(
            functools.partial(
                embed_end_kernel, blocks=blocks, first=first, last=last, scale=1.0 / math.sqrt(rows)
            ),
            "embed_end",
            [SMEM] + [VMEM] * 6 + [ANY] * len(begun),
            [jax.ShapeDtypeStruct((labels_dev, width), BF16), jax.ShapeDtypeStruct((8, 128), F32)],
            out_specs=[ANY, VMEM],
            scratch=[
                pltpu.VMEM((last - first, block, width), F32),
                pltpu.VMEM((last - first, block, width), BF16),
                pltpu.SemaphoreType.DMA((last - first,)),
            ],
            aliases={7: 0} if begun else None,
            vmem=16,
        )(lists, embed, on_a, on_b, back_a, back_b, queries, *begun)

    begun, token_a = embed_end(0, blocks // 2)
    grad_embed, token_b = embed_end(blocks // 2, blocks, begun)
    grad_queries = sum_queries(kept, sent, [token_a, token_b], 1.0 / math.sqrt(labels_dev * count))
    return (grad_embed, grad_queries)


def solution(mesh):
    placed = (
        P("labels", None),
        P("labels", None, None, None),
        P(),
        P("labels"),
        P("groups", None),
        P("groups", None),
    )
    return jax.shard_map(
        per_device,
        mesh=mesh,
        in_specs=placed,
        out_specs=(P(("groups", "labels"), None), P("groups", None)),
        check_vma=False,
    )
```

```python
import functools
import math

import jax
import jax.numpy as jnp
from jax import lax
from jax.experimental import pallas as pl
from jax.experimental.pallas import tpu as pltpu
from jax.sharding import PartitionSpec as P

AXIS = "labels"
BF16 = jnp.bfloat16
F32 = jnp.float32
NT = (((1,), (1,)), ((), ()))
NN = (((1,), (0,)), ((), ()))
TN = (((0,), (0,)), ((), ()))
MIB = 1024 * 1024

OFF, ON = True, False


def dot(a, b, dims):
    return lax.dot_general(a, b, dims, preferred_element_type=F32)


def own_side(device, off):
    odd = device % 2
    return 1 - odd if off else odd


def partner_of(device, count, off):
    ahead = jnp.where(device == count - 1, 0, device + 1)
    behind = jnp.where(device == 0, count - 1, device - 1)
    return jnp.where(own_side(device, off) == 0, ahead, behind)


def own_list(lists, blocks, off):
    device = lax.axis_index(AXIS)
    side = own_side(device, off)
    return [lists[side, device * blocks + g] for g in range(blocks)]


def slots_of(lists, blocks, off):
    named = own_list(lists, blocks, off)
    least = functools.reduce(jnp.minimum, named)
    return [(value != least).astype(jnp.int32) for value in named]


def named_by_partner(lists, blocks, off):
    device = lax.axis_index(AXIS)
    partner = partner_of(device, lax.axis_size(AXIS), off)
    side = 1 - own_side(device, off)
    named = [lists[side, partner * blocks + g] for g in range(blocks)]
    return functools.reduce(jnp.minimum, named), functools.reduce(jnp.maximum, named)


def tile_side(off):
    return own_side(lax.axis_index(AXIS), off)


def block_rows(ref, index, block):
    return ref[pl.ds(pl.multiple_of(index * block, block), block), :]


def project_kernel(lists, queries, embeddings, own, off_a, off_b, for_on, left, right, table, sem, *, scale):
    blocks, _, block = own.shape
    fetches = [pltpu.make_async_copy(lists, table, sem.at[0]), pltpu.make_async_copy(queries, left, sem.at[1])]
    for g in range(blocks):
        rows = pl.ds(g * block, block)
        fetches.append(pltpu.make_async_copy(embeddings.at[rows, :], right.at[rows, :], sem.at[2 + g]))
    for fetch in fetches:
        fetch.start()
    for fetch in fetches[:2]:
        fetch.wait()
    for g in range(blocks):
        fetches[2 + g].wait()
        own[g] = dot(left[...], right[g * block : (g + 1) * block, :], NT) * scale
    for out, index in zip((off_a, off_b), named_by_partner(table, blocks, OFF)):
        out[...] = own[index].astype(BF16)
    for slot, index in enumerate(named_by_partner(table, blocks, ON)):
        for_on[slot] = own[index].astype(BF16)


def hits_kernel(positives, tiles, out, kept, sem):
    fetch = pltpu.make_async_copy(tiles, kept, sem)
    fetch.start()
    blocks, rows, block = out.shape
    first = lax.axis_index(AXIS) * blocks * block
    ids = lax.broadcasted_iota(jnp.int32, (rows, block), 1)
    for g in range(blocks):
        hits = jnp.zeros((rows, block), jnp.bool_)
        for column in range(positives.shape[1]):
            hits = jnp.logical_or(hits, ids == positives[:, column : column + 1] - (first + g * block))
        out[g] = jnp.where(hits, 1.0, 0.0).astype(BF16)
    fetch.wait()


def base_kernel(lists, own, received, tiles, out):
    blocks = out.shape[0]
    side = tile_side(ON)
    for g, slot in enumerate(slots_of(lists, blocks, ON)):
        out[g] = own[g] + dot(received[slot], tiles[g, side], NT)


def signal_kernel(lists, base, hits, propensity, received, tiles, *rest, slot):
    if slot == 0:
        signal, push, carry, total, total_on = rest
        total_on[...] = jnp.zeros_like(total_on)
    else:
        _, before, signal, push, push_on_a, push_on_b, total, total_on = rest
        total_on[...] = before[...]
    blocks, _, block = base.shape
    side_off, side_on = tile_side(OFF), tile_side(ON)
    slots_on = slots_of(lists, blocks, ON)
    total[...] = jnp.zeros_like(total)
    for g, taken in enumerate(slots_of(lists, blocks, OFF)):

        @pl.when(taken == slot)
        def _():
            scores = base[g] + dot(received[...], tiles[g, side_off], NT)
            inverse = 1.0 / propensity[:, g * block : (g + 1) * block]
            value = (jax.nn.sigmoid(scores) - hits[g].astype(F32) * inverse).astype(BF16)
            signal[g] = value
            total[...] += dot(value, tiles[g, side_off], NN)
            total_on[slots_on[g]] += dot(value, tiles[g, side_on], NN)

    push[...] = total[...].astype(BF16)
    if slot == 0:
        carry[...] = total_on[...]
    else:
        push_on_a[...] = total_on[0].astype(BF16)
        push_on_b[...] = total_on[1].astype(BF16)


def query_kernel(signal, embeddings, out):
    blocks, _, block = signal.shape
    total = dot(signal[0], embeddings[0:block, :], NN)
    for g in range(1, blocks):
        total += dot(signal[g], embeddings[g * block : (g + 1) * block, :], NN)
    out[...] = total


def query_half_kernel(lists, part, received, embeddings, after, out, *, blocks):
    del after
    first, _ = named_by_partner(lists, blocks, OFF)
    out[...] = part[...] + dot(received[...], block_rows(embeddings, first, received.shape[1]), NN)


def query_on_kernel(lists, part, received_a, received_b, embeddings, out, *, blocks):
    block = received_a.shape[1]
    first, second = named_by_partner(lists, blocks, ON)
    out[...] = (
        part[...]
        + dot(received_a[...], block_rows(embeddings, first, block), NN)
        + dot(received_b[...], block_rows(embeddings, second, block), NN)
    )


def query_end_kernel(lists, part, received, embeddings, kept, sent, total, *, blocks):
    _, second = named_by_partner(lists, blocks, OFF)
    total[...] = part[...] + dot(received[...], block_rows(embeddings, second, received.shape[1]), NN)
    rows = kept.shape[0]
    core = lax.axis_index(AXIS) % 2
    kept[...] = total[pl.ds(pl.multiple_of(core * rows, rows), rows), :]
    sent[...] = total[pl.ds(pl.multiple_of((1 - core) * rows, rows), rows), :]


def embed_kernel(signal, queries, out):
    for g in range(signal.shape[0]):
        out[g] = dot(signal[g], queries[...], TN)


def embed_end_kernel(lists, part, on_a, on_b, off_a, off_b, queries, *rest, blocks, g, scale):
    out, token, total, ready, sem = rest[-5:]
    block = part.shape[1]
    token[...] = jnp.zeros_like(token)
    total[...] = part[g]
    named = named_by_partner(lists, blocks, ON) + named_by_partner(lists, blocks, OFF)
    for received, index in zip((on_a, on_b, off_a, off_b), named):

        @pl.when(index == g)
        def _():
            total[...] += dot(received[...], queries[...], TN)

    ready[...] = (total[...] * scale).astype(BF16)
    copy = pltpu.make_async_copy(ready, out.at[pl.ds(g * block, block), :], sem)
    copy.start()
    copy.wait()


VMEM = pl.BlockSpec(memory_space=pltpu.VMEM)
SMEM = pl.BlockSpec(memory_space=pltpu.SMEM)
ANY = pl.BlockSpec(memory_space=pl.ANY)
HBM = pl.BlockSpec(memory_space=pltpu.HBM)


def call(kernel, name, in_specs, out_shape, out_specs=None, scratch=(), aliases=None, vmem=12, flops=0):
    if out_specs is None:
        out_specs = jax.tree.map(lambda _: VMEM, out_shape)
    return pl.pallas_call(
        kernel,
        in_specs=in_specs,
        out_specs=out_specs,
        out_shape=out_shape,
        scratch_shapes=scratch,
        input_output_aliases=aliases or {},
        name=name,
        cost_estimate=pl.CostEstimate(flops=flops, bytes_accessed=0, transcendentals=0),
        compiler_params=pltpu.CompilerParams(vmem_limit_bytes=vmem * MIB),
    )


def exchange(value, mask):
    count = lax.axis_size(AXIS)
    return lax.ppermute(value, AXIS, [(i, i ^ mask) for i in range(count)])


def halve_kernel(held, got, kept, sent, *, bit):
    rows = kept.shape[0]
    digit = (lax.axis_index(AXIS) // bit) % 2
    here = pl.ds(pl.multiple_of(digit * rows, rows), rows)
    there = pl.ds(pl.multiple_of((1 - digit) * rows, rows), rows)
    kept[...] = held[here, :] + got[here, :]
    sent[...] = (held[there, :] + got[there, :]).astype(BF16)


def add_kernel(held, got, *rest, scale):
    rest[-1][...] = ((held[...].astype(F32) + got[...].astype(F32)) * scale).astype(BF16)


def join_kernel(held, got, *rest, bit):
    out = rest[-1]
    rows = held.shape[0]
    digit = (lax.axis_index(AXIS) // bit) % 2
    out[pl.ds(pl.multiple_of(digit * rows, rows), rows), :] = held[...]
    out[pl.ds(pl.multiple_of((1 - digit) * rows, rows), rows), :] = got[...]


def place_kernel(held, *rest, own):
    out, wide, sem = rest[-3:]
    rows = held.shape[0]
    core = lax.axis_index(AXIS) % 2
    half = core if own else 1 - core
    wide[...] = held[...].astype(F32)
    copy = pltpu.make_async_copy(wide, out.at[pl.ds(pl.multiple_of(half * rows, rows), rows), :], sem)
    copy.start()
    copy.wait()


def sum_queries(kept, sent, beside, scale):
    count = lax.axis_size(AXIS)
    rows, width = kept.shape
    got = exchange(sent, 1)
    if count & (count - 1) or count < 4:
        half = lax.psum(kept + got, AXIS, axis_index_groups=[list(range(c, count, 2)) for c in range(2)])
        both = jnp.stack([half, exchange(half, 1)])
        both = jnp.where(lax.axis_index(AXIS) % 2 == 0, both, both[::-1])
        return both.reshape(2 * rows, width) * scale
    piece = jax.ShapeDtypeStruct((rows // 2, width), BF16)
    held, sent = call(
        functools.partial(halve_kernel, bit=2),
        "halve",
        [VMEM] * 2,
        [jax.ShapeDtypeStruct(piece.shape, F32), piece],
    )(kept, got)
    got = exchange(sent, 2)
    bits = [1 << k for k in range(2, count.bit_length() - 1)]
    for k in range(len(bits) + 1):
        last = k == len(bits)
        after = beside[k : k + 1]
        held = call(
            functools.partial(add_kernel, scale=scale if last else 1.0),
            "add",
            [VMEM] * 2 + [ANY] * len(after),
            piece,
        )(held, got, *after)
        if not last:
            got = exchange(held, bits[k])
    after = beside[len(bits) + 1 :]
    held = call(
        functools.partial(join_kernel, bit=2),
        "join",
        [VMEM] * 2 + [ANY] * len(after),
        jax.ShapeDtypeStruct((rows, width), BF16),
    )(held, exchange(held, 2), *after)
    got = exchange(held, 1)

    def place(half, own, *begun):
        return call(
            functools.partial(place_kernel, own=own),
            "place",
            [VMEM] + [ANY] * len(begun),
            jax.ShapeDtypeStruct((2 * rows, width), F32),
            out_specs=ANY,
            scratch=[pltpu.VMEM((rows, width), F32), pltpu.SemaphoreType.DMA],
            aliases={1: 0} if begun else None,
        )(half, *begun)

    return place(got, False, place(held, True))


def per_device(embeddings, edge_tiles, neighbour, propensity, queries, positives):
    count = lax.axis_size(AXIS)
    blocks, _, block, _ = edge_tiles.shape
    labels_dev, width = embeddings.shape
    rows = queries.shape[0]
    lists = neighbour.T
    odd = range(1, count, 2)
    off_route = [(i, (i + 1) % count) for i in odd] + [((i + 1) % count, i) for i in odd]

    def off_swap(value):
        return lax.ppermute(value, AXIS, off_route)

    def on_swap(value):
        return exchange(value, 1)

    def in_vmem(shape, dtype):
        return pltpu.VMEM(shape, dtype)

    one = in_vmem((rows, block), BF16)
    full = (blocks, rows, block)
    scale = 1.0 / math.sqrt(width)

    own, off_a, off_b, for_on, queries, embeddings = call(
        functools.partial(project_kernel, scale=scale),
        "project",
        [HBM] * 3,
        [
            in_vmem(full, F32),
            one,
            one,
            in_vmem((2, rows, block), BF16),
            in_vmem(queries.shape, BF16),
            in_vmem(embeddings.shape, BF16),
        ],
        scratch=[pltpu.SMEM(lists.shape, jnp.int32), pltpu.SemaphoreType.DMA((2 + blocks,))],
    )(*(pltpu.with_memory_space_constraint(x, pltpu.HBM) for x in (lists, queries, embeddings)))
    from_off_a = off_swap(off_a)
    from_off_b = off_swap(off_b)
    from_on = on_swap(for_on)
    hits, tiles = call(
        hits_kernel,
        "hits",
        [VMEM, HBM],
        [in_vmem(full, BF16), in_vmem(edge_tiles.shape, BF16)],
        scratch=[pltpu.SemaphoreType.DMA],
    )(positives, pltpu.with_memory_space_constraint(edge_tiles, pltpu.HBM))
    base = call(base_kernel, "base", [SMEM] + [VMEM] * 3, in_vmem(full, F32))(lists, own, from_on, tiles)
    propensity = propensity.reshape(1, labels_dev)

    def signal_of(received, slot, *begun):
        return call(
            functools.partial(signal_kernel, slot=slot),
            "signal",
            [SMEM] + [VMEM] * (5 + len(begun)),
            [in_vmem(full, BF16), one] + ([one, one] if begun else [in_vmem((2, rows, block), F32)]),
            scratch=[pltpu.VMEM((rows, block), F32), pltpu.VMEM((2, rows, block), F32)],
            aliases={6: 0} if begun else None,
        )(lists, base, hits, propensity, received, tiles, *begun)

    signal, push_a, carry = signal_of(from_off_a, 0)
    back_a = off_swap(push_a)
    signal, push_b, push_on_a, push_on_b = signal_of(from_off_b, 1, signal, carry)
    back_b = off_swap(push_b)
    on_a, on_b = on_swap(push_on_a), on_swap(push_on_b)

    whole = in_vmem((rows, width), F32)
    part = call(query_kernel, "query", [VMEM] * 2, whole)(signal, embeddings)
    embed = call(embed_kernel, "embed", [VMEM] * 2, in_vmem((blocks, block, width), F32))(signal, queries)
    part = call(
        functools.partial(query_half_kernel, blocks=blocks),
        "query_half",
        [SMEM] + [VMEM] * 3 + [ANY],
        whole,
        flops=10**9,
    )(lists, part, back_a, embeddings, embed)
    part = call(functools.partial(query_on_kernel, blocks=blocks), "query_on", [SMEM] + [VMEM] * 4, whole)(
        lists, part, on_a, on_b, embeddings
    )
    piece = in_vmem((rows // 2, width), F32)
    kept, sent = call(
        functools.partial(query_end_kernel, blocks=blocks),
        "query_end",
        [SMEM] + [VMEM] * 3,
        [piece, piece],
        scratch=[pltpu.VMEM((rows, width), F32)],
    )(lists, part, back_b, embeddings)

    def embed_end(g, *begun):
        return call(
            functools.partial(embed_end_kernel, blocks=blocks, g=g, scale=1.0 / math.sqrt(rows)),
            "embed_end",
            [SMEM] + [VMEM] * 6 + [ANY] * len(begun),
            [jax.ShapeDtypeStruct((labels_dev, width), BF16), in_vmem((8, 128), F32)],
            out_specs=[ANY, VMEM],
            scratch=[
                pltpu.VMEM((block, width), F32),
                pltpu.VMEM((block, width), BF16),
                pltpu.SemaphoreType.DMA,
            ],
            aliases={7: 0} if begun else None,
        )(lists, embed, on_a, on_b, back_a, back_b, queries, *begun)

    begun, tokens = [], []
    for g in range(blocks):
        grad_embed, token = embed_end(g, *begun)
        begun = [grad_embed]
        tokens.append(token)
    grad_queries = sum_queries(kept, sent, tokens, 1.0 / math.sqrt(labels_dev * count))
    return (grad_embed, grad_queries)


def solution(mesh):
    placed = (
        P("labels", None),
        P("labels", None, None, None),
        P(),
        P("labels"),
        P("groups", None),
        P("groups", None),
    )
    return jax.shard_map(
        per_device,
        mesh=mesh,
        in_specs=placed,
        out_specs=(P(("groups", "labels"), None), P("groups", None)),
        check_vma=False,
    )
```

```python
import functools
import math

import jax
import jax.numpy as jnp
from jax import lax
from jax.experimental import pallas as pl
from jax.experimental.pallas import tpu as pltpu
from jax.sharding import PartitionSpec as P

AXIS = "labels"
BF16 = jnp.bfloat16
F32 = jnp.float32
NT = (((1,), (1,)), ((), ()))
NN = (((1,), (0,)), ((), ()))
TN = (((0,), (0,)), ((), ()))
MIB = 1024 * 1024

OFF, ON = True, False


def dot(a, b, dims):
    return lax.dot_general(a, b, dims, preferred_element_type=F32)


def own_side(device, off):
    odd = device % 2
    return 1 - odd if off else odd


def partner_of(device, count, off):
    ahead = jnp.where(device == count - 1, 0, device + 1)
    behind = jnp.where(device == 0, count - 1, device - 1)
    return jnp.where(own_side(device, off) == 0, ahead, behind)


def own_list(lists, blocks, off):
    device = lax.axis_index(AXIS)
    side = own_side(device, off)
    return [lists[side, device * blocks + g] for g in range(blocks)]


def slots_of(lists, blocks, off):
    named = own_list(lists, blocks, off)
    least = functools.reduce(jnp.minimum, named)
    return [(value != least).astype(jnp.int32) for value in named]


def named_by_partner(lists, blocks, off):
    device = lax.axis_index(AXIS)
    partner = partner_of(device, lax.axis_size(AXIS), off)
    side = 1 - own_side(device, off)
    named = [lists[side, partner * blocks + g] for g in range(blocks)]
    return functools.reduce(jnp.minimum, named), functools.reduce(jnp.maximum, named)


def tile_side(off):
    return own_side(lax.axis_index(AXIS), off)


def block_rows(ref, index, block):
    return ref[pl.ds(pl.multiple_of(index * block, block), block), :]


def project_kernel(lists, queries, embeddings, out, left, right, table, sem, *, scale):
    rows, block = out.shape
    blocks = right.shape[0] // block
    fetches = [pltpu.make_async_copy(lists, table, sem.at[0]), pltpu.make_async_copy(queries, left, sem.at[1])]
    for g in range(blocks):
        place = pl.ds(g * block, block)
        fetches.append(pltpu.make_async_copy(embeddings.at[place, :], right.at[place, :], sem.at[2 + g]))
    for fetch in fetches:
        fetch.start()
    for fetch in fetches:
        fetch.wait()
    first, _ = named_by_partner(table, blocks, OFF)
    out[...] = (dot(left[...], block_rows(right, first, block), NT) * scale).astype(BF16)


def spans_of(pieces, rows):
    spans = []
    begin = 0
    for piece in pieces:
        end = begin + piece.shape[0]
        for slot in range(2):
            low, high = max(begin, slot * rows), min(end, (slot + 1) * rows)
            if low < high:
                inside = slice(low - slot * rows, high - slot * rows)
                spans.append((piece, slice(low - begin, high - begin), slot, inside))
        begin = end
    return spans


def write_pieces(pieces, value):
    rows = sum(piece.shape[0] for piece in pieces) // 2
    for piece, place, slot, inside in spans_of(pieces, rows):
        piece[place, :] = value(slot, inside).astype(BF16)


def gather_pieces(pieces, whole):
    for piece, place, slot, inside in spans_of(pieces, whole.shape[1]):
        whole[slot, inside] = piece[place, :]


def own_kernel(lists, queries, embeddings, own, off, *on, scale):
    blocks, _, block = own.shape
    for g in range(blocks):
        own[g] = dot(queries[...], embeddings[g * block : (g + 1) * block, :], NT) * scale
    _, second = named_by_partner(lists, blocks, OFF)
    off[...] = own[second].astype(BF16)
    first, second = named_by_partner(lists, blocks, ON)
    write_pieces(on, lambda slot, rows: own[(first, second)[slot], rows])


def hits_kernel(positives, tiles, out, kept, sem):
    fetch = pltpu.make_async_copy(tiles, kept, sem)
    fetch.start()
    blocks, rows, block = out.shape
    first = lax.axis_index(AXIS) * blocks * block
    ids = lax.broadcasted_iota(jnp.int32, (rows, block), 1)
    columns = jnp.transpose(positives[...]) - first
    for g in range(blocks):
        hits = jnp.zeros((rows, block), jnp.bool_)
        for column in range(positives.shape[0]):
            hits = jnp.logical_or(hits, ids + g * block == columns[:, column : column + 1])
        out[g] = jnp.where(hits, 1.0, 0.0).astype(BF16)
    fetch.wait()


def base_kernel(lists, own, tiles, *rest):
    *pieces, out, received = rest
    gather_pieces(pieces, received)
    blocks = out.shape[0]
    side = tile_side(ON)
    for g, slot in enumerate(slots_of(lists, blocks, ON)):
        out[g] = own[g] + dot(received[slot], tiles[g, side], NT)


def signal_kernel(lists, base, hits, propensity, received, tiles, *rest, slot):
    signal, push, total = rest[-3:]
    blocks, _, block = base.shape
    side = tile_side(OFF)
    total[...] = jnp.zeros_like(total)
    for g, taken in enumerate(slots_of(lists, blocks, OFF)):

        @pl.when(taken == slot)
        def _():
            scores = base[g] + dot(received[...], tiles[g, side], NT)
            inverse = 1.0 / propensity[:, g * block : (g + 1) * block]
            value = (jax.nn.sigmoid(scores) - hits[g].astype(F32) * inverse).astype(BF16)
            signal[g] = value
            total[...] += dot(value, tiles[g, side], NN)

    push[...] = total[...].astype(BF16)


def push_kernel(lists, signal, tiles, *rest):
    *pieces, total = rest
    blocks = signal.shape[0]
    side = tile_side(ON)
    total[...] = jnp.zeros_like(total)
    for g, slot in enumerate(slots_of(lists, blocks, ON)):
        total[slot] += dot(signal[g], tiles[g, side], NN)
    write_pieces(pieces, lambda slot, rows: total[slot, rows])


def query_kernel(signal, embeddings, out):
    blocks, _, block = signal.shape
    total = dot(signal[0], embeddings[0:block, :], NN)
    for g in range(1, blocks):
        total += dot(signal[g], embeddings[g * block : (g + 1) * block, :], NN)
    out[...] = total


def query_half_kernel(lists, part, received, embeddings, after, out, *, blocks):
    del after
    first, _ = named_by_partner(lists, blocks, OFF)
    out[...] = part[...] + dot(received[...], block_rows(embeddings, first, received.shape[1]), NN)


def query_on_kernel(lists, part, embeddings, *rest, blocks):
    *pieces, out, received = rest
    gather_pieces(pieces, received)
    block = received.shape[2]
    first, second = named_by_partner(lists, blocks, ON)
    out[...] = (
        part[...]
        + dot(received[0], block_rows(embeddings, first, block), NN)
        + dot(received[1], block_rows(embeddings, second, block), NN)
    )


def query_end_kernel(lists, part, received, embeddings, kept, sent, total, *, blocks):
    _, second = named_by_partner(lists, blocks, OFF)
    total[...] = part[...] + dot(received[...], block_rows(embeddings, second, received.shape[1]), NN)
    rows = kept.shape[0]
    core = lax.axis_index(AXIS) % 2
    kept[...] = total[pl.ds(pl.multiple_of(core * rows, rows), rows), :]
    sent[...] = total[pl.ds(pl.multiple_of((1 - core) * rows, rows), rows), :]


def embed_kernel(signal, queries, out):
    for g in range(signal.shape[0]):
        out[g] = dot(signal[g], queries[...], TN)


def embed_end_kernel(lists, part, on, off_a, off_b, queries, *rest, blocks, g, scale):
    out, token, total, ready, sem = rest[-5:]
    block = part.shape[1]
    token[...] = jnp.zeros_like(token)
    total[...] = part[g]
    named = named_by_partner(lists, blocks, ON) + named_by_partner(lists, blocks, OFF)
    for received, index in zip((on.at[0], on.at[1], off_a, off_b), named):

        @pl.when(index == g)
        def _():
            total[...] += dot(received[...], queries[...], TN)

    ready[...] = (total[...] * scale).astype(BF16)
    copy = pltpu.make_async_copy(ready, out.at[pl.ds(g * block, block), :], sem)
    copy.start()
    copy.wait()


VMEM = pl.BlockSpec(memory_space=pltpu.VMEM)
SMEM = pl.BlockSpec(memory_space=pltpu.SMEM)
ANY = pl.BlockSpec(memory_space=pl.ANY)
HBM = pl.BlockSpec(memory_space=pltpu.HBM)


def call(kernel, name, in_specs, out_shape, out_specs=None, scratch=(), aliases=None, vmem=12, flops=0):
    if out_specs is None:
        out_specs = jax.tree.map(lambda _: VMEM, out_shape)
    return pl.pallas_call(
        kernel,
        in_specs=in_specs,
        out_specs=out_specs,
        out_shape=out_shape,
        scratch_shapes=scratch,
        input_output_aliases=aliases or {},
        name=name,
        cost_estimate=pl.CostEstimate(flops=flops, bytes_accessed=0, transcendentals=0),
        compiler_params=pltpu.CompilerParams(vmem_limit_bytes=vmem * MIB),
    )


def exchange(value, mask):
    count = lax.axis_size(AXIS)
    return lax.ppermute(value, AXIS, [(i, i ^ mask) for i in range(count)])


def halve_kernel(held, got, kept, sent, *, bit):
    rows = kept.shape[0]
    digit = (lax.axis_index(AXIS) // bit) % 2
    here = pl.ds(pl.multiple_of(digit * rows, rows), rows)
    there = pl.ds(pl.multiple_of((1 - digit) * rows, rows), rows)
    kept[...] = held[here, :] + got[here, :]
    sent[...] = (held[there, :] + got[there, :]).astype(BF16)


def add_kernel(held, got, *rest, scale):
    rest[-1][...] = ((held[...].astype(F32) + got[...].astype(F32)) * scale).astype(BF16)


def join_kernel(held, got, *rest, bit):
    out = rest[-1]
    rows = held.shape[0]
    digit = (lax.axis_index(AXIS) // bit) % 2
    out[pl.ds(pl.multiple_of(digit * rows, rows), rows), :] = held[...]
    out[pl.ds(pl.multiple_of((1 - digit) * rows, rows), rows), :] = got[...]


def place_kernel(held, *rest, own):
    out, wide, sem = rest[-3:]
    rows = held.shape[0]
    core = lax.axis_index(AXIS) % 2
    half = core if own else 1 - core
    wide[...] = held[...].astype(F32)
    copy = pltpu.make_async_copy(wide, out.at[pl.ds(pl.multiple_of(half * rows, rows), rows), :], sem)
    copy.start()
    copy.wait()


def sum_queries(kept, sent, beside, scale):
    count = lax.axis_size(AXIS)
    rows, width = kept.shape
    got = exchange(sent, 1)
    if count & (count - 1) or count < 4:
        half = lax.psum(kept + got, AXIS, axis_index_groups=[list(range(c, count, 2)) for c in range(2)])
        both = jnp.stack([half, exchange(half, 1)])
        both = jnp.where(lax.axis_index(AXIS) % 2 == 0, both, both[::-1])
        return both.reshape(2 * rows, width) * scale
    piece = jax.ShapeDtypeStruct((rows // 2, width), BF16)
    held, sent = call(
        functools.partial(halve_kernel, bit=2),
        "halve",
        [VMEM] * 2,
        [jax.ShapeDtypeStruct(piece.shape, F32), piece],
    )(kept, got)
    got = exchange(sent, 2)
    bits = [1 << k for k in range(2, count.bit_length() - 1)]
    for k in range(len(bits) + 1):
        last = k == len(bits)
        after = beside[k : k + 1]
        held = call(
            functools.partial(add_kernel, scale=scale if last else 1.0),
            "add",
            [VMEM] * 2 + [ANY] * len(after),
            piece,
        )(held, got, *after)
        if not last:
            got = exchange(held, bits[k])
    after = beside[len(bits) + 1 :]
    held = call(
        functools.partial(join_kernel, bit=2),
        "join",
        [VMEM] * 2 + [ANY] * len(after),
        jax.ShapeDtypeStruct((rows, width), BF16),
    )(held, exchange(held, 2), *after)
    got = exchange(held, 1)

    def place(half, own, *begun):
        return call(
            functools.partial(place_kernel, own=own),
            "place",
            [VMEM] + [ANY] * len(begun),
            jax.ShapeDtypeStruct((2 * rows, width), F32),
            out_specs=ANY,
            scratch=[pltpu.VMEM((rows, width), F32), pltpu.SemaphoreType.DMA],
            aliases={1: 0} if begun else None,
        )(half, *begun)

    return place(got, False, place(held, True))


def per_device(embeddings, edge_tiles, neighbour, propensity, queries, positives):
    count = lax.axis_size(AXIS)
    blocks, _, block, _ = edge_tiles.shape
    labels_dev, width = embeddings.shape
    rows = queries.shape[0]
    lists = neighbour.T
    odd = range(1, count, 2)
    off_route = [(i, (i + 1) % count) for i in odd] + [((i + 1) % count, i) for i in odd]

    def off_swap(value):
        return lax.ppermute(value, AXIS, off_route)

    def on_swap(value):
        return exchange(value, 1)

    def in_vmem(shape, dtype):
        return pltpu.VMEM(shape, dtype)

    one = in_vmem((rows, block), BF16)
    pair = in_vmem((2, rows, block), BF16)
    third = -(-2 * rows // 48) * 16
    thirds = [in_vmem((size, block), BF16) for size in (third, third, 2 * rows - 2 * third)]
    full = (blocks, rows, block)
    scale = 1.0 / math.sqrt(width)

    off_a, queries, embeddings = call(
        functools.partial(project_kernel, scale=scale),
        "project",
        [HBM] * 3,
        [one, in_vmem(queries.shape, BF16), in_vmem(embeddings.shape, BF16)],
        scratch=[pltpu.SMEM(lists.shape, jnp.int32), pltpu.SemaphoreType.DMA((2 + blocks,))],
    )(*(pltpu.with_memory_space_constraint(x, pltpu.HBM) for x in (lists, queries, embeddings)))
    from_off_a = off_swap(off_a)
    own, off_b, *for_on = call(
        functools.partial(own_kernel, scale=scale),
        "own",
        [SMEM, VMEM, VMEM],
        [in_vmem(full, F32), one] + thirds,
    )(lists, queries, embeddings)
    from_on = [on_swap(piece) for piece in for_on]
    hits, tiles = call(
        hits_kernel,
        "hits",
        [VMEM, HBM],
        [in_vmem(full, BF16), in_vmem(edge_tiles.shape, BF16)],
        scratch=[pltpu.SemaphoreType.DMA],
    )(positives.T, pltpu.with_memory_space_constraint(edge_tiles, pltpu.HBM))
    off_b, hits = lax.optimization_barrier((off_b, hits))
    from_off_b = off_swap(off_b)
    base = call(
        base_kernel,
        "base",
        [SMEM] + [VMEM] * 5,
        in_vmem(full, F32),
        scratch=[pltpu.VMEM((2, rows, block), BF16)],
    )(lists, own, tiles, *from_on)
    propensity = propensity.reshape(1, labels_dev)

    def signal_of(received, slot, *begun):
        return call(
            functools.partial(signal_kernel, slot=slot),
            "signal",
            [SMEM] + [VMEM] * (5 + len(begun)),
            [in_vmem(full, BF16), one],
            scratch=[pltpu.VMEM((rows, block), F32)],
            aliases={6: 0} if begun else None,
            flops=0 if begun else 2 * 10**9,
        )(lists, base, hits, propensity, received, tiles, *begun)

    signal, push_a = signal_of(from_off_a, 0)
    back_a = off_swap(push_a)
    signal, push_b = signal_of(from_off_b, 1, signal)
    back_b = off_swap(push_b)
    push_on = call(
        push_kernel,
        "push",
        [SMEM, VMEM, VMEM],
        thirds,
        scratch=[pltpu.VMEM((2, rows, block), F32)],
    )(lists, signal, tiles)
    back_on = [on_swap(piece) for piece in push_on]

    whole = in_vmem((rows, width), F32)
    part = call(query_kernel, "query", [VMEM] * 2, whole)(signal, embeddings)
    embed = call(embed_kernel, "embed", [VMEM] * 2, in_vmem((blocks, block, width), F32))(signal, queries)
    part = call(
        functools.partial(query_half_kernel, blocks=blocks),
        "query_half",
        [SMEM] + [VMEM] * 3 + [ANY],
        whole,
        flops=10**9,
    )(lists, part, back_a, embeddings, embed)
    part, on = call(
        functools.partial(query_on_kernel, blocks=blocks), "query_on", [SMEM] + [VMEM] * 5, [whole, pair]
    )(lists, part, embeddings, *back_on)
    piece = in_vmem((rows // 2, width), F32)
    kept, sent = call(
        functools.partial(query_end_kernel, blocks=blocks),
        "query_end",
        [SMEM] + [VMEM] * 3,
        [piece, piece],
        scratch=[pltpu.VMEM((rows, width), F32)],
    )(lists, part, back_b, embeddings)

    def embed_end(g, *begun):
        return call(
            functools.partial(embed_end_kernel, blocks=blocks, g=g, scale=1.0 / math.sqrt(rows)),
            "embed_end",
            [SMEM] + [VMEM] * 5 + [ANY] * len(begun),
            [jax.ShapeDtypeStruct((labels_dev, width), BF16), in_vmem((8, 128), F32)],
            out_specs=[ANY, VMEM],
            scratch=[
                pltpu.VMEM((block, width), F32),
                pltpu.VMEM((block, width), BF16),
                pltpu.SemaphoreType.DMA,
            ],
            aliases={6: 0} if begun else None,
        )(lists, embed, on, back_a, back_b, queries, *begun)

    begun, tokens = [], []
    for g in range(blocks):
        grad_embed, token = embed_end(g, *begun)
        begun = [grad_embed]
        tokens.append(token)
    grad_queries = sum_queries(kept, sent, tokens, 1.0 / math.sqrt(labels_dev * count))
    return (grad_embed, grad_queries)


def solution(mesh):
    placed = (
        P("labels", None),
        P("labels", None, None, None),
        P(),
        P("labels"),
        P("groups", None),
        P("groups", None),
    )
    return jax.shard_map(
        per_device,
        mesh=mesh,
        in_specs=placed,
        out_specs=(P(("groups", "labels"), None), P("groups", None)),
        check_vma=False,
    )
```

```python
import functools
import math

import jax
import jax.numpy as jnp
from jax import lax
from jax.experimental import pallas as pl
from jax.experimental.pallas import tpu as pltpu
from jax.sharding import PartitionSpec as P

AXIS = "labels"
BF16 = jnp.bfloat16
F32 = jnp.float32
NT = (((1,), (1,)), ((), ()))
NN = (((1,), (0,)), ((), ()))
TN = (((0,), (0,)), ((), ()))
MIB = 1024 * 1024

OFF, ON = True, False


def dot(a, b, dims):
    return lax.dot_general(a, b, dims, preferred_element_type=F32)


def own_side(device, off):
    odd = device % 2
    return 1 - odd if off else odd


def partner_of(device, count, off):
    ahead = jnp.where(device == count - 1, 0, device + 1)
    behind = jnp.where(device == 0, count - 1, device - 1)
    return jnp.where(own_side(device, off) == 0, ahead, behind)


def own_list(lists, blocks, off):
    device = lax.axis_index(AXIS)
    side = own_side(device, off)
    return [lists[side, device * blocks + g] for g in range(blocks)]


def slots_of(lists, blocks, off):
    named = own_list(lists, blocks, off)
    least = functools.reduce(jnp.minimum, named)
    return [(value != least).astype(jnp.int32) for value in named]


def named_by_partner(lists, blocks, off):
    device = lax.axis_index(AXIS)
    partner = partner_of(device, lax.axis_size(AXIS), off)
    side = 1 - own_side(device, off)
    named = [lists[side, partner * blocks + g] for g in range(blocks)]
    return functools.reduce(jnp.minimum, named), functools.reduce(jnp.maximum, named)


def tile_side(off):
    return own_side(lax.axis_index(AXIS), off)


def block_rows(ref, index, block):
    return ref[pl.ds(pl.multiple_of(index * block, block), block), :]


def project_kernel(lists, queries, embeddings, out, left, right, table, sem, *, scale):
    rows, block = out.shape
    blocks = right.shape[0] // block
    fetches = [pltpu.make_async_copy(lists, table, sem.at[0]), pltpu.make_async_copy(queries, left, sem.at[1])]
    for g in range(blocks):
        place = pl.ds(g * block, block)
        fetches.append(pltpu.make_async_copy(embeddings.at[place, :], right.at[place, :], sem.at[2 + g]))
    for fetch in fetches:
        fetch.start()
    fetches[0].wait()
    first, _ = named_by_partner(table, blocks, OFF)
    fetches[1].wait()
    place = pl.ds(pl.multiple_of(first * block, block), block)
    pltpu.make_async_copy(embeddings.at[place, :], right.at[place, :], sem.at[2 + first]).wait()
    out[...] = (dot(left[...], right[place, :], NT) * scale).astype(BF16)
    for g in range(blocks):

        @pl.when(g != first)
        def _():
            fetches[2 + g].wait()


def spans_of(pieces, rows):
    spans = []
    begin = 0
    for piece in pieces:
        end = begin + piece.shape[0]
        for slot in range(2):
            low, high = max(begin, slot * rows), min(end, (slot + 1) * rows)
            if low < high:
                inside = slice(low - slot * rows, high - slot * rows)
                spans.append((piece, slice(low - begin, high - begin), slot, inside))
        begin = end
    return spans


def write_pieces(pieces, value):
    rows = sum(piece.shape[0] for piece in pieces) // 2
    for piece, place, slot, inside in spans_of(pieces, rows):
        piece[place, :] = value(slot, inside).astype(BF16)


def gather_pieces(pieces, whole):
    for piece, place, slot, inside in spans_of(pieces, whole.shape[1]):
        whole[slot, inside] = piece[place, :]


def own_kernel(lists, queries, embeddings, own, off, *on, scale):
    blocks, _, block = own.shape
    for g in range(blocks):
        own[g] = dot(queries[...], embeddings[g * block : (g + 1) * block, :], NT) * scale
    _, second = named_by_partner(lists, blocks, OFF)
    off[...] = own[second].astype(BF16)
    first, second = named_by_partner(lists, blocks, ON)
    write_pieces(on, lambda slot, rows: own[(first, second)[slot], rows])


def hits_kernel(positives, tiles, out, kept, sem):
    fetch = pltpu.make_async_copy(tiles, kept, sem)
    fetch.start()
    blocks, rows, block = out.shape
    first = lax.axis_index(AXIS) * blocks * block
    ids = lax.broadcasted_iota(jnp.int32, (rows, block), 1)
    columns = jnp.transpose(positives[...]) - first
    for g in range(blocks):
        hits = jnp.zeros((rows, block), jnp.bool_)
        for column in range(positives.shape[0]):
            hits = jnp.logical_or(hits, ids + g * block == columns[:, column : column + 1])
        out[g] = jnp.where(hits, 1.0, 0.0).astype(BF16)
    fetch.wait()


def base_kernel(lists, own, tiles, *rest):
    *pieces, out, received = rest
    gather_pieces(pieces, received)
    blocks = out.shape[0]
    side = tile_side(ON)
    for g, slot in enumerate(slots_of(lists, blocks, ON)):
        out[g] = own[g] + dot(received[slot], tiles[g, side], NT)


def signal_kernel(lists, base, hits, propensity, received, tiles, *rest, slot):
    signal, push, total = rest[-3:]
    blocks, _, block = base.shape
    side = tile_side(OFF)
    total[...] = jnp.zeros_like(total)
    for g, taken in enumerate(slots_of(lists, blocks, OFF)):

        @pl.when(taken == slot)
        def _():
            scores = base[g] + dot(received[...], tiles[g, side], NT)
            inverse = 1.0 / propensity[:, g * block : (g + 1) * block]
            value = (jax.nn.sigmoid(scores) - hits[g].astype(F32) * inverse).astype(BF16)
            signal[g] = value
            total[...] += dot(value, tiles[g, side], NN)

    push[...] = total[...].astype(BF16)


def push_kernel(lists, signal, tiles, *rest):
    *pieces, total = rest
    blocks = signal.shape[0]
    side = tile_side(ON)
    total[...] = jnp.zeros_like(total)
    for g, slot in enumerate(slots_of(lists, blocks, ON)):
        total[slot] += dot(signal[g], tiles[g, side], NN)
    write_pieces(pieces, lambda slot, rows: total[slot, rows])


def query_kernel(signal, embeddings, out):
    blocks, _, block = signal.shape
    total = dot(signal[0], embeddings[0:block, :], NN)
    for g in range(1, blocks):
        total += dot(signal[g], embeddings[g * block : (g + 1) * block, :], NN)
    out[...] = total


def query_half_kernel(lists, part, received, embeddings, out, *, blocks):
    first, _ = named_by_partner(lists, blocks, OFF)
    out[...] = part[...] + dot(received[...], block_rows(embeddings, first, received.shape[1]), NN)


def query_on_kernel(lists, part, embeddings, *rest, blocks):
    *pieces, out, received = rest
    gather_pieces(pieces, received)
    block = received.shape[2]
    first, second = named_by_partner(lists, blocks, ON)
    out[...] = (
        part[...]
        + dot(received[0], block_rows(embeddings, first, block), NN)
        + dot(received[1], block_rows(embeddings, second, block), NN)
    )


def query_end_kernel(lists, part, received, embeddings, kept, sent, total, *, blocks):
    _, second = named_by_partner(lists, blocks, OFF)
    total[...] = part[...] + dot(received[...], block_rows(embeddings, second, received.shape[1]), NN)
    rows = kept.shape[0]
    core = lax.axis_index(AXIS) % 2
    kept[...] = total[pl.ds(pl.multiple_of(core * rows, rows), rows), :]
    sent[...] = total[pl.ds(pl.multiple_of((1 - core) * rows, rows), rows), :]


def embed_kernel(lists, signal, on, off_a, off_b, queries, *rest, blocks, g, scale):
    out, token, total, ready, sem = rest[-5:]
    block = signal.shape[2]
    token[...] = jnp.zeros_like(token)
    total[...] = dot(signal[g], queries[...], TN)
    named = named_by_partner(lists, blocks, ON) + named_by_partner(lists, blocks, OFF)
    for received, index in zip((on.at[0], on.at[1], off_a, off_b), named):

        @pl.when(index == g)
        def _():
            total[...] += dot(received[...], queries[...], TN)

    ready[...] = (total[...] * scale).astype(BF16)
    copy = pltpu.make_async_copy(ready, out.at[pl.ds(g * block, block), :], sem)
    copy.start()
    copy.wait()


VMEM = pl.BlockSpec(memory_space=pltpu.VMEM)
SMEM = pl.BlockSpec(memory_space=pltpu.SMEM)
ANY = pl.BlockSpec(memory_space=pl.ANY)
HBM = pl.BlockSpec(memory_space=pltpu.HBM)


def call(kernel, name, in_specs, out_shape, out_specs=None, scratch=(), aliases=None, vmem=12, flops=0):
    if out_specs is None:
        out_specs = jax.tree.map(lambda _: VMEM, out_shape)
    return pl.pallas_call(
        kernel,
        in_specs=in_specs,
        out_specs=out_specs,
        out_shape=out_shape,
        scratch_shapes=scratch,
        input_output_aliases=aliases or {},
        name=name,
        cost_estimate=pl.CostEstimate(flops=flops, bytes_accessed=0, transcendentals=0),
        compiler_params=pltpu.CompilerParams(vmem_limit_bytes=vmem * MIB),
    )


def exchange(value, mask):
    count = lax.axis_size(AXIS)
    return lax.ppermute(value, AXIS, [(i, i ^ mask) for i in range(count)])


def in_vmem(shape, dtype):
    return pltpu.VMEM(shape, dtype)


def digit_of(bit):
    return (lax.axis_index(AXIS) // bit) % 2


def halve_kernel(held, got, *outs, bits):
    total = outs[-1]
    total[...] = held[...] + got[...]
    rows = outs[0].shape[0]
    for chain, bit in enumerate(bits):
        kept, sent = outs[2 * chain], outs[2 * chain + 1]
        begin = 2 * chain * rows
        digit = digit_of(bit)
        kept[...] = total[pl.ds(pl.multiple_of(begin + digit * rows, rows), rows), :]
        sent[...] = total[pl.ds(pl.multiple_of(begin + (1 - digit) * rows, rows), rows), :].astype(BF16)


def add_kernel(*refs, scale):
    *ins, out_a, out_b = refs
    for held, got, out in ((ins[0], ins[1], out_a), (ins[2], ins[3], out_b)):
        out[...] = ((held[...].astype(F32) + got[...].astype(F32)) * scale).astype(BF16)


def join_kernel(*refs, bits):
    *ins, out = refs
    rows = ins[0].shape[0]
    for chain, bit in enumerate(bits):
        held, got = ins[2 * chain], ins[2 * chain + 1]
        begin = 2 * chain * rows
        digit = digit_of(bit)
        out[pl.ds(pl.multiple_of(begin + digit * rows, rows), rows), :] = held[...]
        out[pl.ds(pl.multiple_of(begin + (1 - digit) * rows, rows), rows), :] = got[...]


def place_kernel(held, *rest, own):
    out, wide, sem = rest[-3:]
    rows = held.shape[0]
    core = lax.axis_index(AXIS) % 2
    half = core if own else 1 - core
    wide[...] = held[...].astype(F32)
    copy = pltpu.make_async_copy(wide, out.at[pl.ds(pl.multiple_of(half * rows, rows), rows), :], sem)
    copy.start()
    copy.wait()


def sum_queries(kept, sent, beside, scale):
    count = lax.axis_size(AXIS)
    rows, width = kept.shape
    got = exchange(sent, 1)
    if count & (count - 1) or count < 8:
        half = lax.psum(kept + got, AXIS, axis_index_groups=[list(range(c, count, 2)) for c in range(2)])
        both = jnp.stack([half, exchange(half, 1)])
        both = jnp.where(lax.axis_index(AXIS) % 2 == 0, both, both[::-1])
        return both.reshape(2 * rows, width) * scale
    piece = jax.ShapeDtypeStruct((rows // 2, width), BF16)
    bits = [1 << k for k in range(1, count.bit_length() - 1)]
    orders = [[bits[0], *bits[2:], bits[1]], [bits[1], bits[0], *bits[2:]]]
    ends = [order[0] for order in orders]
    wide, narrow = in_vmem((rows // 4, width), F32), in_vmem((rows // 4, width), BF16)
    kept_a, sent_a, kept_b, sent_b = call(
        functools.partial(halve_kernel, bits=ends),
        "halve",
        [VMEM] * 2,
        [wide, narrow, wide, narrow],
        scratch=[pltpu.VMEM((rows, width), F32)],
    )(kept, got)
    held, sent = [kept_a, kept_b], [sent_a, sent_b]
    for k in range(len(bits)):
        got = [exchange(piece, order[k]) for piece, order in zip(sent, orders)]
        after = beside[k : k + 1]
        held = sent = call(
            functools.partial(add_kernel, scale=scale if k == len(bits) - 1 else 1.0),
            "add",
            [VMEM] * 4 + [ANY] * len(after),
            [narrow, narrow],
        )(held[0], got[0], held[1], got[1], *after)
    got = [exchange(piece, bit) for piece, bit in zip(held, ends)]
    after = beside[len(bits) :]
    held = call(
        functools.partial(join_kernel, bits=ends),
        "join",
        [VMEM] * 4 + [ANY] * len(after),
        in_vmem((rows, width), BF16),
    )(held[0], got[0], held[1], got[1], *after)
    got = exchange(held, 1)

    def place(half, own, *begun):
        return call(
            functools.partial(place_kernel, own=own),
            "place",
            [VMEM] + [ANY] * len(begun),
            jax.ShapeDtypeStruct((2 * rows, width), F32),
            out_specs=ANY,
            scratch=[pltpu.VMEM((rows, width), F32), pltpu.SemaphoreType.DMA],
            aliases={1: 0} if begun else None,
        )(half, *begun)

    return place(got, False, place(held, True))


def per_device(embeddings, edge_tiles, neighbour, propensity, queries, positives):
    count = lax.axis_size(AXIS)
    blocks, _, block, _ = edge_tiles.shape
    labels_dev, width = embeddings.shape
    rows = queries.shape[0]
    lists = neighbour.T
    odd = range(1, count, 2)
    off_route = [(i, (i + 1) % count) for i in odd] + [((i + 1) % count, i) for i in odd]

    def off_swap(value):
        return lax.ppermute(value, AXIS, off_route)

    def on_swap(value):
        return exchange(value, 1)

    one = in_vmem((rows, block), BF16)
    pair = in_vmem((2, rows, block), BF16)
    third = -(-2 * rows // 48) * 16
    thirds = [in_vmem((size, block), BF16) for size in (third, third, 2 * rows - 2 * third)]
    full = (blocks, rows, block)
    scale = 1.0 / math.sqrt(width)

    off_a, queries, embeddings = call(
        functools.partial(project_kernel, scale=scale),
        "project",
        [HBM] * 3,
        [one, in_vmem(queries.shape, BF16), in_vmem(embeddings.shape, BF16)],
        scratch=[pltpu.SMEM(lists.shape, jnp.int32), pltpu.SemaphoreType.DMA((2 + blocks,))],
    )(*(pltpu.with_memory_space_constraint(x, pltpu.HBM) for x in (lists, queries, embeddings)))
    from_off_a = off_swap(off_a)
    own, off_b, *for_on = call(
        functools.partial(own_kernel, scale=scale),
        "own",
        [SMEM, VMEM, VMEM],
        [in_vmem(full, F32), one] + thirds,
    )(lists, queries, embeddings)
    from_on = [on_swap(piece) for piece in for_on]
    hits, tiles = call(
        hits_kernel,
        "hits",
        [VMEM, HBM],
        [in_vmem(full, BF16), in_vmem(edge_tiles.shape, BF16)],
        scratch=[pltpu.SemaphoreType.DMA],
    )(positives.T, pltpu.with_memory_space_constraint(edge_tiles, pltpu.HBM))
    off_b, hits = lax.optimization_barrier((off_b, hits))
    from_off_b = off_swap(off_b)
    base = call(
        base_kernel,
        "base",
        [SMEM] + [VMEM] * 5,
        in_vmem(full, F32),
        scratch=[pltpu.VMEM((2, rows, block), BF16)],
    )(lists, own, tiles, *from_on)
    propensity = propensity.reshape(1, labels_dev)

    def signal_of(received, slot, *begun):
        return call(
            functools.partial(signal_kernel, slot=slot),
            "signal",
            [SMEM] + [VMEM] * (5 + len(begun)),
            [in_vmem(full, BF16), one],
            scratch=[pltpu.VMEM((rows, block), F32)],
            aliases={6: 0} if begun else None,
            flops=0 if begun else 2 * 10**9,
        )(lists, base, hits, propensity, received, tiles, *begun)

    signal, push_a = signal_of(from_off_a, 0)
    back_a = off_swap(push_a)
    signal, push_b = signal_of(from_off_b, 1, signal)
    back_b = off_swap(push_b)
    push_on = call(
        push_kernel,
        "push",
        [SMEM, VMEM, VMEM],
        thirds,
        scratch=[pltpu.VMEM((2, rows, block), F32)],
    )(lists, signal, tiles)
    back_on = [on_swap(piece) for piece in push_on]

    whole = in_vmem((rows, width), F32)
    part = call(query_kernel, "query", [VMEM] * 2, whole)(signal, embeddings)
    part = call(
        functools.partial(query_half_kernel, blocks=blocks),
        "query_half",
        [SMEM] + [VMEM] * 3,
        whole,
        flops=10**9,
    )(lists, part, back_a, embeddings)
    part, on = call(
        functools.partial(query_on_kernel, blocks=blocks), "query_on", [SMEM] + [VMEM] * 5, [whole, pair]
    )(lists, part, embeddings, *back_on)
    piece = in_vmem((rows // 2, width), F32)
    kept, sent = call(
        functools.partial(query_end_kernel, blocks=blocks),
        "query_end",
        [SMEM] + [VMEM] * 3,
        [piece, piece],
        scratch=[pltpu.VMEM((rows, width), F32)],
    )(lists, part, back_b, embeddings)

    def embed(g, *begun):
        return call(
            functools.partial(embed_kernel, blocks=blocks, g=g, scale=1.0 / math.sqrt(rows)),
            "embed",
            [SMEM] + [VMEM] * 5 + [ANY] * len(begun),
            [jax.ShapeDtypeStruct((labels_dev, width), BF16), in_vmem((8, 128), F32)],
            out_specs=[ANY, VMEM],
            scratch=[
                pltpu.VMEM((block, width), F32),
                pltpu.VMEM((block, width), BF16),
                pltpu.SemaphoreType.DMA,
            ],
            aliases={6: 0} if begun else None,
        )(lists, signal, on, back_a, back_b, queries, *begun)

    begun, tokens = [], []
    for g in range(blocks):
        grad_embed, token = embed(g, *begun)
        begun = [grad_embed]
        tokens.append(token)
    grad_queries = sum_queries(kept, sent, tokens, 1.0 / math.sqrt(labels_dev * count))
    return (grad_embed, grad_queries)


def solution(mesh):
    placed = (
        P("labels", None),
        P("labels", None, None, None),
        P(),
        P("labels"),
        P("groups", None),
        P("groups", None),
    )
    return jax.shard_map(
        per_device,
        mesh=mesh,
        in_specs=placed,
        out_specs=(P(("groups", "labels"), None), P("groups", None)),
        check_vma=False,
    )
```

```python
import functools
import math

import jax
import jax.numpy as jnp
from jax import lax
from jax.experimental import pallas as pl
from jax.experimental.pallas import tpu as pltpu
from jax.sharding import PartitionSpec as P

AXIS = "labels"
BF16 = jnp.bfloat16
F32 = jnp.float32
NT = (((1,), (1,)), ((), ()))
NN = (((1,), (0,)), ((), ()))
TN = (((0,), (0,)), ((), ()))
MIB = 1024 * 1024

OFF, ON = True, False


def dot(a, b, dims):
    return lax.dot_general(a, b, dims, preferred_element_type=F32)


def own_side(device, off):
    odd = device % 2
    return 1 - odd if off else odd


def partner_of(device, count, off):
    ahead = jnp.where(device == count - 1, 0, device + 1)
    behind = jnp.where(device == 0, count - 1, device - 1)
    return jnp.where(own_side(device, off) == 0, ahead, behind)


def own_list(lists, blocks, off):
    device = lax.axis_index(AXIS)
    side = own_side(device, off)
    return [lists[side, device * blocks + g] for g in range(blocks)]


def slots_of(lists, blocks, off):
    named = own_list(lists, blocks, off)
    least = functools.reduce(jnp.minimum, named)
    return [(value != least).astype(jnp.int32) for value in named]


def named_by_partner(lists, blocks, off):
    device = lax.axis_index(AXIS)
    partner = partner_of(device, lax.axis_size(AXIS), off)
    side = 1 - own_side(device, off)
    named = [lists[side, partner * blocks + g] for g in range(blocks)]
    return functools.reduce(jnp.minimum, named), functools.reduce(jnp.maximum, named)


def tile_side(off):
    return own_side(lax.axis_index(AXIS), off)


def block_rows(ref, index, block):
    return ref[pl.ds(pl.multiple_of(index * block, block), block), :]


def project_kernel(lists, queries, embeddings, out, left, right, table, sem, *, scale):
    rows, block = out.shape
    blocks = right.shape[0] // block
    fetches = [pltpu.make_async_copy(lists, table, sem.at[0]), pltpu.make_async_copy(queries, left, sem.at[1])]
    for g in range(blocks):
        place = pl.ds(g * block, block)
        fetches.append(pltpu.make_async_copy(embeddings.at[place, :], right.at[place, :], sem.at[2 + g]))
    for fetch in fetches:
        fetch.start()
    fetches[0].wait()
    first, _ = named_by_partner(table, blocks, OFF)
    fetches[1].wait()
    place = pl.ds(pl.multiple_of(first * block, block), block)
    pltpu.make_async_copy(embeddings.at[place, :], right.at[place, :], sem.at[2 + first]).wait()
    out[...] = (dot(left[...], right[place, :], NT) * scale).astype(BF16)
    for g in range(blocks):

        @pl.when(g != first)
        def _():
            fetches[2 + g].wait()


def spans_of(pieces, rows):
    spans = []
    begin = 0
    for piece in pieces:
        end = begin + piece.shape[0]
        for slot in range(2):
            low, high = max(begin, slot * rows), min(end, (slot + 1) * rows)
            if low < high:
                inside = slice(low - slot * rows, high - slot * rows)
                spans.append((piece, slice(low - begin, high - begin), slot, inside))
        begin = end
    return spans


def write_pieces(pieces, value):
    rows = sum(piece.shape[0] for piece in pieces) // 2
    for piece, place, slot, inside in spans_of(pieces, rows):
        piece[place, :] = value(slot, inside).astype(BF16)


def gather_pieces(pieces, whole):
    for piece, place, slot, inside in spans_of(pieces, whole.shape[1]):
        whole[slot, inside] = piece[place, :]


def own_kernel(lists, queries, embeddings, own, off, *on, scale):
    blocks, _, block = own.shape
    for g in range(blocks):
        own[g] = dot(queries[...], embeddings[g * block : (g + 1) * block, :], NT) * scale
    _, second = named_by_partner(lists, blocks, OFF)
    off[...] = own[second].astype(BF16)
    first, second = named_by_partner(lists, blocks, ON)
    write_pieces(on, lambda slot, rows: own[(first, second)[slot], rows])


def hits_kernel(positives, tiles, out, kept, sem):
    fetch = pltpu.make_async_copy(tiles, kept, sem)
    fetch.start()
    blocks, rows, block = out.shape
    first = lax.axis_index(AXIS) * blocks * block
    ids = lax.broadcasted_iota(jnp.int32, (rows, block), 1)
    columns = jnp.transpose(positives[...]) - first
    for g in range(blocks):
        hits = jnp.zeros((rows, block), jnp.bool_)
        for column in range(positives.shape[0]):
            hits = jnp.logical_or(hits, ids + g * block == columns[:, column : column + 1])
        out[g] = jnp.where(hits, 1.0, 0.0).astype(BF16)
    fetch.wait()


def base_kernel(lists, own, tiles, *rest):
    *pieces, out, received = rest
    gather_pieces(pieces, received)
    blocks = out.shape[0]
    side = tile_side(ON)
    for g, slot in enumerate(slots_of(lists, blocks, ON)):
        out[g] = own[g] + dot(received[slot], tiles[g, side], NT)


def signal_kernel(lists, base, hits, propensity, received, tiles, *rest, slot):
    signal, push, total = rest[-3:]
    blocks, _, block = base.shape
    side = tile_side(OFF)
    total[...] = jnp.zeros_like(total)
    for g, taken in enumerate(slots_of(lists, blocks, OFF)):

        @pl.when(taken == slot)
        def _():
            scores = base[g] + dot(received[...], tiles[g, side], NT)
            inverse = 1.0 / propensity[:, g * block : (g + 1) * block]
            value = (jax.nn.sigmoid(scores) - hits[g].astype(F32) * inverse).astype(BF16)
            signal[g] = value
            total[...] += dot(value, tiles[g, side], NN)

    push[...] = total[...].astype(BF16)


def push_kernel(lists, signal, tiles, *rest):
    *pieces, total = rest
    blocks = signal.shape[0]
    side = tile_side(ON)
    total[...] = jnp.zeros_like(total)
    for g, slot in enumerate(slots_of(lists, blocks, ON)):
        total[slot] += dot(signal[g], tiles[g, side], NN)
    write_pieces(pieces, lambda slot, rows: total[slot, rows])


def query_kernel(signal, embeddings, out):
    blocks, _, block = signal.shape
    total = dot(signal[0], embeddings[0:block, :], NN)
    for g in range(1, blocks):
        total += dot(signal[g], embeddings[g * block : (g + 1) * block, :], NN)
    out[...] = total


def query_half_kernel(lists, part, received, embeddings, out, *, blocks):
    first, _ = named_by_partner(lists, blocks, OFF)
    out[...] = part[...] + dot(received[...], block_rows(embeddings, first, received.shape[1]), NN)


def query_on_kernel(lists, part, embeddings, *rest, blocks):
    *pieces, out, received = rest
    gather_pieces(pieces, received)
    block = received.shape[2]
    first, second = named_by_partner(lists, blocks, ON)
    out[...] = (
        part[...]
        + dot(received[0], block_rows(embeddings, first, block), NN)
        + dot(received[1], block_rows(embeddings, second, block), NN)
    )


def query_end_kernel(lists, part, received, embeddings, kept, sent, total, *, blocks):
    _, second = named_by_partner(lists, blocks, OFF)
    total[...] = part[...] + dot(received[...], block_rows(embeddings, second, received.shape[1]), NN)
    rows = kept.shape[0]
    core = lax.axis_index(AXIS) % 2
    kept[...] = total[pl.ds(pl.multiple_of(core * rows, rows), rows), :]
    sent[...] = total[pl.ds(pl.multiple_of((1 - core) * rows, rows), rows), :]


def embed_kernel(lists, signal, on, off_a, off_b, queries, *rest, blocks, g, scale):
    out, token, total, ready, sem = rest[-5:]
    block = signal.shape[2]
    token[...] = jnp.zeros_like(token)
    total[...] = signal[g].astype(F32)
    named = named_by_partner(lists, blocks, ON) + named_by_partner(lists, blocks, OFF)
    for received, index in zip((on.at[0], on.at[1], off_a, off_b), named):

        @pl.when(index == g)
        def _():
            total[...] += received[...].astype(F32)

    ready[...] = (dot(total[...].astype(BF16), queries[...], TN) * scale).astype(BF16)
    copy = pltpu.make_async_copy(ready, out.at[pl.ds(g * block, block), :], sem)
    copy.start()
    copy.wait()


VMEM = pl.BlockSpec(memory_space=pltpu.VMEM)
SMEM = pl.BlockSpec(memory_space=pltpu.SMEM)
ANY = pl.BlockSpec(memory_space=pl.ANY)
HBM = pl.BlockSpec(memory_space=pltpu.HBM)


def call(kernel, name, in_specs, out_shape, out_specs=None, scratch=(), aliases=None, vmem=12, flops=0):
    if out_specs is None:
        out_specs = jax.tree.map(lambda _: VMEM, out_shape)
    return pl.pallas_call(
        kernel,
        in_specs=in_specs,
        out_specs=out_specs,
        out_shape=out_shape,
        scratch_shapes=scratch,
        input_output_aliases=aliases or {},
        name=name,
        cost_estimate=pl.CostEstimate(flops=flops, bytes_accessed=0, transcendentals=0),
        compiler_params=pltpu.CompilerParams(vmem_limit_bytes=vmem * MIB),
    )


def exchange(value, mask):
    count = lax.axis_size(AXIS)
    return lax.ppermute(value, AXIS, [(i, i ^ mask) for i in range(count)])


def in_vmem(shape, dtype):
    return pltpu.VMEM(shape, dtype)


def digit_of(bit):
    return (lax.axis_index(AXIS) // bit) % 2


def halve_kernel(held, got, *outs, bits):
    total = outs[-1]
    total[...] = held[...] + got[...]
    rows = outs[0].shape[0]
    for chain, bit in enumerate(bits):
        kept, sent = outs[2 * chain], outs[2 * chain + 1]
        begin = 2 * chain * rows
        digit = digit_of(bit)
        kept[...] = total[pl.ds(pl.multiple_of(begin + digit * rows, rows), rows), :]
        sent[...] = total[pl.ds(pl.multiple_of(begin + (1 - digit) * rows, rows), rows), :].astype(BF16)


def add_kernel(*refs, scale):
    *ins, out_a, out_b = refs
    for held, got, out in ((ins[0], ins[1], out_a), (ins[2], ins[3], out_b)):
        out[...] = ((held[...].astype(F32) + got[...].astype(F32)) * scale).astype(BF16)


def join_kernel(*refs, bits):
    *ins, out = refs
    rows = ins[0].shape[0]
    for chain, bit in enumerate(bits):
        held, got = ins[2 * chain], ins[2 * chain + 1]
        begin = 2 * chain * rows
        digit = digit_of(bit)
        out[pl.ds(pl.multiple_of(begin + digit * rows, rows), rows), :] = held[...]
        out[pl.ds(pl.multiple_of(begin + (1 - digit) * rows, rows), rows), :] = got[...]


def place_kernel(held, *rest, own):
    out, wide, sem = rest[-3:]
    rows = held.shape[0]
    core = lax.axis_index(AXIS) % 2
    half = core if own else 1 - core
    wide[...] = held[...].astype(F32)
    copy = pltpu.make_async_copy(wide, out.at[pl.ds(pl.multiple_of(half * rows, rows), rows), :], sem)
    copy.start()
    copy.wait()


def sum_queries(kept, sent, beside, scale):
    count = lax.axis_size(AXIS)
    rows, width = kept.shape
    got = exchange(sent, 1)
    if count & (count - 1) or count < 8:
        half = lax.psum(kept + got, AXIS, axis_index_groups=[list(range(c, count, 2)) for c in range(2)])
        both = jnp.stack([half, exchange(half, 1)])
        both = jnp.where(lax.axis_index(AXIS) % 2 == 0, both, both[::-1])
        return both.reshape(2 * rows, width) * scale
    piece = jax.ShapeDtypeStruct((rows // 2, width), BF16)
    bits = [1 << k for k in range(1, count.bit_length() - 1)]
    orders = [[bits[0], *bits[2:], bits[1]], [bits[1], bits[0], *bits[2:]]]
    ends = [order[0] for order in orders]
    wide, narrow = in_vmem((rows // 4, width), F32), in_vmem((rows // 4, width), BF16)
    kept_a, sent_a, kept_b, sent_b = call(
        functools.partial(halve_kernel, bits=ends),
        "halve",
        [VMEM] * 2,
        [wide, narrow, wide, narrow],
        scratch=[pltpu.VMEM((rows, width), F32)],
    )(kept, got)
    held, sent = [kept_a, kept_b], [sent_a, sent_b]
    for k in range(len(bits)):
        got = [exchange(piece, order[k]) for piece, order in zip(sent, orders)]
        after = beside[k : k + 1]
        held = sent = call(
            functools.partial(add_kernel, scale=scale if k == len(bits) - 1 else 1.0),
            "add",
            [VMEM] * 4 + [ANY] * len(after),
            [narrow, narrow],
        )(held[0], got[0], held[1], got[1], *after)
    got = [exchange(piece, bit) for piece, bit in zip(held, ends)]
    after = beside[len(bits) :]
    held = call(
        functools.partial(join_kernel, bits=ends),
        "join",
        [VMEM] * 4 + [ANY] * len(after),
        in_vmem((rows, width), BF16),
    )(held[0], got[0], held[1], got[1], *after)
    got = exchange(held, 1)

    def place(half, own, *begun):
        return call(
            functools.partial(place_kernel, own=own),
            "place",
            [VMEM] + [ANY] * len(begun),
            jax.ShapeDtypeStruct((2 * rows, width), F32),
            out_specs=ANY,
            scratch=[pltpu.VMEM((rows, width), F32), pltpu.SemaphoreType.DMA],
            aliases={1: 0} if begun else None,
        )(half, *begun)

    return place(got, False, place(held, True))


def per_device(embeddings, edge_tiles, neighbour, propensity, queries, positives):
    count = lax.axis_size(AXIS)
    blocks, _, block, _ = edge_tiles.shape
    labels_dev, width = embeddings.shape
    rows = queries.shape[0]
    lists = neighbour.T
    odd = range(1, count, 2)
    off_route = [(i, (i + 1) % count) for i in odd] + [((i + 1) % count, i) for i in odd]

    def off_swap(value):
        return lax.ppermute(value, AXIS, off_route)

    def on_swap(value):
        return exchange(value, 1)

    one = in_vmem((rows, block), BF16)
    pair = in_vmem((2, rows, block), BF16)
    third = -(-2 * rows // 48) * 16
    thirds = [in_vmem((size, block), BF16) for size in (third, third, 2 * rows - 2 * third)]
    full = (blocks, rows, block)
    scale = 1.0 / math.sqrt(width)

    off_a, queries, embeddings = call(
        functools.partial(project_kernel, scale=scale),
        "project",
        [HBM] * 3,
        [one, in_vmem(queries.shape, BF16), in_vmem(embeddings.shape, BF16)],
        scratch=[pltpu.SMEM(lists.shape, jnp.int32), pltpu.SemaphoreType.DMA((2 + blocks,))],
    )(*(pltpu.with_memory_space_constraint(x, pltpu.HBM) for x in (lists, queries, embeddings)))
    from_off_a = off_swap(off_a)
    own, off_b, *for_on = call(
        functools.partial(own_kernel, scale=scale),
        "own",
        [SMEM, VMEM, VMEM],
        [in_vmem(full, F32), one] + thirds,
    )(lists, queries, embeddings)
    from_on = [on_swap(piece) for piece in for_on]
    hits, tiles = call(
        hits_kernel,
        "hits",
        [VMEM, HBM],
        [in_vmem(full, BF16), in_vmem(edge_tiles.shape, BF16)],
        scratch=[pltpu.SemaphoreType.DMA],
    )(positives.T, pltpu.with_memory_space_constraint(edge_tiles, pltpu.HBM))
    from_off_b = off_swap(off_b)
    base = call(
        base_kernel,
        "base",
        [SMEM] + [VMEM] * 5,
        in_vmem(full, F32),
        scratch=[pltpu.VMEM((2, rows, block), BF16)],
    )(lists, own, tiles, *from_on)
    propensity = propensity.reshape(1, labels_dev)

    def signal_of(received, slot, *begun):
        return call(
            functools.partial(signal_kernel, slot=slot),
            "signal",
            [SMEM] + [VMEM] * (5 + len(begun)),
            [in_vmem(full, BF16), one],
            scratch=[pltpu.VMEM((rows, block), F32)],
            aliases={6: 0} if begun else None,
            flops=0 if begun else 2 * 10**9,
        )(lists, base, hits, propensity, received, tiles, *begun)

    signal, push_a = signal_of(from_off_a, 0)
    back_a = off_swap(push_a)
    signal, push_b = signal_of(from_off_b, 1, signal)
    back_b = off_swap(push_b)
    push_on = call(
        push_kernel,
        "push",
        [SMEM, VMEM, VMEM],
        thirds,
        scratch=[pltpu.VMEM((2, rows, block), F32)],
    )(lists, signal, tiles)
    back_on = [on_swap(piece) for piece in push_on]

    whole = in_vmem((rows, width), F32)
    part = call(query_kernel, "query", [VMEM] * 2, whole)(signal, embeddings)
    part = call(
        functools.partial(query_half_kernel, blocks=blocks),
        "query_half",
        [SMEM] + [VMEM] * 3,
        whole,
        flops=10**9,
    )(lists, part, back_a, embeddings)
    part, on = call(
        functools.partial(query_on_kernel, blocks=blocks), "query_on", [SMEM] + [VMEM] * 5, [whole, pair]
    )(lists, part, embeddings, *back_on)
    piece = in_vmem((rows // 2, width), F32)
    kept, sent = call(
        functools.partial(query_end_kernel, blocks=blocks),
        "query_end",
        [SMEM] + [VMEM] * 3,
        [piece, piece],
        scratch=[pltpu.VMEM((rows, width), F32)],
    )(lists, part, back_b, embeddings)

    def embed(g, *begun):
        return call(
            functools.partial(embed_kernel, blocks=blocks, g=g, scale=1.0 / math.sqrt(rows)),
            "embed",
            [SMEM] + [VMEM] * 5 + [ANY] * len(begun),
            [jax.ShapeDtypeStruct((labels_dev, width), BF16), in_vmem((8, 128), F32)],
            out_specs=[ANY, VMEM],
            scratch=[
                pltpu.VMEM((rows, block), F32),
                pltpu.VMEM((block, width), BF16),
                pltpu.SemaphoreType.DMA,
            ],
            aliases={6: 0} if begun else None,
        )(lists, signal, on, back_a, back_b, queries, *begun)

    begun, tokens = [], []
    for g in range(blocks):
        grad_embed, token = embed(g, *begun)
        begun = [grad_embed]
        tokens.append(token)
    grad_queries = sum_queries(kept, sent, tokens, 1.0 / math.sqrt(labels_dev * count))
    return (grad_embed, grad_queries)


def solution(mesh):
    placed = (
        P("labels", None),
        P("labels", None, None, None),
        P(),
        P("labels"),
        P("groups", None),
        P("groups", None),
    )
    return jax.shard_map(
        per_device,
        mesh=mesh,
        in_specs=placed,
        out_specs=(P(("groups", "labels"), None), P("groups", None)),
        check_vma=False,
    )
```

```python
import functools
import math

import jax
import jax.numpy as jnp
from jax import lax
from jax.experimental import pallas as pl
from jax.experimental.pallas import tpu as pltpu
from jax.sharding import PartitionSpec as P

AXIS = "labels"
BF16 = jnp.bfloat16
F32 = jnp.float32
NT = (((1,), (1,)), ((), ()))
NN = (((1,), (0,)), ((), ()))
TN = (((0,), (0,)), ((), ()))
MIB = 1024 * 1024

OFF, ON = True, False


def dot(a, b, dims):
    return lax.dot_general(a, b, dims, preferred_element_type=F32)


def own_side(device, off):
    odd = device % 2
    return 1 - odd if off else odd


def partner_of(device, count, off):
    ahead = jnp.where(device == count - 1, 0, device + 1)
    behind = jnp.where(device == 0, count - 1, device - 1)
    return jnp.where(own_side(device, off) == 0, ahead, behind)


def own_list(lists, blocks, off):
    device = lax.axis_index(AXIS)
    side = own_side(device, off)
    return [lists[side, device * blocks + g] for g in range(blocks)]


def slots_of(lists, blocks, off):
    named = own_list(lists, blocks, off)
    least = functools.reduce(jnp.minimum, named)
    return [(value != least).astype(jnp.int32) for value in named]


def named_by_partner(lists, blocks, off):
    device = lax.axis_index(AXIS)
    partner = partner_of(device, lax.axis_size(AXIS), off)
    side = 1 - own_side(device, off)
    named = [lists[side, partner * blocks + g] for g in range(blocks)]
    return functools.reduce(jnp.minimum, named), functools.reduce(jnp.maximum, named)


def tile_side(off):
    return own_side(lax.axis_index(AXIS), off)


def block_rows(ref, index, block):
    return ref[pl.ds(pl.multiple_of(index * block, block), block), :]


def project_kernel(lists, queries, embeddings, out, left, right, table, sem, *, scale):
    rows, block = out.shape
    blocks = right.shape[0] // block
    fetches = [pltpu.make_async_copy(lists, table, sem.at[0]), pltpu.make_async_copy(queries, left, sem.at[1])]
    for g in range(blocks):
        place = pl.ds(g * block, block)
        fetches.append(pltpu.make_async_copy(embeddings.at[place, :], right.at[place, :], sem.at[2 + g]))
    for fetch in fetches:
        fetch.start()
    fetches[0].wait()
    first, _ = named_by_partner(table, blocks, OFF)
    fetches[1].wait()
    place = pl.ds(pl.multiple_of(first * block, block), block)
    pltpu.make_async_copy(embeddings.at[place, :], right.at[place, :], sem.at[2 + first]).wait()
    out[...] = (dot(left[...], right[place, :], NT) * scale).astype(BF16)
    for g in range(blocks):

        @pl.when(g != first)
        def _():
            fetches[2 + g].wait()


def spans_of(pieces, rows):
    spans = []
    begin = 0
    for piece in pieces:
        end = begin + piece.shape[0]
        for slot in range(2):
            low, high = max(begin, slot * rows), min(end, (slot + 1) * rows)
            if low < high:
                inside = slice(low - slot * rows, high - slot * rows)
                spans.append((piece, slice(low - begin, high - begin), slot, inside))
        begin = end
    return spans


def write_pieces(pieces, value):
    rows = sum(piece.shape[0] for piece in pieces) // 2
    for piece, place, slot, inside in spans_of(pieces, rows):
        piece[place, :] = value(slot, inside).astype(BF16)


def gather_pieces(pieces, whole):
    for piece, place, slot, inside in spans_of(pieces, whole.shape[1]):
        whole[slot, inside] = piece[place, :]


def own_kernel(lists, queries, embeddings, own, off, *on, scale):
    blocks, _, block = own.shape
    for g in range(blocks):
        own[g] = dot(queries[...], embeddings[g * block : (g + 1) * block, :], NT) * scale
    _, second = named_by_partner(lists, blocks, OFF)
    off[...] = own[second].astype(BF16)
    first, second = named_by_partner(lists, blocks, ON)
    write_pieces(on, lambda slot, rows: own[(first, second)[slot], rows])


def hits_kernel(positives, tiles, out, kept, sem):
    fetch = pltpu.make_async_copy(tiles, kept, sem)
    fetch.start()
    blocks, rows, block = out.shape
    first = lax.axis_index(AXIS) * blocks * block
    ids = lax.broadcasted_iota(jnp.int32, (rows, block), 1)
    columns = jnp.transpose(positives[...]) - first
    for g in range(blocks):
        hits = jnp.zeros((rows, block), jnp.bool_)
        for column in range(positives.shape[0]):
            hits = jnp.logical_or(hits, ids + g * block == columns[:, column : column + 1])
        out[g] = jnp.where(hits, 1.0, 0.0).astype(BF16)
    fetch.wait()


def base_kernel(lists, own, tiles, *rest):
    *pieces, out, received = rest
    gather_pieces(pieces, received)
    blocks = out.shape[0]
    side = tile_side(ON)
    for g, slot in enumerate(slots_of(lists, blocks, ON)):
        out[g] = own[g] + dot(received[slot], tiles[g, side], NT)


def signal_kernel(lists, base, hits, propensity, received, tiles, *rest, slot):
    signal, push, total = rest[-3:]
    blocks, _, block = base.shape
    side = tile_side(OFF)
    total[...] = jnp.zeros_like(total)
    for g, taken in enumerate(slots_of(lists, blocks, OFF)):

        @pl.when(taken == slot)
        def _():
            scores = base[g] + dot(received[...], tiles[g, side], NT)
            inverse = 1.0 / propensity[:, g * block : (g + 1) * block]
            value = (jax.nn.sigmoid(scores) - hits[g].astype(F32) * inverse).astype(BF16)
            signal[g] = value
            total[...] += dot(value, tiles[g, side], NN)

    push[...] = total[...].astype(BF16)


def push_kernel(lists, signal, tiles, *rest):
    *pieces, total = rest
    blocks = signal.shape[0]
    side = tile_side(ON)
    total[...] = jnp.zeros_like(total)
    for g, slot in enumerate(slots_of(lists, blocks, ON)):
        total[slot] += dot(signal[g], tiles[g, side], NN)
    write_pieces(pieces, lambda slot, rows: total[slot, rows])


def query_kernel(signal, embeddings, out):
    blocks, _, block = signal.shape
    total = dot(signal[0], embeddings[0:block, :], NN)
    for g in range(1, blocks):
        total += dot(signal[g], embeddings[g * block : (g + 1) * block, :], NN)
    out[...] = total


def query_half_kernel(lists, part, received, embeddings, out, *, blocks):
    first, _ = named_by_partner(lists, blocks, OFF)
    out[...] = part[...] + dot(received[...], block_rows(embeddings, first, received.shape[1]), NN)


def query_on_kernel(lists, part, embeddings, *rest, blocks):
    *pieces, out, received = rest
    gather_pieces(pieces, received)
    block = received.shape[2]
    first, second = named_by_partner(lists, blocks, ON)
    out[...] = (
        part[...]
        + dot(received[0], block_rows(embeddings, first, block), NN)
        + dot(received[1], block_rows(embeddings, second, block), NN)
    )


def query_end_kernel(lists, part, received, embeddings, kept, sent, total, *, blocks):
    _, second = named_by_partner(lists, blocks, OFF)
    total[...] = part[...] + dot(received[...], block_rows(embeddings, second, received.shape[1]), NN)
    rows = kept.shape[0]
    core = lax.axis_index(AXIS) % 2
    kept[...] = total[pl.ds(pl.multiple_of(core * rows, rows), rows), :]
    sent[...] = total[pl.ds(pl.multiple_of((1 - core) * rows, rows), rows), :].astype(BF16)


def embed_kernel(lists, signal, on, off_a, off_b, queries, *rest, blocks, g, scale):
    out, token, total, ready, sem = rest[-5:]
    block = signal.shape[2]
    token[...] = jnp.zeros_like(token)
    total[...] = signal[g].astype(F32)
    named = named_by_partner(lists, blocks, ON) + named_by_partner(lists, blocks, OFF)
    for received, index in zip((on.at[0], on.at[1], off_a, off_b), named):

        @pl.when(index == g)
        def _():
            total[...] += received[...].astype(F32)

    ready[...] = (dot(total[...].astype(BF16), queries[...], TN) * scale).astype(BF16)
    copy = pltpu.make_async_copy(ready, out.at[pl.ds(g * block, block), :], sem)
    copy.start()
    copy.wait()


VMEM = pl.BlockSpec(memory_space=pltpu.VMEM)
SMEM = pl.BlockSpec(memory_space=pltpu.SMEM)
ANY = pl.BlockSpec(memory_space=pl.ANY)
HBM = pl.BlockSpec(memory_space=pltpu.HBM)


def call(kernel, name, in_specs, out_shape, out_specs=None, scratch=(), aliases=None, vmem=12, flops=0):
    if out_specs is None:
        out_specs = jax.tree.map(lambda _: VMEM, out_shape)
    return pl.pallas_call(
        kernel,
        in_specs=in_specs,
        out_specs=out_specs,
        out_shape=out_shape,
        scratch_shapes=scratch,
        input_output_aliases=aliases or {},
        name=name,
        cost_estimate=pl.CostEstimate(flops=flops, bytes_accessed=0, transcendentals=0),
        compiler_params=pltpu.CompilerParams(vmem_limit_bytes=vmem * MIB),
    )


def exchange(value, mask):
    count = lax.axis_size(AXIS)
    return lax.ppermute(value, AXIS, [(i, i ^ mask) for i in range(count)])


def in_vmem(shape, dtype):
    return pltpu.VMEM(shape, dtype)


def digit_of(bit):
    return (lax.axis_index(AXIS) // bit) % 2


def halve_kernel(held, got, kept, sent, total, *, bit):
    total[...] = held[...] + got[...].astype(F32)
    rows = kept.shape[0]
    digit = digit_of(bit)
    kept[...] = total[pl.ds(pl.multiple_of(digit * rows, rows), rows), :]
    sent[...] = total[pl.ds(pl.multiple_of((1 - digit) * rows, rows), rows), :].astype(BF16)


def add_kernel(held, got, *rest, scale):
    rest[-1][...] = ((held[...].astype(F32) + got[...].astype(F32)) * scale).astype(BF16)


def join_kernel(held, got, *rest, bit):
    out = rest[-1]
    rows = held.shape[0]
    digit = digit_of(bit)
    out[pl.ds(pl.multiple_of(digit * rows, rows), rows), :] = held[...]
    out[pl.ds(pl.multiple_of((1 - digit) * rows, rows), rows), :] = got[...]


def place_kernel(held, *rest, own):
    out, wide, sem = rest[-3:]
    rows = held.shape[0]
    core = lax.axis_index(AXIS) % 2
    half = core if own else 1 - core
    wide[...] = held[...].astype(F32)
    copy = pltpu.make_async_copy(wide, out.at[pl.ds(pl.multiple_of(half * rows, rows), rows), :], sem)
    copy.start()
    copy.wait()


def sum_queries(kept, sent, beside, scale):
    count = lax.axis_size(AXIS)
    rows, width = kept.shape
    got = exchange(sent, 1)
    if count & (count - 1) or count < 4:
        half = kept + got.astype(F32)
        half = lax.psum(half, AXIS, axis_index_groups=[list(range(c, count, 2)) for c in range(2)])
        both = jnp.stack([half, exchange(half, 1)])
        both = jnp.where(lax.axis_index(AXIS) % 2 == 0, both, both[::-1])
        return both.reshape(2 * rows, width) * scale
    bits = [1 << k for k in range(1, count.bit_length() - 1)]
    narrow = in_vmem((rows // 2, width), BF16)
    held, sent = call(
        functools.partial(halve_kernel, bit=bits[0]),
        "halve",
        [VMEM] * 2,
        [in_vmem(narrow.shape, F32), narrow],
        scratch=[pltpu.VMEM((rows, width), F32)],
    )(kept, got)
    for k, bit in enumerate(bits):
        after = beside[k : k + 1]
        held = sent = call(
            functools.partial(add_kernel, scale=scale if k == len(bits) - 1 else 1.0),
            "add",
            [VMEM] * 2 + [ANY] * len(after),
            narrow,
        )(held, exchange(sent, bit), *after)
    after = beside[len(bits) :]
    held = call(
        functools.partial(join_kernel, bit=bits[0]),
        "join",
        [VMEM] * 2 + [ANY] * len(after),
        in_vmem((rows, width), BF16),
    )(held, exchange(held, bits[0]), *after)
    got = exchange(held, 1)

    def place(half, own, *begun):
        return call(
            functools.partial(place_kernel, own=own),
            "place",
            [VMEM] + [ANY] * len(begun),
            jax.ShapeDtypeStruct((2 * rows, width), F32),
            out_specs=ANY,
            scratch=[pltpu.VMEM((rows, width), F32), pltpu.SemaphoreType.DMA],
            aliases={1: 0} if begun else None,
        )(half, *begun)

    return place(got, False, place(held, True))


def per_device(embeddings, edge_tiles, neighbour, propensity, queries, positives):
    count = lax.axis_size(AXIS)
    blocks, _, block, _ = edge_tiles.shape
    labels_dev, width = embeddings.shape
    rows = queries.shape[0]
    lists = neighbour.T
    odd = range(1, count, 2)
    off_route = [(i, (i + 1) % count) for i in odd] + [((i + 1) % count, i) for i in odd]

    def off_swap(value):
        return lax.ppermute(value, AXIS, off_route)

    def on_swap(value):
        return exchange(value, 1)

    one = in_vmem((rows, block), BF16)
    pair = in_vmem((2, rows, block), BF16)
    third = -(-2 * rows // 48) * 16
    thirds = [in_vmem((size, block), BF16) for size in (third, third, 2 * rows - 2 * third)]
    full = (blocks, rows, block)
    scale = 1.0 / math.sqrt(width)

    off_a, queries, embeddings = call(
        functools.partial(project_kernel, scale=scale),
        "project",
        [HBM] * 3,
        [one, in_vmem(queries.shape, BF16), in_vmem(embeddings.shape, BF16)],
        scratch=[pltpu.SMEM(lists.shape, jnp.int32), pltpu.SemaphoreType.DMA((2 + blocks,))],
    )(*(pltpu.with_memory_space_constraint(x, pltpu.HBM) for x in (lists, queries, embeddings)))
    from_off_a = off_swap(off_a)
    own, off_b, *for_on = call(
        functools.partial(own_kernel, scale=scale),
        "own",
        [SMEM, VMEM, VMEM],
        [in_vmem(full, F32), one] + thirds,
    )(lists, queries, embeddings)
    from_on = [on_swap(piece) for piece in for_on]
    hits, tiles = call(
        hits_kernel,
        "hits",
        [VMEM, HBM],
        [in_vmem(full, BF16), in_vmem(edge_tiles.shape, BF16)],
        scratch=[pltpu.SemaphoreType.DMA],
    )(positives.T, pltpu.with_memory_space_constraint(edge_tiles, pltpu.HBM))
    from_off_b = off_swap(off_b)
    base = call(
        base_kernel,
        "base",
        [SMEM] + [VMEM] * 5,
        in_vmem(full, F32),
        scratch=[pltpu.VMEM((2, rows, block), BF16)],
    )(lists, own, tiles, *from_on)
    propensity = propensity.reshape(1, labels_dev)

    def signal_of(received, slot, *begun):
        return call(
            functools.partial(signal_kernel, slot=slot),
            "signal",
            [SMEM] + [VMEM] * (5 + len(begun)),
            [in_vmem(full, BF16), one],
            scratch=[pltpu.VMEM((rows, block), F32)],
            aliases={6: 0} if begun else None,
            flops=0 if begun else 2 * 10**9,
        )(lists, base, hits, propensity, received, tiles, *begun)

    signal, push_a = signal_of(from_off_a, 0)
    back_a = off_swap(push_a)
    signal, push_b = signal_of(from_off_b, 1, signal)
    back_b = off_swap(push_b)
    push_on = call(
        push_kernel,
        "push",
        [SMEM, VMEM, VMEM],
        thirds,
        scratch=[pltpu.VMEM((2, rows, block), F32)],
    )(lists, signal, tiles)
    back_on = [on_swap(piece) for piece in push_on]

    whole = in_vmem((rows, width), F32)
    part = call(query_kernel, "query", [VMEM] * 2, whole)(signal, embeddings)
    part = call(
        functools.partial(query_half_kernel, blocks=blocks),
        "query_half",
        [SMEM] + [VMEM] * 3,
        whole,
        flops=10**9,
    )(lists, part, back_a, embeddings)
    part, on = call(
        functools.partial(query_on_kernel, blocks=blocks), "query_on", [SMEM] + [VMEM] * 5, [whole, pair]
    )(lists, part, embeddings, *back_on)
    kept, sent = (in_vmem((rows // 2, width), kind) for kind in (F32, BF16))
    kept, sent = call(
        functools.partial(query_end_kernel, blocks=blocks),
        "query_end",
        [SMEM] + [VMEM] * 3,
        [kept, sent],
        scratch=[pltpu.VMEM((rows, width), F32)],
    )(lists, part, back_b, embeddings)

    def embed(g, *begun):
        return call(
            functools.partial(embed_kernel, blocks=blocks, g=g, scale=1.0 / math.sqrt(rows)),
            "embed",
            [SMEM] + [VMEM] * 5 + [ANY] * len(begun),
            [jax.ShapeDtypeStruct((labels_dev, width), BF16), in_vmem((8, 128), F32)],
            out_specs=[ANY, VMEM],
            scratch=[
                pltpu.VMEM((rows, block), F32),
                pltpu.VMEM((block, width), BF16),
                pltpu.SemaphoreType.DMA,
            ],
            aliases={6: 0} if begun else None,
        )(lists, signal, on, back_a, back_b, queries, *begun)

    begun, tokens = [], []
    for g in range(blocks):
        grad_embed, token = embed(g, *begun)
        begun = [grad_embed]
        tokens.append(token)
    grad_queries = sum_queries(kept, sent, tokens, 1.0 / math.sqrt(labels_dev * count))
    return (grad_embed, grad_queries)


def solution(mesh):
    placed = (
        P("labels", None),
        P("labels", None, None, None),
        P(),
        P("labels"),
        P("groups", None),
        P("groups", None),
    )
    return jax.shard_map(
        per_device,
        mesh=mesh,
        in_specs=placed,
        out_specs=(P(("groups", "labels"), None), P("groups", None)),
        check_vma=False,
    )
```

```python
import functools
import math

import jax
import jax.numpy as jnp
from jax import lax
from jax.experimental import pallas as pl
from jax.experimental.pallas import tpu as pltpu
from jax.sharding import PartitionSpec as P

AXIS = "labels"
BF16 = jnp.bfloat16
F32 = jnp.float32
NT = (((1,), (1,)), ((), ()))
NN = (((1,), (0,)), ((), ()))
TN = (((0,), (0,)), ((), ()))
MIB = 1024 * 1024

OFF, ON = True, False


def dot(a, b, dims):
    return lax.dot_general(a, b, dims, preferred_element_type=F32)


def own_side(device, off):
    odd = device % 2
    return 1 - odd if off else odd


def partner_of(device, count, off):
    ahead = jnp.where(device == count - 1, 0, device + 1)
    behind = jnp.where(device == 0, count - 1, device - 1)
    return jnp.where(own_side(device, off) == 0, ahead, behind)


def own_list(lists, blocks, off):
    device = lax.axis_index(AXIS)
    side = own_side(device, off)
    return [lists[side, device * blocks + g] for g in range(blocks)]


def slots_of(lists, blocks, off):
    named = own_list(lists, blocks, off)
    least = functools.reduce(jnp.minimum, named)
    return [(value != least).astype(jnp.int32) for value in named]


def named_by_partner(lists, blocks, off):
    device = lax.axis_index(AXIS)
    partner = partner_of(device, lax.axis_size(AXIS), off)
    side = 1 - own_side(device, off)
    named = [lists[side, partner * blocks + g] for g in range(blocks)]
    return functools.reduce(jnp.minimum, named), functools.reduce(jnp.maximum, named)


def tile_side(off):
    return own_side(lax.axis_index(AXIS), off)


def block_rows(ref, index, block):
    return ref[pl.ds(pl.multiple_of(index * block, block), block), :]


def project_kernel(lists, queries, embeddings, out, left, right, table, sem, *, scale):
    rows, block = out.shape
    blocks = right.shape[0] // block
    fetches = [pltpu.make_async_copy(lists, table, sem.at[0]), pltpu.make_async_copy(queries, left, sem.at[1])]
    for g in range(blocks):
        place = pl.ds(g * block, block)
        fetches.append(pltpu.make_async_copy(embeddings.at[place, :], right.at[place, :], sem.at[2 + g]))
    for fetch in fetches:
        fetch.start()
    fetches[0].wait()
    first, _ = named_by_partner(table, blocks, OFF)
    fetches[1].wait()
    place = pl.ds(pl.multiple_of(first * block, block), block)
    pltpu.make_async_copy(embeddings.at[place, :], right.at[place, :], sem.at[2 + first]).wait()
    out[...] = (dot(left[...], right[place, :], NT) * scale).astype(BF16)
    for g in range(blocks):

        @pl.when(g != first)
        def _():
            fetches[2 + g].wait()


def spans_of(pieces, rows):
    spans = []
    begin = 0
    for piece in pieces:
        end = begin + piece.shape[0]
        for slot in range(2):
            low, high = max(begin, slot * rows), min(end, (slot + 1) * rows)
            if low < high:
                inside = slice(low - slot * rows, high - slot * rows)
                spans.append((piece, slice(low - begin, high - begin), slot, inside))
        begin = end
    return spans


def write_pieces(pieces, value):
    rows = sum(piece.shape[0] for piece in pieces) // 2
    for piece, place, slot, inside in spans_of(pieces, rows):
        piece[place, :] = value(slot, inside).astype(BF16)


def gather_pieces(pieces, whole):
    for piece, place, slot, inside in spans_of(pieces, whole.shape[1]):
        whole[slot, inside] = piece[place, :]


def own_kernel(lists, queries, embeddings, own, off, *on, scale):
    blocks, _, block = own.shape
    for g in range(blocks):
        own[g] = dot(queries[...], embeddings[g * block : (g + 1) * block, :], NT) * scale
    _, second = named_by_partner(lists, blocks, OFF)
    off[...] = own[second].astype(BF16)
    first, second = named_by_partner(lists, blocks, ON)
    write_pieces(on, lambda slot, rows: own[(first, second)[slot], rows])


def hits_kernel(positives, tiles, out, kept, sem):
    fetch = pltpu.make_async_copy(tiles, kept, sem)
    fetch.start()
    blocks, rows, block = out.shape
    first = lax.axis_index(AXIS) * blocks * block
    ids = lax.broadcasted_iota(jnp.int32, (rows, block), 1)
    columns = jnp.transpose(positives[...]) - first
    for g in range(blocks):
        hits = jnp.zeros((rows, block), jnp.bool_)
        for column in range(positives.shape[0]):
            hits = jnp.logical_or(hits, ids + g * block == columns[:, column : column + 1])
        out[g] = jnp.where(hits, 1.0, 0.0).astype(BF16)
    fetch.wait()


def base_kernel(lists, own, tiles, *rest):
    *pieces, out, received = rest
    gather_pieces(pieces, received)
    blocks = out.shape[0]
    side = tile_side(ON)
    for g, slot in enumerate(slots_of(lists, blocks, ON)):
        out[g] = own[g] + dot(received[slot], tiles[g, side], NT)


def signal_kernel(lists, base, hits, propensity, received, tiles, *rest, slot):
    signal, push, total = rest[-3:]
    blocks, _, block = base.shape
    side = tile_side(OFF)
    total[...] = jnp.zeros_like(total)
    for g, taken in enumerate(slots_of(lists, blocks, OFF)):

        @pl.when(taken == slot)
        def _():
            scores = base[g] + dot(received[...], tiles[g, side], NT)
            inverse = 1.0 / propensity[:, g * block : (g + 1) * block]
            value = (jax.nn.sigmoid(scores) - hits[g].astype(F32) * inverse).astype(BF16)
            signal[g] = value
            total[...] += dot(value, tiles[g, side], NN)

    push[...] = total[...].astype(BF16)


def push_kernel(lists, signal, tiles, *rest):
    *pieces, total = rest
    blocks = signal.shape[0]
    side = tile_side(ON)
    total[...] = jnp.zeros_like(total)
    for g, slot in enumerate(slots_of(lists, blocks, ON)):
        total[slot] += dot(signal[g], tiles[g, side], NN)
    write_pieces(pieces, lambda slot, rows: total[slot, rows])


def query_kernel(signal, embeddings, out):
    blocks, _, block = signal.shape
    total = dot(signal[0], embeddings[0:block, :], NN)
    for g in range(1, blocks):
        total += dot(signal[g], embeddings[g * block : (g + 1) * block, :], NN)
    out[...] = total


def query_half_kernel(lists, part, received, embeddings, out, *, blocks):
    first, _ = named_by_partner(lists, blocks, OFF)
    out[...] = part[...] + dot(received[...], block_rows(embeddings, first, received.shape[1]), NN)


def query_on_kernel(lists, part, embeddings, *rest, blocks):
    *pieces, out, received = rest
    gather_pieces(pieces, received)
    block = received.shape[2]
    first, second = named_by_partner(lists, blocks, ON)
    out[...] = (
        part[...]
        + dot(received[0], block_rows(embeddings, first, block), NN)
        + dot(received[1], block_rows(embeddings, second, block), NN)
    )


def query_end_kernel(lists, part, received, embeddings, kept, sent, total, *, blocks):
    _, second = named_by_partner(lists, blocks, OFF)
    total[...] = part[...] + dot(received[...], block_rows(embeddings, second, received.shape[1]), NN)
    rows = kept.shape[0]
    core = lax.axis_index(AXIS) % 2
    kept[...] = total[pl.ds(pl.multiple_of(core * rows, rows), rows), :]
    sent[...] = total[pl.ds(pl.multiple_of((1 - core) * rows, rows), rows), :].astype(BF16)


def embed_kernel(lists, signal, on, off_a, off_b, queries, *rest, blocks, g, scale):
    out, token, total, ready, sem = rest[-5:]
    block = signal.shape[2]
    token[...] = jnp.zeros_like(token)
    total[...] = signal[g].astype(F32)
    named = named_by_partner(lists, blocks, ON) + named_by_partner(lists, blocks, OFF)
    for received, index in zip((on.at[0], on.at[1], off_a, off_b), named):

        @pl.when(index == g)
        def _():
            total[...] += received[...].astype(F32)

    ready[...] = (dot(total[...].astype(BF16), queries[...], TN) * scale).astype(BF16)
    copy = pltpu.make_async_copy(ready, out.at[pl.ds(g * block, block), :], sem)
    copy.start()
    copy.wait()


VMEM = pl.BlockSpec(memory_space=pltpu.VMEM)
SMEM = pl.BlockSpec(memory_space=pltpu.SMEM)
ANY = pl.BlockSpec(memory_space=pl.ANY)
HBM = pl.BlockSpec(memory_space=pltpu.HBM)


def call(kernel, name, in_specs, out_shape, out_specs=None, scratch=(), aliases=None, vmem=12, flops=0):
    if out_specs is None:
        out_specs = jax.tree.map(lambda _: VMEM, out_shape)
    return pl.pallas_call(
        kernel,
        in_specs=in_specs,
        out_specs=out_specs,
        out_shape=out_shape,
        scratch_shapes=scratch,
        input_output_aliases=aliases or {},
        name=name,
        cost_estimate=pl.CostEstimate(flops=flops, bytes_accessed=0, transcendentals=0),
        compiler_params=pltpu.CompilerParams(vmem_limit_bytes=vmem * MIB),
    )


def exchange(value, mask):
    count = lax.axis_size(AXIS)
    return lax.ppermute(value, AXIS, [(i, i ^ mask) for i in range(count)])


def in_vmem(shape, dtype):
    return pltpu.VMEM(shape, dtype)


def digit_of(bit):
    return (lax.axis_index(AXIS) // bit) % 2


def cores_kernel(held, got, out):
    out[...] = (held[...] + got[...].astype(F32)).astype(BF16)


def pieces_kernel(pieces, *rest, scale):
    rows = pieces.shape[0] // 4
    value = pieces[:rows, :].astype(F32)
    for k in range(1, 4):
        value = value + pieces[k * rows : (k + 1) * rows, :].astype(F32)
    rest[-1][...] = (value * scale).astype(BF16)


def add_kernel(held, got, *rest, scale, copies):
    out = rest[-1]
    rows = held.shape[0]
    value = ((held[...].astype(F32) + got[...].astype(F32)) * scale).astype(BF16)
    for k in range(copies):
        out[k * rows : (k + 1) * rows, :] = value


def place_kernel(held, *rest, own):
    out, wide, sem = rest[-3:]
    rows = held.shape[0]
    core = lax.axis_index(AXIS) % 2
    half = core if own else 1 - core
    wide[...] = held[...].astype(F32)
    copy = pltpu.make_async_copy(wide, out.at[pl.ds(pl.multiple_of(half * rows, rows), rows), :], sem)
    copy.start()
    copy.wait()


def sum_queries(kept, sent, beside, scale):
    count = lax.axis_size(AXIS)
    rows, width = kept.shape
    got = exchange(sent, 1)
    if count & (count - 1) or count < 16:
        half = kept + got.astype(F32)
        half = lax.psum(half, AXIS, axis_index_groups=[list(range(c, count, 2)) for c in range(2)])
        both = jnp.stack([half, exchange(half, 1)])
        both = jnp.where(lax.axis_index(AXIS) % 2 == 0, both, both[::-1])
        return both.reshape(2 * rows, width) * scale
    half = call(cores_kernel, "cores", [VMEM] * 2, in_vmem((rows, width), BF16))(kept, got)
    near = [0, 2, 4, 6]
    groups = [[first + step for step in near] for first in range(count) if first & 6 == 0]

    def swap_pieces(value):
        value = lax.all_to_all(value.reshape(4, rows // 4, width), AXIS, 0, 0, axis_index_groups=groups)
        return value.reshape(rows, width)

    bits = [1 << k for k in range(3, count.bit_length() - 1)]
    narrow = in_vmem((rows // 4, width), BF16)
    held = call(
        functools.partial(pieces_kernel, scale=1.0), "pieces", [VMEM, ANY], narrow
    )(swap_pieces(half), beside[0])
    for k, bit in enumerate(bits):
        last = k == len(bits) - 1
        after = [beside[1]] if k == 0 else []
        held = call(
            functools.partial(add_kernel, scale=scale if last else 1.0, copies=4 if last else 1),
            "add",
            [VMEM] * 2 + [ANY] * len(after),
            in_vmem((rows, width), BF16) if last else narrow,
        )(held, exchange(held, bit), *after)
    held, *_ = lax.optimization_barrier((swap_pieces(held), *beside[2:]))
    got = exchange(held, 1)

    def place(half, own, *begun):
        return call(
            functools.partial(place_kernel, own=own),
            "place",
            [VMEM] + [ANY] * len(begun),
            jax.ShapeDtypeStruct((2 * rows, width), F32),
            out_specs=ANY,
            scratch=[pltpu.VMEM((rows, width), F32), pltpu.SemaphoreType.DMA],
            aliases={1: 0} if begun else None,
        )(half, *begun)

    return place(got, False, place(held, True))


def per_device(embeddings, edge_tiles, neighbour, propensity, queries, positives):
    count = lax.axis_size(AXIS)
    blocks, _, block, _ = edge_tiles.shape
    labels_dev, width = embeddings.shape
    rows = queries.shape[0]
    lists = neighbour.T
    odd = range(1, count, 2)
    off_route = [(i, (i + 1) % count) for i in odd] + [((i + 1) % count, i) for i in odd]

    def off_swap(value):
        return lax.ppermute(value, AXIS, off_route)

    def on_swap(value):
        return exchange(value, 1)

    one = in_vmem((rows, block), BF16)
    pair = in_vmem((2, rows, block), BF16)
    third = -(-2 * rows // 48) * 16
    thirds = [in_vmem((size, block), BF16) for size in (third, third, 2 * rows - 2 * third)]
    full = (blocks, rows, block)
    scale = 1.0 / math.sqrt(width)

    off_a, queries, embeddings = call(
        functools.partial(project_kernel, scale=scale),
        "project",
        [HBM] * 3,
        [one, in_vmem(queries.shape, BF16), in_vmem(embeddings.shape, BF16)],
        scratch=[pltpu.SMEM(lists.shape, jnp.int32), pltpu.SemaphoreType.DMA((2 + blocks,))],
    )(*(pltpu.with_memory_space_constraint(x, pltpu.HBM) for x in (lists, queries, embeddings)))
    from_off_a = off_swap(off_a)
    own, off_b, *for_on = call(
        functools.partial(own_kernel, scale=scale),
        "own",
        [SMEM, VMEM, VMEM],
        [in_vmem(full, F32), one] + thirds,
    )(lists, queries, embeddings)
    from_on = [on_swap(piece) for piece in for_on]
    hits, tiles = call(
        hits_kernel,
        "hits",
        [VMEM, HBM],
        [in_vmem(full, BF16), in_vmem(edge_tiles.shape, BF16)],
        scratch=[pltpu.SemaphoreType.DMA],
    )(positives.T, pltpu.with_memory_space_constraint(edge_tiles, pltpu.HBM))
    from_off_b = off_swap(off_b)
    base = call(
        base_kernel,
        "base",
        [SMEM] + [VMEM] * 5,
        in_vmem(full, F32),
        scratch=[pltpu.VMEM((2, rows, block), BF16)],
    )(lists, own, tiles, *from_on)
    propensity = propensity.reshape(1, labels_dev)

    def signal_of(received, slot, *begun):
        return call(
            functools.partial(signal_kernel, slot=slot),
            "signal",
            [SMEM] + [VMEM] * (5 + len(begun)),
            [in_vmem(full, BF16), one],
            scratch=[pltpu.VMEM((rows, block), F32)],
            aliases={6: 0} if begun else None,
            flops=0 if begun else 2 * 10**9,
        )(lists, base, hits, propensity, received, tiles, *begun)

    signal, push_a = signal_of(from_off_a, 0)
    back_a = off_swap(push_a)
    signal, push_b = signal_of(from_off_b, 1, signal)
    back_b = off_swap(push_b)
    push_on = call(
        push_kernel,
        "push",
        [SMEM, VMEM, VMEM],
        thirds,
        scratch=[pltpu.VMEM((2, rows, block), F32)],
    )(lists, signal, tiles)
    back_on = [on_swap(piece) for piece in push_on]

    whole = in_vmem((rows, width), F32)
    part = call(query_kernel, "query", [VMEM] * 2, whole)(signal, embeddings)
    part = call(
        functools.partial(query_half_kernel, blocks=blocks),
        "query_half",
        [SMEM] + [VMEM] * 3,
        whole,
        flops=10**9,
    )(lists, part, back_a, embeddings)
    part, on = call(
        functools.partial(query_on_kernel, blocks=blocks), "query_on", [SMEM] + [VMEM] * 5, [whole, pair]
    )(lists, part, embeddings, *back_on)
    kept, sent = (in_vmem((rows // 2, width), kind) for kind in (F32, BF16))
    kept, sent = call(
        functools.partial(query_end_kernel, blocks=blocks),
        "query_end",
        [SMEM] + [VMEM] * 3,
        [kept, sent],
        scratch=[pltpu.VMEM((rows, width), F32)],
    )(lists, part, back_b, embeddings)

    def embed(g, *begun):
        return call(
            functools.partial(embed_kernel, blocks=blocks, g=g, scale=1.0 / math.sqrt(rows)),
            "embed",
            [SMEM] + [VMEM] * 5 + [ANY] * len(begun),
            [jax.ShapeDtypeStruct((labels_dev, width), BF16), in_vmem((8, 128), F32)],
            out_specs=[ANY, VMEM],
            scratch=[
                pltpu.VMEM((rows, block), F32),
                pltpu.VMEM((block, width), BF16),
                pltpu.SemaphoreType.DMA,
            ],
            aliases={6: 0} if begun else None,
        )(lists, signal, on, back_a, back_b, queries, *begun)

    begun, tokens = [], []
    for g in range(blocks):
        grad_embed, token = embed(g, *begun)
        begun = [grad_embed]
        tokens.append(token)
    grad_queries = sum_queries(kept, sent, tokens, 1.0 / math.sqrt(labels_dev * count))
    return (grad_embed, grad_queries)


def solution(mesh):
    placed = (
        P("labels", None),
        P("labels", None, None, None),
        P(),
        P("labels"),
        P("groups", None),
        P("groups", None),
    )
    return jax.shard_map(
        per_device,
        mesh=mesh,
        in_specs=placed,
        out_specs=(P(("groups", "labels"), None), P("groups", None)),
        check_vma=False,
    )
```

```python
import functools
import math

import jax
import jax.numpy as jnp
from jax import lax
from jax.experimental import pallas as pl
from jax.experimental.pallas import tpu as pltpu
from jax.sharding import PartitionSpec as P

AXIS = "labels"
BF16 = jnp.bfloat16
F32 = jnp.float32
NT = (((1,), (1,)), ((), ()))
NN = (((1,), (0,)), ((), ()))
TN = (((0,), (0,)), ((), ()))
MIB = 1024 * 1024

OFF, ON = True, False


def dot(a, b, dims):
    return lax.dot_general(a, b, dims, preferred_element_type=F32)


def own_side(device, off):
    odd = device % 2
    return 1 - odd if off else odd


def partner_of(device, count, off):
    ahead = jnp.where(device == count - 1, 0, device + 1)
    behind = jnp.where(device == 0, count - 1, device - 1)
    return jnp.where(own_side(device, off) == 0, ahead, behind)


def own_list(lists, blocks, off):
    device = lax.axis_index(AXIS)
    side = own_side(device, off)
    return [lists[side, device * blocks + g] for g in range(blocks)]


def slots_of(lists, blocks, off):
    named = own_list(lists, blocks, off)
    least = functools.reduce(jnp.minimum, named)
    return [(value != least).astype(jnp.int32) for value in named]


def named_by_partner(lists, blocks, off):
    device = lax.axis_index(AXIS)
    partner = partner_of(device, lax.axis_size(AXIS), off)
    side = 1 - own_side(device, off)
    named = [lists[side, partner * blocks + g] for g in range(blocks)]
    return functools.reduce(jnp.minimum, named), functools.reduce(jnp.maximum, named)


def tile_side(off):
    return own_side(lax.axis_index(AXIS), off)


def block_rows(ref, index, block):
    return ref[pl.ds(pl.multiple_of(index * block, block), block), :]


def project_kernel(lists, queries, embeddings, out, left, right, table, sem, *, scale):
    rows, block = out.shape
    blocks = right.shape[0] // block
    fetches = [pltpu.make_async_copy(lists, table, sem.at[0]), pltpu.make_async_copy(queries, left, sem.at[1])]
    for g in range(blocks):
        place = pl.ds(g * block, block)
        fetches.append(pltpu.make_async_copy(embeddings.at[place, :], right.at[place, :], sem.at[2 + g]))
    for fetch in fetches:
        fetch.start()
    fetches[0].wait()
    first, _ = named_by_partner(table, blocks, OFF)
    fetches[1].wait()
    place = pl.ds(pl.multiple_of(first * block, block), block)
    pltpu.make_async_copy(embeddings.at[place, :], right.at[place, :], sem.at[2 + first]).wait()
    out[...] = (dot(left[...], right[place, :], NT) * scale).astype(BF16)
    for g in range(blocks):

        @pl.when(g != first)
        def _():
            fetches[2 + g].wait()


def spans_of(pieces, rows):
    spans = []
    begin = 0
    for piece in pieces:
        end = begin + piece.shape[0]
        for slot in range(2):
            low, high = max(begin, slot * rows), min(end, (slot + 1) * rows)
            if low < high:
                inside = slice(low - slot * rows, high - slot * rows)
                spans.append((piece, slice(low - begin, high - begin), slot, inside))
        begin = end
    return spans


def write_pieces(pieces, value):
    rows = sum(piece.shape[0] for piece in pieces) // 2
    for piece, place, slot, inside in spans_of(pieces, rows):
        piece[place, :] = value(slot, inside).astype(BF16)


def gather_pieces(pieces, whole):
    for piece, place, slot, inside in spans_of(pieces, whole.shape[1]):
        whole[slot, inside] = piece[place, :]


def own_kernel(lists, queries, embeddings, own, off, *on, scale):
    blocks, _, block = own.shape
    for g in range(blocks):
        own[g] = dot(queries[...], embeddings[g * block : (g + 1) * block, :], NT) * scale
    _, second = named_by_partner(lists, blocks, OFF)
    off[...] = own[second].astype(BF16)
    first, second = named_by_partner(lists, blocks, ON)
    write_pieces(on, lambda slot, rows: own[(first, second)[slot], rows])


def hits_kernel(positives, tiles, out, kept, sem):
    fetch = pltpu.make_async_copy(tiles, kept, sem)
    fetch.start()
    blocks, rows, block = out.shape
    first = lax.axis_index(AXIS) * blocks * block
    ids = lax.broadcasted_iota(jnp.int32, (rows, block), 1)
    columns = jnp.transpose(positives[...]) - first
    for g in range(blocks):
        hits = jnp.zeros((rows, block), jnp.bool_)
        for column in range(positives.shape[0]):
            hits = jnp.logical_or(hits, ids + g * block == columns[:, column : column + 1])
        out[g] = jnp.where(hits, 1.0, 0.0).astype(BF16)
    fetch.wait()


def base_kernel(lists, own, tiles, *rest):
    *pieces, out, received = rest
    gather_pieces(pieces, received)
    blocks = out.shape[0]
    side = tile_side(ON)
    for g, slot in enumerate(slots_of(lists, blocks, ON)):
        out[g] = own[g] + dot(received[slot], tiles[g, side], NT)


def signal_kernel(lists, base, hits, propensity, received, tiles, *rest, slot):
    signal, push, total = rest[-3:]
    blocks, _, block = base.shape
    side = tile_side(OFF)
    total[...] = jnp.zeros_like(total)
    for g, taken in enumerate(slots_of(lists, blocks, OFF)):

        @pl.when(taken == slot)
        def _():
            scores = base[g] + dot(received[...], tiles[g, side], NT)
            inverse = 1.0 / propensity[:, g * block : (g + 1) * block]
            value = (jax.nn.sigmoid(scores) - hits[g].astype(F32) * inverse).astype(BF16)
            signal[g] = value
            total[...] += dot(value, tiles[g, side], NN)

    push[...] = total[...].astype(BF16)


def push_kernel(lists, signal, tiles, *rest):
    *pieces, total = rest
    blocks = signal.shape[0]
    side = tile_side(ON)
    total[...] = jnp.zeros_like(total)
    for g, slot in enumerate(slots_of(lists, blocks, ON)):
        total[slot] += dot(signal[g], tiles[g, side], NN)
    write_pieces(pieces, lambda slot, rows: total[slot, rows])


def query_kernel(signal, embeddings, out):
    blocks, _, block = signal.shape
    total = dot(signal[0], embeddings[0:block, :], NN)
    for g in range(1, blocks):
        total += dot(signal[g], embeddings[g * block : (g + 1) * block, :], NN)
    out[...] = total


def query_half_kernel(lists, part, received, embeddings, out, *, blocks):
    first, _ = named_by_partner(lists, blocks, OFF)
    out[...] = part[...] + dot(received[...], block_rows(embeddings, first, received.shape[1]), NN)


def query_on_kernel(lists, part, embeddings, *rest, blocks):
    *pieces, out, received = rest
    gather_pieces(pieces, received)
    block = received.shape[2]
    first, second = named_by_partner(lists, blocks, ON)
    out[...] = (
        part[...]
        + dot(received[0], block_rows(embeddings, first, block), NN)
        + dot(received[1], block_rows(embeddings, second, block), NN)
    )


def query_end_kernel(lists, part, received, embeddings, kept, sent, total, *, blocks):
    _, second = named_by_partner(lists, blocks, OFF)
    total[...] = part[...] + dot(received[...], block_rows(embeddings, second, received.shape[1]), NN)
    rows = kept.shape[0]
    core = lax.axis_index(AXIS) % 2
    kept[...] = total[pl.ds(pl.multiple_of(core * rows, rows), rows), :]
    sent[...] = total[pl.ds(pl.multiple_of((1 - core) * rows, rows), rows), :].astype(BF16)


def embed_kernel(lists, signal, on, off_a, off_b, queries, *rest, blocks, g, scale):
    if g == 0:
        ready, token, total = rest
    else:
        before = rest[0]
        out, ready, token, total, sem = rest[-5:]
    rows, block = total.shape
    writes = []

    def write(source, index, slot):
        writes.append(pltpu.make_async_copy(source, out.at[pl.ds(index * block, block), :], sem.at[slot]))
        writes[-1].start()

    if g > 0:
        write(before, g - 1, 0)
    token[...] = jnp.zeros_like(token)
    total[...] = signal[g].astype(F32)
    named = named_by_partner(lists, blocks, ON) + named_by_partner(lists, blocks, OFF)
    for received, index in zip((on.at[0], on.at[1], off_a, off_b), named):

        @pl.when(index == g)
        def _():
            total[...] += received[...].astype(F32)

    ready[...] = (dot(total[...].astype(BF16), queries[...], TN) * scale).astype(BF16)
    if g == blocks - 1:
        write(ready, g, 1)
    for copy in writes:
        copy.wait()


VMEM = pl.BlockSpec(memory_space=pltpu.VMEM)
SMEM = pl.BlockSpec(memory_space=pltpu.SMEM)
ANY = pl.BlockSpec(memory_space=pl.ANY)
HBM = pl.BlockSpec(memory_space=pltpu.HBM)


def call(kernel, name, in_specs, out_shape, out_specs=None, scratch=(), aliases=None, vmem=12, flops=0):
    if out_specs is None:
        out_specs = jax.tree.map(lambda _: VMEM, out_shape)
    return pl.pallas_call(
        kernel,
        in_specs=in_specs,
        out_specs=out_specs,
        out_shape=out_shape,
        scratch_shapes=scratch,
        input_output_aliases=aliases or {},
        name=name,
        cost_estimate=pl.CostEstimate(flops=flops, bytes_accessed=0, transcendentals=0),
        compiler_params=pltpu.CompilerParams(vmem_limit_bytes=vmem * MIB),
    )


def exchange(value, mask):
    count = lax.axis_size(AXIS)
    return lax.ppermute(value, AXIS, [(i, i ^ mask) for i in range(count)])


def in_vmem(shape, dtype):
    return pltpu.VMEM(shape, dtype)


def digit_of(bit):
    return (lax.axis_index(AXIS) // bit) % 2


def halve_kernel(held, got, *outs, bits):
    total = outs[-1]
    total[...] = held[...] + got[...].astype(F32)
    rows = outs[0].shape[0]
    for chain, bit in enumerate(bits):
        kept, sent = outs[2 * chain], outs[2 * chain + 1]
        begin = 2 * chain * rows
        digit = digit_of(bit)
        kept[...] = total[pl.ds(pl.multiple_of(begin + digit * rows, rows), rows), :]
        sent[...] = total[pl.ds(pl.multiple_of(begin + (1 - digit) * rows, rows), rows), :].astype(BF16)


def add_kernel(held, got, *rest, scale):
    rest[-1][...] = ((held[...].astype(F32) + got[...].astype(F32)) * scale).astype(BF16)


def join_kernel(held, got, *rest, bit):
    out = rest[-1]
    rows = held.shape[0]
    begin = out.shape[0] - 2 * rows
    if begin:
        out[:begin, :] = rest[0][...]
    digit = digit_of(bit)
    out[pl.ds(pl.multiple_of(begin + digit * rows, rows), rows), :] = held[...]
    out[pl.ds(pl.multiple_of(begin + (1 - digit) * rows, rows), rows), :] = got[...]


def place_kernel(held, *rest, own):
    out, wide, sem = rest[-3:]
    rows = held.shape[0]
    core = lax.axis_index(AXIS) % 2
    half = core if own else 1 - core
    wide[...] = held[...].astype(F32)
    copy = pltpu.make_async_copy(wide, out.at[pl.ds(pl.multiple_of(half * rows, rows), rows), :], sem)
    copy.start()
    copy.wait()


def sum_queries(kept, sent, beside, scale):
    count = lax.axis_size(AXIS)
    rows, width = kept.shape
    got = exchange(sent, 1)
    if count & (count - 1) or count < 8:
        half = kept + got.astype(F32)
        half = lax.psum(half, AXIS, axis_index_groups=[list(range(c, count, 2)) for c in range(2)])
        both = jnp.stack([half, exchange(half, 1)])
        both = jnp.where(lax.axis_index(AXIS) % 2 == 0, both, both[::-1])
        return both.reshape(2 * rows, width) * scale
    bits = [1 << k for k in range(1, count.bit_length() - 1)]
    orders = [[bits[0], *bits[2:], bits[1]], [bits[1], bits[0], *bits[2:]]]
    ends = [order[0] for order in orders]
    wide, narrow = in_vmem((rows // 4, width), F32), in_vmem((rows // 4, width), BF16)
    kept_a, sent_a, kept_b, sent_b = call(
        functools.partial(halve_kernel, bits=ends),
        "halve",
        [VMEM] * 2,
        [wide, narrow, wide, narrow],
        scratch=[pltpu.VMEM((rows, width), F32)],
    )(kept, got)
    held, sent = [kept_a, kept_b], [sent_a, sent_b]
    for k in range(len(bits)):
        got = [exchange(piece, order[k]) for piece, order in zip(sent, orders)]
        for chain in range(2):
            after = beside[k : k + 1] if chain == 0 else []
            held[chain] = call(
                functools.partial(add_kernel, scale=scale if k == len(bits) - 1 else 1.0),
                "add",
                [VMEM] * 2 + [ANY] * len(after),
                narrow,
            )(held[chain], got[chain], *after)
        sent = list(held)
    got = [exchange(piece, bit) for piece, bit in zip(held, ends)]
    joined = []
    for chain, bit in enumerate(ends):
        rows_out = (chain + 1) * rows // 2
        after = beside[len(bits) :] if chain == 0 else []
        joined = [
            call(
                functools.partial(join_kernel, bit=bit),
                "join",
                [VMEM] * (2 + len(joined)) + [ANY] * len(after),
                in_vmem((rows_out, width), BF16),
                flops=2 * 10**8,
            )(held[chain], got[chain], *joined, *after)
        ]
    held = joined[0]
    got = exchange(held, 1)

    def place(half, own, *begun):
        return call(
            functools.partial(place_kernel, own=own),
            "place",
            [VMEM] + [ANY] * len(begun),
            jax.ShapeDtypeStruct((2 * rows, width), F32),
            out_specs=ANY,
            scratch=[pltpu.VMEM((rows, width), F32), pltpu.SemaphoreType.DMA],
            aliases={1: 0} if begun else None,
        )(half, *begun)

    return place(got, False, place(held, True))


def per_device(embeddings, edge_tiles, neighbour, propensity, queries, positives):
    count = lax.axis_size(AXIS)
    blocks, _, block, _ = edge_tiles.shape
    labels_dev, width = embeddings.shape
    rows = queries.shape[0]
    lists = neighbour.T
    odd = range(1, count, 2)
    off_route = [(i, (i + 1) % count) for i in odd] + [((i + 1) % count, i) for i in odd]

    def off_swap(value):
        return lax.ppermute(value, AXIS, off_route)

    def on_swap(value):
        return exchange(value, 1)

    one = in_vmem((rows, block), BF16)
    pair = in_vmem((2, rows, block), BF16)
    third = -(-2 * rows // 48) * 16
    thirds = [in_vmem((size, block), BF16) for size in (third, third, 2 * rows - 2 * third)]
    full = (blocks, rows, block)
    scale = 1.0 / math.sqrt(width)

    off_a, queries, embeddings = call(
        functools.partial(project_kernel, scale=scale),
        "project",
        [HBM] * 3,
        [one, in_vmem(queries.shape, BF16), in_vmem(embeddings.shape, BF16)],
        scratch=[pltpu.SMEM(lists.shape, jnp.int32), pltpu.SemaphoreType.DMA((2 + blocks,))],
    )(*(pltpu.with_memory_space_constraint(x, pltpu.HBM) for x in (lists, queries, embeddings)))
    from_off_a = off_swap(off_a)
    own, off_b, *for_on = call(
        functools.partial(own_kernel, scale=scale),
        "own",
        [SMEM, VMEM, VMEM],
        [in_vmem(full, F32), one] + thirds,
    )(lists, queries, embeddings)
    from_on = [on_swap(piece) for piece in for_on]
    hits, tiles = call(
        hits_kernel,
        "hits",
        [VMEM, HBM],
        [in_vmem(full, BF16), in_vmem(edge_tiles.shape, BF16)],
        scratch=[pltpu.SemaphoreType.DMA],
    )(positives.T, pltpu.with_memory_space_constraint(edge_tiles, pltpu.HBM))
    from_off_b = off_swap(off_b)
    base = call(
        base_kernel,
        "base",
        [SMEM] + [VMEM] * 5,
        in_vmem(full, F32),
        scratch=[pltpu.VMEM((2, rows, block), BF16)],
    )(lists, own, tiles, *from_on)
    propensity = propensity.reshape(1, labels_dev)

    def signal_of(received, slot, *begun):
        return call(
            functools.partial(signal_kernel, slot=slot),
            "signal",
            [SMEM] + [VMEM] * (5 + len(begun)),
            [in_vmem(full, BF16), one],
            scratch=[pltpu.VMEM((rows, block), F32)],
            aliases={6: 0} if begun else None,
            flops=0 if begun else 2 * 10**9,
        )(lists, base, hits, propensity, received, tiles, *begun)

    signal, push_a = signal_of(from_off_a, 0)
    back_a = off_swap(push_a)
    signal, push_b = signal_of(from_off_b, 1, signal)
    back_b = off_swap(push_b)
    push_on = call(
        push_kernel,
        "push",
        [SMEM, VMEM, VMEM],
        thirds,
        scratch=[pltpu.VMEM((2, rows, block), F32)],
    )(lists, signal, tiles)
    back_on = [on_swap(piece) for piece in push_on]

    whole = in_vmem((rows, width), F32)
    part = call(query_kernel, "query", [VMEM] * 2, whole)(signal, embeddings)
    part = call(
        functools.partial(query_half_kernel, blocks=blocks),
        "query_half",
        [SMEM] + [VMEM] * 3,
        whole,
        flops=10**9,
    )(lists, part, back_a, embeddings)
    part, on = call(
        functools.partial(query_on_kernel, blocks=blocks), "query_on", [SMEM] + [VMEM] * 5, [whole, pair]
    )(lists, part, embeddings, *back_on)
    kept, sent = (in_vmem((rows // 2, width), kind) for kind in (F32, BF16))
    kept, sent = call(
        functools.partial(query_end_kernel, blocks=blocks),
        "query_end",
        [SMEM] + [VMEM] * 3,
        [kept, sent],
        scratch=[pltpu.VMEM((rows, width), F32)],
    )(lists, part, back_b, embeddings)

    ready = in_vmem((block, width), BF16)
    written = jax.ShapeDtypeStruct((labels_dev, width), BF16)
    outs, tokens = [], []
    for g in range(blocks):
        *outs, token = call(
            functools.partial(embed_kernel, blocks=blocks, g=g, scale=1.0 / math.sqrt(rows)),
            "embed",
            [SMEM] + [VMEM] * (5 + min(g, 1)) + [ANY] * (len(outs) - 1),
            ([written] if g else []) + [ready, in_vmem((8, 128), F32)],
            out_specs=([ANY] if g else []) + [VMEM] * 2,
            scratch=[pltpu.VMEM((rows, block), F32)] + ([pltpu.SemaphoreType.DMA((2,))] if g else []),
            aliases={7: 0} if g > 1 else None,
        )(lists, signal, on, back_a, back_b, queries, *outs[::-1])
        tokens.append(token)
    grad_embed = outs[0]
    grad_queries = sum_queries(kept, sent, tokens, 1.0 / math.sqrt(labels_dev * count))
    return (grad_embed, grad_queries)


def solution(mesh):
    placed = (
        P("labels", None),
        P("labels", None, None, None),
        P(),
        P("labels"),
        P("groups", None),
        P("groups", None),
    )
    return jax.shard_map(
        per_device,
        mesh=mesh,
        in_specs=placed,
        out_specs=(P(("groups", "labels"), None), P("groups", None)),
        check_vma=False,
    )
```

```python
import functools
import math

import jax
import jax.numpy as jnp
from jax import lax
from jax.experimental import pallas as pl
from jax.experimental.pallas import tpu as pltpu
from jax.sharding import PartitionSpec as P

AXIS = "labels"
BF16 = jnp.bfloat16
F32 = jnp.float32
NT = (((1,), (1,)), ((), ()))
NN = (((1,), (0,)), ((), ()))
TN = (((0,), (0,)), ((), ()))
MIB = 1024 * 1024

OFF, ON = True, False


def dot(a, b, dims):
    return lax.dot_general(a, b, dims, preferred_element_type=F32)


def own_side(device, off):
    odd = device % 2
    return 1 - odd if off else odd


def partner_of(device, count, off):
    ahead = jnp.where(device == count - 1, 0, device + 1)
    behind = jnp.where(device == 0, count - 1, device - 1)
    return jnp.where(own_side(device, off) == 0, ahead, behind)


def own_list(lists, blocks, off):
    device = lax.axis_index(AXIS)
    side = own_side(device, off)
    return [lists[side, device * blocks + g] for g in range(blocks)]


def slots_of(lists, blocks, off):
    named = own_list(lists, blocks, off)
    least = functools.reduce(jnp.minimum, named)
    return [(value != least).astype(jnp.int32) for value in named]


def named_by_partner(lists, blocks, off):
    device = lax.axis_index(AXIS)
    partner = partner_of(device, lax.axis_size(AXIS), off)
    side = 1 - own_side(device, off)
    named = [lists[side, partner * blocks + g] for g in range(blocks)]
    return functools.reduce(jnp.minimum, named), functools.reduce(jnp.maximum, named)


def tile_side(off):
    return own_side(lax.axis_index(AXIS), off)


def block_rows(ref, index, block):
    return ref[pl.ds(pl.multiple_of(index * block, block), block), :]


def project_kernel(lists, queries, embeddings, out, left, right, table, sem, *, scale):
    rows, block = out.shape
    blocks = right.shape[0] // block
    fetches = [pltpu.make_async_copy(lists, table, sem.at[0]), pltpu.make_async_copy(queries, left, sem.at[1])]
    for g in range(blocks):
        place = pl.ds(g * block, block)
        fetches.append(pltpu.make_async_copy(embeddings.at[place, :], right.at[place, :], sem.at[2 + g]))
    for fetch in fetches:
        fetch.start()
    fetches[0].wait()
    first, _ = named_by_partner(table, blocks, OFF)
    fetches[1].wait()
    place = pl.ds(pl.multiple_of(first * block, block), block)
    pltpu.make_async_copy(embeddings.at[place, :], right.at[place, :], sem.at[2 + first]).wait()
    out[...] = (dot(left[...], right[place, :], NT) * scale).astype(BF16)
    for g in range(blocks):

        @pl.when(g != first)
        def _():
            fetches[2 + g].wait()


def spans_of(pieces, rows):
    spans = []
    begin = 0
    for piece in pieces:
        end = begin + piece.shape[0]
        for slot in range(2):
            low, high = max(begin, slot * rows), min(end, (slot + 1) * rows)
            if low < high:
                inside = slice(low - slot * rows, high - slot * rows)
                spans.append((piece, slice(low - begin, high - begin), slot, inside))
        begin = end
    return spans


def write_pieces(pieces, value):
    rows = sum(piece.shape[0] for piece in pieces) // 2
    for piece, place, slot, inside in spans_of(pieces, rows):
        piece[place, :] = value(slot, inside).astype(BF16)


def gather_pieces(pieces, whole):
    for piece, place, slot, inside in spans_of(pieces, whole.shape[1]):
        whole[slot, inside] = piece[place, :]


def own_kernel(lists, queries, embeddings, own, off, *on, scale):
    blocks, _, block = own.shape
    for g in range(blocks):
        own[g] = dot(queries[...], embeddings[g * block : (g + 1) * block, :], NT) * scale
    _, second = named_by_partner(lists, blocks, OFF)
    off[...] = own[second].astype(BF16)
    first, second = named_by_partner(lists, blocks, ON)
    write_pieces(on, lambda slot, rows: own[(first, second)[slot], rows])


def hits_kernel(positives, tiles, out, kept, sem):
    fetch = pltpu.make_async_copy(tiles, kept, sem)
    fetch.start()
    blocks, rows, block = out.shape
    first = lax.axis_index(AXIS) * blocks * block
    ids = lax.broadcasted_iota(jnp.int32, (rows, block), 1)
    columns = jnp.transpose(positives[...]) - first
    for g in range(blocks):
        hits = jnp.zeros((rows, block), jnp.bool_)
        for column in range(positives.shape[0]):
            hits = jnp.logical_or(hits, ids + g * block == columns[:, column : column + 1])
        out[g] = jnp.where(hits, 1.0, 0.0).astype(BF16)
    fetch.wait()


def base_kernel(lists, own, tiles, *rest):
    *pieces, out, received = rest
    gather_pieces(pieces, received)
    blocks = out.shape[0]
    side = tile_side(ON)
    for g, slot in enumerate(slots_of(lists, blocks, ON)):
        out[g] = own[g] + dot(received[slot], tiles[g, side], NT)


def signal_kernel(lists, base, hits, propensity, received, tiles, *rest, slot):
    signal, push, total = rest[-3:]
    blocks, _, block = base.shape
    side = tile_side(OFF)
    total[...] = jnp.zeros_like(total)
    for g, taken in enumerate(slots_of(lists, blocks, OFF)):

        @pl.when(taken == slot)
        def _():
            scores = base[g] + dot(received[...], tiles[g, side], NT)
            inverse = 1.0 / propensity[:, g * block : (g + 1) * block]
            value = (jax.nn.sigmoid(scores) - hits[g].astype(F32) * inverse).astype(BF16)
            signal[g] = value
            total[...] += dot(value, tiles[g, side], NN)

    push[...] = total[...].astype(BF16)


def push_kernel(lists, signal, tiles, *rest):
    *pieces, total = rest
    blocks = signal.shape[0]
    side = tile_side(ON)
    total[...] = jnp.zeros_like(total)
    for g, slot in enumerate(slots_of(lists, blocks, ON)):
        total[slot] += dot(signal[g], tiles[g, side], NN)
    write_pieces(pieces, lambda slot, rows: total[slot, rows])


def query_kernel(signal, embeddings, out):
    blocks, _, block = signal.shape
    total = dot(signal[0], embeddings[0:block, :], NN)
    for g in range(1, blocks):
        total += dot(signal[g], embeddings[g * block : (g + 1) * block, :], NN)
    out[...] = total


def query_half_kernel(lists, part, received, embeddings, out, *, blocks):
    first, _ = named_by_partner(lists, blocks, OFF)
    out[...] = part[...] + dot(received[...], block_rows(embeddings, first, received.shape[1]), NN)


def query_on_kernel(lists, part, embeddings, *rest, blocks):
    *pieces, out, received = rest
    gather_pieces(pieces, received)
    block = received.shape[2]
    first, second = named_by_partner(lists, blocks, ON)
    out[...] = (
        part[...]
        + dot(received[0], block_rows(embeddings, first, block), NN)
        + dot(received[1], block_rows(embeddings, second, block), NN)
    )


def query_end_kernel(lists, part, received, embeddings, out, *, blocks, own):
    _, second = named_by_partner(lists, blocks, OFF)
    rows = out.shape[0]
    core = lax.axis_index(AXIS) % 2
    half = core if own else 1 - core
    place = pl.ds(pl.multiple_of(half * rows, rows), rows)
    right = block_rows(embeddings, second, received.shape[1])
    out[...] = (part[place, :] + dot(received[place, :], right, NN)).astype(out.dtype)


def embed_kernel(lists, signal, on, off_a, off_b, queries, *rest, blocks, g, scale):
    if g == 0:
        ready, token, total = rest
    else:
        before = rest[0]
        out, ready, token, total, sem = rest[-5:]
    rows, block = total.shape
    writes = []

    def write(source, index, slot):
        writes.append(pltpu.make_async_copy(source, out.at[pl.ds(index * block, block), :], sem.at[slot]))
        writes[-1].start()

    if g > 0:
        write(before, g - 1, 0)
    token[...] = jnp.zeros_like(token)
    total[...] = signal[g].astype(F32)
    named = named_by_partner(lists, blocks, ON) + named_by_partner(lists, blocks, OFF)
    for received, index in zip((on.at[0], on.at[1], off_a, off_b), named):

        @pl.when(index == g)
        def _():
            total[...] += received[...].astype(F32)

    ready[...] = (dot(total[...].astype(BF16), queries[...], TN) * scale).astype(BF16)
    if g == blocks - 1:
        write(ready, g, 1)
    for copy in writes:
        copy.wait()


VMEM = pl.BlockSpec(memory_space=pltpu.VMEM)
SMEM = pl.BlockSpec(memory_space=pltpu.SMEM)
ANY = pl.BlockSpec(memory_space=pl.ANY)
HBM = pl.BlockSpec(memory_space=pltpu.HBM)


def call(kernel, name, in_specs, out_shape, out_specs=None, scratch=(), aliases=None, vmem=12, flops=0):
    if out_specs is None:
        out_specs = jax.tree.map(lambda _: VMEM, out_shape)
    return pl.pallas_call(
        kernel,
        in_specs=in_specs,
        out_specs=out_specs,
        out_shape=out_shape,
        scratch_shapes=scratch,
        input_output_aliases=aliases or {},
        name=name,
        cost_estimate=pl.CostEstimate(flops=flops, bytes_accessed=0, transcendentals=0),
        compiler_params=pltpu.CompilerParams(vmem_limit_bytes=vmem * MIB),
    )


def exchange(value, mask):
    count = lax.axis_size(AXIS)
    return lax.ppermute(value, AXIS, [(i, i ^ mask) for i in range(count)])


def in_vmem(shape, dtype):
    return pltpu.VMEM(shape, dtype)


def digit_of(bit):
    return (lax.axis_index(AXIS) // bit) % 2


def halve_kernel(held, got, *outs, bits):
    total = outs[-1]
    total[...] = held[...] + got[...].astype(F32)
    rows = outs[0].shape[0]
    for chain, bit in enumerate(bits):
        kept, sent = outs[2 * chain], outs[2 * chain + 1]
        begin = 2 * chain * rows
        digit = digit_of(bit)
        kept[...] = total[pl.ds(pl.multiple_of(begin + digit * rows, rows), rows), :]
        sent[...] = total[pl.ds(pl.multiple_of(begin + (1 - digit) * rows, rows), rows), :].astype(BF16)


def add_kernel(held, got, *rest, scale):
    rest[-1][...] = ((held[...].astype(F32) + got[...].astype(F32)) * scale).astype(BF16)


def join_kernel(held, got, *rest, bit):
    out = rest[-1]
    rows = held.shape[0]
    digit = digit_of(bit)
    out[pl.ds(pl.multiple_of(digit * rows, rows), rows), :] = held[...]
    out[pl.ds(pl.multiple_of((1 - digit) * rows, rows), rows), :] = got[...]


def place_kernel(*refs, places):
    out, wide, sem = refs[-3:]
    rows = refs[0].shape[0]
    core = lax.axis_index(AXIS) % 2
    copies = []
    for k, (chain, own) in enumerate(places):
        wide[k] = refs[k][...].astype(F32)
        half = core if own else 1 - core
        begin = pl.multiple_of((2 * half + chain) * rows, rows)
        copies.append(pltpu.make_async_copy(wide.at[k], out.at[pl.ds(begin, rows), :], sem.at[k]))
        copies[-1].start()
    for copy in copies:
        copy.wait()


def sum_queries(kept, sent, beside, scale):
    count = lax.axis_size(AXIS)
    rows, width = kept.shape
    got = exchange(sent, 1)
    if count & (count - 1) or count < 8:
        half = kept + got.astype(F32)
        half = lax.psum(half, AXIS, axis_index_groups=[list(range(c, count, 2)) for c in range(2)])
        both = jnp.stack([half, exchange(half, 1)])
        both = jnp.where(lax.axis_index(AXIS) % 2 == 0, both, both[::-1])
        return both.reshape(2 * rows, width) * scale
    bits = [1 << k for k in range(1, count.bit_length() - 1)]
    orders = [[bits[0], *bits[2:], bits[1]], [bits[1], bits[0], *bits[2:]]]
    ends = [order[0] for order in orders]
    wide, narrow = in_vmem((rows // 4, width), F32), in_vmem((rows // 4, width), BF16)
    kept_a, sent_a, kept_b, sent_b = call(
        functools.partial(halve_kernel, bits=ends),
        "halve",
        [VMEM] * 2,
        [wide, narrow, wide, narrow],
        scratch=[pltpu.VMEM((rows, width), F32)],
    )(kept, got)
    held, sent = [kept_a, kept_b], [sent_a, sent_b]
    for k in range(len(bits)):
        got = [exchange(piece, order[k]) for piece, order in zip(sent, orders)]
        for chain in range(2):
            after = beside[k : k + 1] if chain == 0 else []
            held[chain] = call(
                functools.partial(add_kernel, scale=scale if k == len(bits) - 1 else 1.0),
                "add",
                [VMEM] * 2 + [ANY] * len(after),
                narrow,
            )(held[chain], got[chain], *after)
        sent = list(held)
    got = [exchange(piece, bit) for piece, bit in zip(held, ends)]
    joined, swapped = [], []
    for chain, bit in enumerate(ends):
        after = beside[len(bits) :] if chain == 0 else joined
        joined.append(
            call(
                functools.partial(join_kernel, bit=bit),
                "join",
                [VMEM] * 2 + [ANY] * len(after),
                in_vmem((rows // 2, width), BF16),
                flops=2 * 10**8,
            )(held[chain], got[chain], *after)
        )
        swapped.append(exchange(joined[chain], 1))

    def place(values, places, *begun):
        return call(
            functools.partial(place_kernel, places=places),
            "place",
            [VMEM] * len(values) + [ANY] * len(begun),
            jax.ShapeDtypeStruct((2 * rows, width), F32),
            out_specs=ANY,
            scratch=[
                pltpu.VMEM((len(values), rows // 2, width), F32),
                pltpu.SemaphoreType.DMA((len(values),)),
            ],
            aliases={len(values): 0} if begun else None,
        )(*values, *begun)

    early = place([joined[0], joined[1], swapped[0]], [(0, True), (1, True), (0, False)])
    return place([swapped[1]], [(1, False)], early)


def per_device(embeddings, edge_tiles, neighbour, propensity, queries, positives):
    count = lax.axis_size(AXIS)
    blocks, _, block, _ = edge_tiles.shape
    labels_dev, width = embeddings.shape
    rows = queries.shape[0]
    lists = neighbour.T
    odd = range(1, count, 2)
    off_route = [(i, (i + 1) % count) for i in odd] + [((i + 1) % count, i) for i in odd]

    def off_swap(value):
        return lax.ppermute(value, AXIS, off_route)

    def on_swap(value):
        return exchange(value, 1)

    one = in_vmem((rows, block), BF16)
    pair = in_vmem((2, rows, block), BF16)
    third = -(-2 * rows // 48) * 16
    thirds = [in_vmem((size, block), BF16) for size in (third, third, 2 * rows - 2 * third)]
    full = (blocks, rows, block)
    scale = 1.0 / math.sqrt(width)

    off_a, queries, embeddings = call(
        functools.partial(project_kernel, scale=scale),
        "project",
        [HBM] * 3,
        [one, in_vmem(queries.shape, BF16), in_vmem(embeddings.shape, BF16)],
        scratch=[pltpu.SMEM(lists.shape, jnp.int32), pltpu.SemaphoreType.DMA((2 + blocks,))],
    )(*(pltpu.with_memory_space_constraint(x, pltpu.HBM) for x in (lists, queries, embeddings)))
    from_off_a = off_swap(off_a)
    own, off_b, *for_on = call(
        functools.partial(own_kernel, scale=scale),
        "own",
        [SMEM, VMEM, VMEM],
        [in_vmem(full, F32), one] + thirds,
    )(lists, queries, embeddings)
    from_on = [on_swap(piece) for piece in for_on]
    hits, tiles = call(
        hits_kernel,
        "hits",
        [VMEM, HBM],
        [in_vmem(full, BF16), in_vmem(edge_tiles.shape, BF16)],
        scratch=[pltpu.SemaphoreType.DMA],
    )(positives.T, pltpu.with_memory_space_constraint(edge_tiles, pltpu.HBM))
    from_off_b = off_swap(off_b)
    base = call(
        base_kernel,
        "base",
        [SMEM] + [VMEM] * 5,
        in_vmem(full, F32),
        scratch=[pltpu.VMEM((2, rows, block), BF16)],
    )(lists, own, tiles, *from_on)
    propensity = propensity.reshape(1, labels_dev)

    def signal_of(received, slot, *begun):
        return call(
            functools.partial(signal_kernel, slot=slot),
            "signal",
            [SMEM] + [VMEM] * (5 + len(begun)),
            [in_vmem(full, BF16), one],
            scratch=[pltpu.VMEM((rows, block), F32)],
            aliases={6: 0} if begun else None,
            flops=0 if begun else 2 * 10**9,
        )(lists, base, hits, propensity, received, tiles, *begun)

    signal, push_a = signal_of(from_off_a, 0)
    back_a = off_swap(push_a)
    signal, push_b = signal_of(from_off_b, 1, signal)
    back_b = off_swap(push_b)
    push_on = call(
        push_kernel,
        "push",
        [SMEM, VMEM, VMEM],
        thirds,
        scratch=[pltpu.VMEM((2, rows, block), F32)],
    )(lists, signal, tiles)
    back_on = [on_swap(piece) for piece in push_on]

    whole = in_vmem((rows, width), F32)
    part = call(query_kernel, "query", [VMEM] * 2, whole)(signal, embeddings)
    part = call(
        functools.partial(query_half_kernel, blocks=blocks),
        "query_half",
        [SMEM] + [VMEM] * 3,
        whole,
        flops=10**9,
    )(lists, part, back_a, embeddings)
    part, on = call(
        functools.partial(query_on_kernel, blocks=blocks), "query_on", [SMEM] + [VMEM] * 5, [whole, pair]
    )(lists, part, embeddings, *back_on)
    def query_end(own, kind):
        return call(
            functools.partial(query_end_kernel, blocks=blocks, own=own),
            "query_end",
            [SMEM] + [VMEM] * 3,
            in_vmem((rows // 2, width), kind),
        )(lists, part, back_b, embeddings)

    sent, kept = query_end(False, BF16), query_end(True, F32)
    ready = in_vmem((block, width), BF16)
    written = jax.ShapeDtypeStruct((labels_dev, width), BF16)
    outs, tokens = [], []
    for g in range(blocks):
        *outs, token = call(
            functools.partial(embed_kernel, blocks=blocks, g=g, scale=1.0 / math.sqrt(rows)),
            "embed",
            [SMEM] + [VMEM] * (5 + min(g, 1)) + [ANY] * (len(outs) - 1),
            ([written] if g else []) + [ready, in_vmem((8, 128), F32)],
            out_specs=([ANY] if g else []) + [VMEM] * 2,
            scratch=[pltpu.VMEM((rows, block), F32)] + ([pltpu.SemaphoreType.DMA((2,))] if g else []),
            aliases={7: 0} if g > 1 else None,
        )(lists, signal, on, back_a, back_b, queries, *outs[::-1])
        tokens.append(token)
    grad_embed = outs[0]
    grad_queries = sum_queries(kept, sent, tokens, 1.0 / math.sqrt(labels_dev * count))
    return (grad_embed, grad_queries)


def solution(mesh):
    placed = (
        P("labels", None),
        P("labels", None, None, None),
        P(),
        P("labels"),
        P("groups", None),
        P("groups", None),
    )
    return jax.shard_map(
        per_device,
        mesh=mesh,
        in_specs=placed,
        out_specs=(P(("groups", "labels"), None), P("groups", None)),
        check_vma=False,
    )
```

```python
import functools
import math

import jax
import jax.numpy as jnp
from jax import lax
from jax.experimental import pallas as pl
from jax.experimental.pallas import tpu as pltpu
from jax.sharding import PartitionSpec as P

AXIS = "labels"
BF16 = jnp.bfloat16
F32 = jnp.float32
NT = (((1,), (1,)), ((), ()))
NN = (((1,), (0,)), ((), ()))
TN = (((0,), (0,)), ((), ()))
MIB = 1024 * 1024

OFF, ON = True, False


def dot(a, b, dims):
    return lax.dot_general(a, b, dims, preferred_element_type=F32)


def own_side(device, off):
    odd = device % 2
    return 1 - odd if off else odd


def partner_of(device, count, off):
    ahead = jnp.where(device == count - 1, 0, device + 1)
    behind = jnp.where(device == 0, count - 1, device - 1)
    return jnp.where(own_side(device, off) == 0, ahead, behind)


def own_list(lists, blocks, off):
    device = lax.axis_index(AXIS)
    side = own_side(device, off)
    return [lists[side, device * blocks + g] for g in range(blocks)]


def slots_of(lists, blocks, off):
    named = own_list(lists, blocks, off)
    least = functools.reduce(jnp.minimum, named)
    return [(value != least).astype(jnp.int32) for value in named]


def named_by_partner(lists, blocks, off):
    device = lax.axis_index(AXIS)
    partner = partner_of(device, lax.axis_size(AXIS), off)
    side = 1 - own_side(device, off)
    named = [lists[side, partner * blocks + g] for g in range(blocks)]
    return functools.reduce(jnp.minimum, named), functools.reduce(jnp.maximum, named)


def tile_side(off):
    return own_side(lax.axis_index(AXIS), off)


def block_rows(ref, index, block):
    return ref[pl.ds(pl.multiple_of(index * block, block), block), :]


def project_kernel(lists, queries, embeddings, out, left, right, table, sem, *, scale):
    rows, block = out.shape
    blocks = right.shape[0] // block
    fetches = [pltpu.make_async_copy(lists, table, sem.at[0]), pltpu.make_async_copy(queries, left, sem.at[1])]
    for g in range(blocks):
        place = pl.ds(g * block, block)
        fetches.append(pltpu.make_async_copy(embeddings.at[place, :], right.at[place, :], sem.at[2 + g]))
    for fetch in fetches:
        fetch.start()
    fetches[0].wait()
    first, _ = named_by_partner(table, blocks, OFF)
    fetches[1].wait()
    place = pl.ds(pl.multiple_of(first * block, block), block)
    pltpu.make_async_copy(embeddings.at[place, :], right.at[place, :], sem.at[2 + first]).wait()
    out[...] = (dot(left[...], right[place, :], NT) * scale).astype(BF16)
    for g in range(blocks):

        @pl.when(g != first)
        def _():
            fetches[2 + g].wait()


def spans_of(pieces, rows):
    spans = []
    begin = 0
    for piece in pieces:
        end = begin + piece.shape[0]
        for slot in range(2):
            low, high = max(begin, slot * rows), min(end, (slot + 1) * rows)
            if low < high:
                inside = slice(low - slot * rows, high - slot * rows)
                spans.append((piece, slice(low - begin, high - begin), slot, inside))
        begin = end
    return spans


def write_pieces(pieces, value):
    rows = sum(piece.shape[0] for piece in pieces) // 2
    for piece, place, slot, inside in spans_of(pieces, rows):
        piece[place, :] = value(slot, inside).astype(BF16)


def gather_pieces(pieces, whole):
    for piece, place, slot, inside in spans_of(pieces, whole.shape[1]):
        whole[slot, inside] = piece[place, :]


def own_kernel(lists, queries, embeddings, own, off, *on, scale):
    blocks, _, block = own.shape
    for g in range(blocks):
        own[g] = dot(queries[...], embeddings[g * block : (g + 1) * block, :], NT) * scale
    _, second = named_by_partner(lists, blocks, OFF)
    off[...] = own[second].astype(BF16)
    first, second = named_by_partner(lists, blocks, ON)
    write_pieces(on, lambda slot, rows: own[(first, second)[slot], rows])


def hits_kernel(positives, tiles, out, kept, sem):
    fetch = pltpu.make_async_copy(tiles, kept, sem)
    fetch.start()
    blocks, rows, block = out.shape
    first = lax.axis_index(AXIS) * blocks * block
    ids = lax.broadcasted_iota(jnp.int32, (rows, block), 1)
    columns = jnp.transpose(positives[...]) - first
    for g in range(blocks):
        hits = jnp.zeros((rows, block), jnp.bool_)
        for column in range(positives.shape[0]):
            hits = jnp.logical_or(hits, ids + g * block == columns[:, column : column + 1])
        out[g] = jnp.where(hits, 1.0, 0.0).astype(BF16)
    fetch.wait()


def base_kernel(lists, own, tiles, *rest):
    *pieces, out, received = rest
    gather_pieces(pieces, received)
    blocks = out.shape[0]
    side = tile_side(ON)
    for g, slot in enumerate(slots_of(lists, blocks, ON)):
        out[g] = own[g] + dot(received[slot], tiles[g, side], NT)


def signal_kernel(lists, base, hits, propensity, received, tiles, *rest, slot):
    signal, push, total = rest[-3:]
    blocks, _, block = base.shape
    side = tile_side(OFF)
    total[...] = jnp.zeros_like(total)
    for g, taken in enumerate(slots_of(lists, blocks, OFF)):

        @pl.when(taken == slot)
        def _():
            scores = base[g] + dot(received[...], tiles[g, side], NT)
            inverse = 1.0 / propensity[:, g * block : (g + 1) * block]
            value = (jax.nn.sigmoid(scores) - hits[g].astype(F32) * inverse).astype(BF16)
            signal[g] = value
            total[...] += dot(value, tiles[g, side], NN)

    push[...] = total[...].astype(BF16)


def push_kernel(lists, signal, tiles, *rest):
    *pieces, total = rest
    blocks = signal.shape[0]
    side = tile_side(ON)
    total[...] = jnp.zeros_like(total)
    for g, slot in enumerate(slots_of(lists, blocks, ON)):
        total[slot] += dot(signal[g], tiles[g, side], NN)
    write_pieces(pieces, lambda slot, rows: total[slot, rows])


def query_kernel(signal, embeddings, out):
    blocks, _, block = signal.shape
    total = dot(signal[0], embeddings[0:block, :], NN)
    for g in range(1, blocks):
        total += dot(signal[g], embeddings[g * block : (g + 1) * block, :], NN)
    out[...] = total


def query_half_kernel(lists, part, received, embeddings, out, *, blocks):
    first, _ = named_by_partner(lists, blocks, OFF)
    out[...] = part[...] + dot(received[...], block_rows(embeddings, first, received.shape[1]), NN)


def query_on_kernel(lists, part, embeddings, *rest, blocks):
    *pieces, out, received = rest
    gather_pieces(pieces, received)
    block = received.shape[2]
    first, second = named_by_partner(lists, blocks, ON)
    out[...] = (
        part[...]
        + dot(received[0], block_rows(embeddings, first, block), NN)
        + dot(received[1], block_rows(embeddings, second, block), NN)
    )


def query_end_kernel(lists, part, received, embeddings, out, *, blocks):
    _, second = named_by_partner(lists, blocks, OFF)
    right = block_rows(embeddings, second, received.shape[1])
    out[...] = (part[...] + dot(received[...], right, NN)).astype(out.dtype)


def embed_kernel(lists, signal, on, off_a, off_b, queries, *rest, blocks, g, scale):
    if g == 0:
        ready, token, total = rest
    else:
        before = rest[0]
        out, ready, token, total, sem = rest[-5:]
    rows, block = total.shape
    writes = []

    def write(source, index, slot):
        writes.append(pltpu.make_async_copy(source, out.at[pl.ds(index * block, block), :], sem.at[slot]))
        writes[-1].start()

    if g > 0:
        write(before, g - 1, 0)
    token[...] = jnp.zeros_like(token)
    total[...] = signal[g].astype(F32)
    named = named_by_partner(lists, blocks, ON) + named_by_partner(lists, blocks, OFF)
    for received, index in zip((on.at[0], on.at[1], off_a, off_b), named):

        @pl.when(index == g)
        def _():
            total[...] += received[...].astype(F32)

    ready[...] = (dot(total[...].astype(BF16), queries[...], TN) * scale).astype(BF16)
    if g == blocks - 1:
        write(ready, g, 1)
    for copy in writes:
        copy.wait()


VMEM = pl.BlockSpec(memory_space=pltpu.VMEM)
SMEM = pl.BlockSpec(memory_space=pltpu.SMEM)
ANY = pl.BlockSpec(memory_space=pl.ANY)
HBM = pl.BlockSpec(memory_space=pltpu.HBM)


def call(kernel, name, in_specs, out_shape, out_specs=None, scratch=(), aliases=None, vmem=12, flops=0):
    if out_specs is None:
        out_specs = jax.tree.map(lambda _: VMEM, out_shape)
    return pl.pallas_call(
        kernel,
        in_specs=in_specs,
        out_specs=out_specs,
        out_shape=out_shape,
        scratch_shapes=scratch,
        input_output_aliases=aliases or {},
        name=name,
        cost_estimate=pl.CostEstimate(flops=flops, bytes_accessed=0, transcendentals=0),
        compiler_params=pltpu.CompilerParams(vmem_limit_bytes=vmem * MIB),
    )


def exchange(value, mask):
    count = lax.axis_size(AXIS)
    return lax.ppermute(value, AXIS, [(i, i ^ mask) for i in range(count)])


def in_vmem(shape, dtype):
    return pltpu.VMEM(shape, dtype)


def digit_of(bit):
    return (lax.axis_index(AXIS) // bit) % 2


def halve_kernel(held, got, *outs, bits):
    total = outs[-1]
    total[...] = held[...] + got[...].astype(F32)
    rows = outs[0].shape[0]
    for chain, bit in enumerate(bits):
        kept, sent = outs[2 * chain], outs[2 * chain + 1]
        begin = 2 * chain * rows
        digit = digit_of(bit)
        kept[...] = total[pl.ds(pl.multiple_of(begin + digit * rows, rows), rows), :]
        sent[...] = total[pl.ds(pl.multiple_of(begin + (1 - digit) * rows, rows), rows), :].astype(BF16)


def add_kernel(held, got, *rest, scale):
    rest[-1][...] = ((held[...].astype(F32) + got[...].astype(F32)) * scale).astype(BF16)


def join_kernel(held, got, *rest, bit):
    out = rest[-1]
    rows = held.shape[0]
    digit = digit_of(bit)
    out[pl.ds(pl.multiple_of(digit * rows, rows), rows), :] = held[...]
    out[pl.ds(pl.multiple_of((1 - digit) * rows, rows), rows), :] = got[...]


def place_kernel(held, got, *rest, chain):
    out, wide, sem = rest[-3:]
    rows = held.shape[0]
    wide[...] = jnp.where(lax.axis_index(AXIS) % 2 == 1, held[...], got[...]).astype(F32)
    copy = pltpu.make_async_copy(wide, out.at[pl.ds(chain * rows, rows), :], sem)
    copy.start()
    copy.wait()


def sum_queries(kept, sent, beside, scale):
    count = lax.axis_size(AXIS)
    rows, width = kept.shape
    if count & (count - 1) or count < 8:
        return lax.psum(kept, AXIS) * scale
    got = lax.ppermute(sent, AXIS, [(i, i + 1) for i in range(0, count, 2)])

    def chip_exchange(value, bit):
        return lax.ppermute(value, AXIS, [(i, i ^ bit) for i in range(1, count, 2)])

    bits = [1 << k for k in range(1, count.bit_length() - 1)]
    orders = [[bits[0], *bits[2:], bits[1]], [bits[1], bits[0], *bits[2:]]]
    ends = [order[0] for order in orders]
    wide, narrow = in_vmem((rows // 4, width), F32), in_vmem((rows // 4, width), BF16)
    kept_a, sent_a, kept_b, sent_b = call(
        functools.partial(halve_kernel, bits=ends),
        "halve",
        [VMEM] * 2,
        [wide, narrow, wide, narrow],
        scratch=[pltpu.VMEM((rows, width), F32)],
    )(kept, got)
    held, sent = [kept_a, kept_b], [sent_a, sent_b]
    for k in range(len(bits)):
        got = [chip_exchange(piece, order[k]) for piece, order in zip(sent, orders)]
        for chain in range(2):
            after = beside[k : k + 1] if chain == 0 else []
            held[chain] = call(
                functools.partial(add_kernel, scale=scale if k == len(bits) - 1 else 1.0),
                "add",
                [VMEM] * 2 + [ANY] * len(after),
                narrow,
            )(held[chain], got[chain], *after)
        sent = list(held)
    got = [chip_exchange(piece, bit) for piece, bit in zip(held, ends)]
    joined, handed = [], []
    for chain, bit in enumerate(ends):
        after = beside[len(bits) :] if chain == 0 else joined
        joined.append(
            call(
                functools.partial(join_kernel, bit=bit),
                "join",
                [VMEM] * 2 + [ANY] * len(after),
                in_vmem((rows // 2, width), BF16),
                flops=2 * 10**8,
            )(held[chain], got[chain], *after)
        )
        handed.append(lax.ppermute(joined[chain], AXIS, [(i + 1, i) for i in range(0, count, 2)]))
    begun = []
    for chain in range(2):
        begun = [
            call(
                functools.partial(place_kernel, chain=chain),
                "place",
                [VMEM] * 2 + [ANY] * chain,
                jax.ShapeDtypeStruct((rows, width), F32),
                out_specs=ANY,
                scratch=[pltpu.VMEM((rows // 2, width), F32), pltpu.SemaphoreType.DMA],
                aliases={2: 0} if chain else None,
            )(joined[chain], handed[chain], *begun)
        ]
    return begun[0]


def per_device(embeddings, edge_tiles, neighbour, propensity, queries, positives):
    count = lax.axis_size(AXIS)
    blocks, _, block, _ = edge_tiles.shape
    labels_dev, width = embeddings.shape
    rows = queries.shape[0]
    lists = neighbour.T
    odd = range(1, count, 2)
    off_route = [(i, (i + 1) % count) for i in odd] + [((i + 1) % count, i) for i in odd]

    def off_swap(value):
        return lax.ppermute(value, AXIS, off_route)

    def on_swap(value):
        return exchange(value, 1)

    one = in_vmem((rows, block), BF16)
    pair = in_vmem((2, rows, block), BF16)
    third = -(-2 * rows // 48) * 16
    thirds = [in_vmem((size, block), BF16) for size in (third, third, 2 * rows - 2 * third)]
    full = (blocks, rows, block)
    scale = 1.0 / math.sqrt(width)

    off_a, queries, embeddings = call(
        functools.partial(project_kernel, scale=scale),
        "project",
        [HBM] * 3,
        [one, in_vmem(queries.shape, BF16), in_vmem(embeddings.shape, BF16)],
        scratch=[pltpu.SMEM(lists.shape, jnp.int32), pltpu.SemaphoreType.DMA((2 + blocks,))],
    )(*(pltpu.with_memory_space_constraint(x, pltpu.HBM) for x in (lists, queries, embeddings)))
    from_off_a = off_swap(off_a)
    own, off_b, *for_on = call(
        functools.partial(own_kernel, scale=scale),
        "own",
        [SMEM, VMEM, VMEM],
        [in_vmem(full, F32), one] + thirds,
    )(lists, queries, embeddings)
    from_on = [on_swap(piece) for piece in for_on]
    hits, tiles = call(
        hits_kernel,
        "hits",
        [VMEM, HBM],
        [in_vmem(full, BF16), in_vmem(edge_tiles.shape, BF16)],
        scratch=[pltpu.SemaphoreType.DMA],
    )(positives.T, pltpu.with_memory_space_constraint(edge_tiles, pltpu.HBM))
    from_off_b = off_swap(off_b)
    base = call(
        base_kernel,
        "base",
        [SMEM] + [VMEM] * 5,
        in_vmem(full, F32),
        scratch=[pltpu.VMEM((2, rows, block), BF16)],
    )(lists, own, tiles, *from_on)
    propensity = propensity.reshape(1, labels_dev)

    def signal_of(received, slot, *begun):
        return call(
            functools.partial(signal_kernel, slot=slot),
            "signal",
            [SMEM] + [VMEM] * (5 + len(begun)),
            [in_vmem(full, BF16), one],
            scratch=[pltpu.VMEM((rows, block), F32)],
            aliases={6: 0} if begun else None,
            flops=0 if begun else 2 * 10**9,
        )(lists, base, hits, propensity, received, tiles, *begun)

    signal, push_a = signal_of(from_off_a, 0)
    back_a = off_swap(push_a)
    signal, push_b = signal_of(from_off_b, 1, signal)
    back_b = off_swap(push_b)
    push_on = call(
        push_kernel,
        "push",
        [SMEM, VMEM, VMEM],
        thirds,
        scratch=[pltpu.VMEM((2, rows, block), F32)],
    )(lists, signal, tiles)
    back_on = [on_swap(piece) for piece in push_on]

    whole = in_vmem((rows, width), F32)
    part = call(query_kernel, "query", [VMEM] * 2, whole)(signal, embeddings)
    part = call(
        functools.partial(query_half_kernel, blocks=blocks),
        "query_half",
        [SMEM] + [VMEM] * 3,
        whole,
        flops=10**9,
    )(lists, part, back_a, embeddings)
    part, on = call(
        functools.partial(query_on_kernel, blocks=blocks), "query_on", [SMEM] + [VMEM] * 5, [whole, pair]
    )(lists, part, embeddings, *back_on)
    def query_end(kind):
        return call(
            functools.partial(query_end_kernel, blocks=blocks),
            "query_end",
            [SMEM] + [VMEM] * 3,
            in_vmem((rows, width), kind),
        )(lists, part, back_b, embeddings)

    sent, kept = query_end(BF16), query_end(F32)
    ready = in_vmem((block, width), BF16)
    written = jax.ShapeDtypeStruct((labels_dev, width), BF16)
    outs, tokens = [], []
    for g in range(blocks):
        *outs, token = call(
            functools.partial(embed_kernel, blocks=blocks, g=g, scale=1.0 / math.sqrt(rows)),
            "embed",
            [SMEM] + [VMEM] * (5 + min(g, 1)) + [ANY] * (len(outs) - 1),
            ([written] if g else []) + [ready, in_vmem((8, 128), F32)],
            out_specs=([ANY] if g else []) + [VMEM] * 2,
            scratch=[pltpu.VMEM((rows, block), F32)] + ([pltpu.SemaphoreType.DMA((2,))] if g else []),
            aliases={7: 0} if g > 1 else None,
        )(lists, signal, on, back_a, back_b, queries, *outs[::-1])
        tokens.append(token)
    grad_embed = outs[0]
    grad_queries = sum_queries(kept, sent, tokens, 1.0 / math.sqrt(labels_dev * count))
    return (grad_embed, grad_queries)


def solution(mesh):
    placed = (
        P("labels", None),
        P("labels", None, None, None),
        P(),
        P("labels"),
        P("groups", None),
        P("groups", None),
    )
    return jax.shard_map(
        per_device,
        mesh=mesh,
        in_specs=placed,
        out_specs=(P(("groups", "labels"), None), P("groups", None)),
        check_vma=False,
    )
```

```python
import functools
import math

import jax
import jax.numpy as jnp
from jax import lax
from jax.experimental import pallas as pl
from jax.experimental.pallas import tpu as pltpu
from jax.sharding import PartitionSpec as P

AXIS = "labels"
BF16 = jnp.bfloat16
F32 = jnp.float32
NT = (((1,), (1,)), ((), ()))
NN = (((1,), (0,)), ((), ()))
TN = (((0,), (0,)), ((), ()))
MIB = 1024 * 1024

OFF, ON = True, False


def dot(a, b, dims):
    return lax.dot_general(a, b, dims, preferred_element_type=F32)


def own_side(device, off):
    odd = device % 2
    return 1 - odd if off else odd


def partner_of(device, count, off):
    ahead = jnp.where(device == count - 1, 0, device + 1)
    behind = jnp.where(device == 0, count - 1, device - 1)
    return jnp.where(own_side(device, off) == 0, ahead, behind)


def own_list(lists, blocks, off):
    device = lax.axis_index(AXIS)
    side = own_side(device, off)
    return [lists[side, device * blocks + g] for g in range(blocks)]


def slots_of(lists, blocks, off):
    named = own_list(lists, blocks, off)
    least = functools.reduce(jnp.minimum, named)
    return [(value != least).astype(jnp.int32) for value in named]


def named_by_partner(lists, blocks, off):
    device = lax.axis_index(AXIS)
    partner = partner_of(device, lax.axis_size(AXIS), off)
    side = 1 - own_side(device, off)
    named = [lists[side, partner * blocks + g] for g in range(blocks)]
    return functools.reduce(jnp.minimum, named), functools.reduce(jnp.maximum, named)


def tile_side(off):
    return own_side(lax.axis_index(AXIS), off)


def block_rows(ref, index, block):
    return ref[pl.ds(pl.multiple_of(index * block, block), block), :]


def project_kernel(lists, queries, embeddings, out, left, right, table, sem, *, scale):
    rows, block = out.shape
    blocks = right.shape[0] // block
    fetches = [pltpu.make_async_copy(lists, table, sem.at[0]), pltpu.make_async_copy(queries, left, sem.at[1])]
    for g in range(blocks):
        place = pl.ds(g * block, block)
        fetches.append(pltpu.make_async_copy(embeddings.at[place, :], right.at[place, :], sem.at[2 + g]))
    for fetch in fetches:
        fetch.start()
    fetches[0].wait()
    first, _ = named_by_partner(table, blocks, OFF)
    fetches[1].wait()
    place = pl.ds(pl.multiple_of(first * block, block), block)
    pltpu.make_async_copy(embeddings.at[place, :], right.at[place, :], sem.at[2 + first]).wait()
    out[...] = (dot(left[...], right[place, :], NT) * scale).astype(BF16)
    for g in range(blocks):

        @pl.when(g != first)
        def _():
            fetches[2 + g].wait()


def spans_of(pieces, rows):
    spans = []
    begin = 0
    for piece in pieces:
        end = begin + piece.shape[0]
        for slot in range(2):
            low, high = max(begin, slot * rows), min(end, (slot + 1) * rows)
            if low < high:
                inside = slice(low - slot * rows, high - slot * rows)
                spans.append((piece, slice(low - begin, high - begin), slot, inside))
        begin = end
    return spans


def write_pieces(pieces, value):
    rows = sum(piece.shape[0] for piece in pieces) // 2
    for piece, place, slot, inside in spans_of(pieces, rows):
        piece[place, :] = value(slot, inside).astype(BF16)


def gather_pieces(pieces, whole):
    for piece, place, slot, inside in spans_of(pieces, whole.shape[1]):
        whole[slot, inside] = piece[place, :]


def own_kernel(lists, queries, embeddings, own, off, *on, scale):
    blocks, _, block = own.shape
    for g in range(blocks):
        own[g] = dot(queries[...], embeddings[g * block : (g + 1) * block, :], NT) * scale
    _, second = named_by_partner(lists, blocks, OFF)
    off[...] = own[second].astype(BF16)
    first, second = named_by_partner(lists, blocks, ON)
    write_pieces(on, lambda slot, rows: own[(first, second)[slot], rows])


def hits_kernel(positives, tiles, out, kept, sem):
    fetch = pltpu.make_async_copy(tiles, kept, sem)
    fetch.start()
    blocks, rows, block = out.shape
    first = lax.axis_index(AXIS) * blocks * block
    ids = lax.broadcasted_iota(jnp.int32, (rows, block), 1)
    columns = jnp.transpose(positives[...]) - first
    for g in range(blocks):
        hits = jnp.zeros((rows, block), jnp.bool_)
        for column in range(positives.shape[0]):
            hits = jnp.logical_or(hits, ids + g * block == columns[:, column : column + 1])
        out[g] = jnp.where(hits, 1.0, 0.0).astype(BF16)
    fetch.wait()


def base_kernel(lists, own, tiles, *rest):
    *pieces, out, received = rest
    gather_pieces(pieces, received)
    blocks = out.shape[0]
    side = tile_side(ON)
    for g, slot in enumerate(slots_of(lists, blocks, ON)):
        out[g] = own[g] + dot(received[slot], tiles[g, side], NT)


def signal_kernel(lists, base, hits, propensity, received, tiles, *rest, slot):
    signal, push, total = rest[-3:]
    blocks, _, block = base.shape
    side = tile_side(OFF)
    total[...] = jnp.zeros_like(total)
    for g, taken in enumerate(slots_of(lists, blocks, OFF)):

        @pl.when(taken == slot)
        def _():
            scores = base[g] + dot(received[...], tiles[g, side], NT)
            inverse = 1.0 / propensity[:, g * block : (g + 1) * block]
            value = (jax.nn.sigmoid(scores) - hits[g].astype(F32) * inverse).astype(BF16)
            signal[g] = value
            total[...] += dot(value, tiles[g, side], NN)

    push[...] = total[...].astype(BF16)


def push_kernel(lists, signal, tiles, *rest):
    *pieces, total = rest
    blocks = signal.shape[0]
    side = tile_side(ON)
    total[...] = jnp.zeros_like(total)
    for g, slot in enumerate(slots_of(lists, blocks, ON)):
        total[slot] += dot(signal[g], tiles[g, side], NN)
    write_pieces(pieces, lambda slot, rows: total[slot, rows])


def query_kernel(signal, embeddings, out):
    blocks, _, block = signal.shape
    total = dot(signal[0], embeddings[0:block, :], NN)
    for g in range(1, blocks):
        total += dot(signal[g], embeddings[g * block : (g + 1) * block, :], NN)
    out[...] = total


def query_half_kernel(lists, part, received, embeddings, out, *, blocks):
    first, _ = named_by_partner(lists, blocks, OFF)
    out[...] = part[...] + dot(received[...], block_rows(embeddings, first, received.shape[1]), NN)


def query_on_kernel(lists, part, embeddings, *rest, blocks):
    *pieces, out, received = rest
    gather_pieces(pieces, received)
    block = received.shape[2]
    first, second = named_by_partner(lists, blocks, ON)
    out[...] = (
        part[...]
        + dot(received[0], block_rows(embeddings, first, block), NN)
        + dot(received[1], block_rows(embeddings, second, block), NN)
    )


def query_end_kernel(lists, part, received, embeddings, out, *, blocks):
    _, second = named_by_partner(lists, blocks, OFF)
    right = block_rows(embeddings, second, received.shape[1])
    out[...] = (part[...] + dot(received[...], right, NN)).astype(out.dtype)


def embed_kernel(lists, signal, on, off_a, off_b, queries, *rest, blocks, g, scale):
    if g == 0:
        ready, token, total = rest
    else:
        before = rest[0]
        out, ready, token, total, sem = rest[-5:]
    rows, block = total.shape
    writes = []

    def write(source, index, slot):
        writes.append(pltpu.make_async_copy(source, out.at[pl.ds(index * block, block), :], sem.at[slot]))
        writes[-1].start()

    if g > 0:
        write(before, g - 1, 0)
    token[...] = jnp.zeros_like(token)
    total[...] = signal[g].astype(F32)
    named = named_by_partner(lists, blocks, ON) + named_by_partner(lists, blocks, OFF)
    for received, index in zip((on.at[0], on.at[1], off_a, off_b), named):

        @pl.when(index == g)
        def _():
            total[...] += received[...].astype(F32)

    ready[...] = (dot(total[...].astype(BF16), queries[...], TN) * scale).astype(BF16)
    if g == blocks - 1:
        write(ready, g, 1)
    for copy in writes:
        copy.wait()


VMEM = pl.BlockSpec(memory_space=pltpu.VMEM)
SMEM = pl.BlockSpec(memory_space=pltpu.SMEM)
ANY = pl.BlockSpec(memory_space=pl.ANY)
HBM = pl.BlockSpec(memory_space=pltpu.HBM)


def call(kernel, name, in_specs, out_shape, out_specs=None, scratch=(), aliases=None, vmem=12, flops=0):
    if out_specs is None:
        out_specs = jax.tree.map(lambda _: VMEM, out_shape)
    return pl.pallas_call(
        kernel,
        in_specs=in_specs,
        out_specs=out_specs,
        out_shape=out_shape,
        scratch_shapes=scratch,
        input_output_aliases=aliases or {},
        name=name,
        cost_estimate=pl.CostEstimate(flops=flops, bytes_accessed=0, transcendentals=0),
        compiler_params=pltpu.CompilerParams(vmem_limit_bytes=vmem * MIB),
    )


def exchange(value, mask):
    count = lax.axis_size(AXIS)
    return lax.ppermute(value, AXIS, [(i, i ^ mask) for i in range(count)])


def in_vmem(shape, dtype):
    return pltpu.VMEM(shape, dtype)


def digit_of(bit):
    return (lax.axis_index(AXIS) // bit) % 2


def halve_kernel(held, got, *outs, bits):
    total = outs[-1]
    total[...] = held[...] + got[...].astype(F32)
    rows = outs[0].shape[0]
    for chain, bit in enumerate(bits):
        kept, sent = outs[2 * chain], outs[2 * chain + 1]
        begin = 2 * chain * rows
        digit = digit_of(bit)
        kept[...] = total[pl.ds(pl.multiple_of(begin + digit * rows, rows), rows), :]
        sent[...] = total[pl.ds(pl.multiple_of(begin + (1 - digit) * rows, rows), rows), :].astype(BF16)


def add_kernel(held, got, *rest, scale):
    rest[-1][...] = ((held[...].astype(F32) + got[...].astype(F32)) * scale).astype(BF16)


def join_kernel(held, got, *rest, bit):
    out = rest[-1]
    rows = held.shape[0]
    digit = digit_of(bit)
    out[pl.ds(pl.multiple_of(digit * rows, rows), rows), :] = held[...]
    out[pl.ds(pl.multiple_of((1 - digit) * rows, rows), rows), :] = got[...]


def place_kernel(held, got, *rest, chain):
    out, wide, sem = rest[-3:]
    rows = held.shape[0]
    wide[...] = jnp.where(lax.axis_index(AXIS) % 2 == 1, held[...], got[...]).astype(F32)
    copy = pltpu.make_async_copy(wide, out.at[pl.ds(chain * rows, rows), :], sem)
    copy.start()
    copy.wait()


def sum_queries(kept, sent, beside, scale):
    count = lax.axis_size(AXIS)
    rows, width = kept.shape
    if count & (count - 1) or count < 8:
        return lax.psum(kept, AXIS) * scale
    got = exchange(sent, 1)

    def chip_exchange(value, bit):
        return lax.ppermute(value, AXIS, [(i, i ^ bit if i % 2 else i) for i in range(count)])

    bits = [1 << k for k in range(1, count.bit_length() - 1)]
    orders = [[bits[0], *bits[2:], bits[1]], [bits[1], bits[0], *bits[2:]]]
    ends = [order[0] for order in orders]
    wide, narrow = in_vmem((rows // 4, width), F32), in_vmem((rows // 4, width), BF16)
    kept_a, sent_a, kept_b, sent_b = call(
        functools.partial(halve_kernel, bits=ends),
        "halve",
        [VMEM] * 2,
        [wide, narrow, wide, narrow],
        scratch=[pltpu.VMEM((rows, width), F32)],
    )(kept, got)
    held, sent = [kept_a, kept_b], [sent_a, sent_b]
    for k in range(len(bits)):
        got = [chip_exchange(piece, order[k]) for piece, order in zip(sent, orders)]
        for chain in range(2):
            after = beside[k : k + 1] if chain == 0 else []
            held[chain] = call(
                functools.partial(add_kernel, scale=scale if k == len(bits) - 1 else 1.0),
                "add",
                [VMEM] * 2 + [ANY] * len(after),
                narrow,
            )(held[chain], got[chain], *after)
        sent = list(held)
    got = [chip_exchange(piece, bit) for piece, bit in zip(held, ends)]
    joined, handed = [], []
    for chain, bit in enumerate(ends):
        after = beside[len(bits) :] if chain == 0 else joined
        joined.append(
            call(
                functools.partial(join_kernel, bit=bit),
                "join",
                [VMEM] * 2 + [ANY] * len(after),
                in_vmem((rows // 2, width), BF16),
                flops=2 * 10**8,
            )(held[chain], got[chain], *after)
        )
        handed.append(exchange(joined[chain], 1))
    begun = []
    for chain in range(2):
        begun = [
            call(
                functools.partial(place_kernel, chain=chain),
                "place",
                [VMEM] * 2 + [ANY] * chain,
                jax.ShapeDtypeStruct((rows, width), F32),
                out_specs=ANY,
                scratch=[pltpu.VMEM((rows // 2, width), F32), pltpu.SemaphoreType.DMA],
                aliases={2: 0} if chain else None,
            )(joined[chain], handed[chain], *begun)
        ]
    return begun[0]


def per_device(embeddings, edge_tiles, neighbour, propensity, queries, positives):
    count = lax.axis_size(AXIS)
    blocks, _, block, _ = edge_tiles.shape
    labels_dev, width = embeddings.shape
    rows = queries.shape[0]
    lists = neighbour.T
    odd = range(1, count, 2)
    off_route = [(i, (i + 1) % count) for i in odd] + [((i + 1) % count, i) for i in odd]

    def off_swap(value):
        return lax.ppermute(value, AXIS, off_route)

    def on_swap(value):
        return exchange(value, 1)

    one = in_vmem((rows, block), BF16)
    pair = in_vmem((2, rows, block), BF16)
    third = -(-2 * rows // 48) * 16
    thirds = [in_vmem((size, block), BF16) for size in (third, third, 2 * rows - 2 * third)]
    full = (blocks, rows, block)
    scale = 1.0 / math.sqrt(width)

    off_a, queries, embeddings = call(
        functools.partial(project_kernel, scale=scale),
        "project",
        [HBM] * 3,
        [one, in_vmem(queries.shape, BF16), in_vmem(embeddings.shape, BF16)],
        scratch=[pltpu.SMEM(lists.shape, jnp.int32), pltpu.SemaphoreType.DMA((2 + blocks,))],
    )(*(pltpu.with_memory_space_constraint(x, pltpu.HBM) for x in (lists, queries, embeddings)))
    from_off_a = off_swap(off_a)
    own, off_b, *for_on = call(
        functools.partial(own_kernel, scale=scale),
        "own",
        [SMEM, VMEM, VMEM],
        [in_vmem(full, F32), one] + thirds,
    )(lists, queries, embeddings)
    from_on = [on_swap(piece) for piece in for_on]
    hits, tiles = call(
        hits_kernel,
        "hits",
        [VMEM, HBM],
        [in_vmem(full, BF16), in_vmem(edge_tiles.shape, BF16)],
        scratch=[pltpu.SemaphoreType.DMA],
    )(positives.T, pltpu.with_memory_space_constraint(edge_tiles, pltpu.HBM))
    from_off_b = off_swap(off_b)
    base = call(
        base_kernel,
        "base",
        [SMEM] + [VMEM] * 5,
        in_vmem(full, F32),
        scratch=[pltpu.VMEM((2, rows, block), BF16)],
    )(lists, own, tiles, *from_on)
    propensity = propensity.reshape(1, labels_dev)

    def signal_of(received, slot, *begun):
        return call(
            functools.partial(signal_kernel, slot=slot),
            "signal",
            [SMEM] + [VMEM] * (5 + len(begun)),
            [in_vmem(full, BF16), one],
            scratch=[pltpu.VMEM((rows, block), F32)],
            aliases={6: 0} if begun else None,
            flops=0 if begun else 2 * 10**9,
        )(lists, base, hits, propensity, received, tiles, *begun)

    signal, push_a = signal_of(from_off_a, 0)
    back_a = off_swap(push_a)
    signal, push_b = signal_of(from_off_b, 1, signal)
    back_b = off_swap(push_b)
    push_on = call(
        push_kernel,
        "push",
        [SMEM, VMEM, VMEM],
        thirds,
        scratch=[pltpu.VMEM((2, rows, block), F32)],
    )(lists, signal, tiles)
    back_on = [on_swap(piece) for piece in push_on]

    whole = in_vmem((rows, width), F32)
    part = call(query_kernel, "query", [VMEM] * 2, whole)(signal, embeddings)
    part = call(
        functools.partial(query_half_kernel, blocks=blocks),
        "query_half",
        [SMEM] + [VMEM] * 3,
        whole,
        flops=10**9,
    )(lists, part, back_a, embeddings)
    part, on = call(
        functools.partial(query_on_kernel, blocks=blocks), "query_on", [SMEM] + [VMEM] * 5, [whole, pair]
    )(lists, part, embeddings, *back_on)
    def query_end(kind):
        return call(
            functools.partial(query_end_kernel, blocks=blocks),
            "query_end",
            [SMEM] + [VMEM] * 3,
            in_vmem((rows, width), kind),
        )(lists, part, back_b, embeddings)

    sent, kept = query_end(BF16), query_end(F32)
    ready = in_vmem((block, width), BF16)
    written = jax.ShapeDtypeStruct((labels_dev, width), BF16)
    outs, tokens = [], []
    for g in range(blocks):
        *outs, token = call(
            functools.partial(embed_kernel, blocks=blocks, g=g, scale=1.0 / math.sqrt(rows)),
            "embed",
            [SMEM] + [VMEM] * (5 + min(g, 1)) + [ANY] * (len(outs) - 1),
            ([written] if g else []) + [ready, in_vmem((8, 128), F32)],
            out_specs=([ANY] if g else []) + [VMEM] * 2,
            scratch=[pltpu.VMEM((rows, block), F32)] + ([pltpu.SemaphoreType.DMA((2,))] if g else []),
            aliases={7: 0} if g > 1 else None,
        )(lists, signal, on, back_a, back_b, queries, *outs[::-1])
        tokens.append(token)
    grad_embed = outs[0]
    grad_queries = sum_queries(kept, sent, tokens, 1.0 / math.sqrt(labels_dev * count))
    return (grad_embed, grad_queries)


def solution(mesh):
    placed = (
        P("labels", None),
        P("labels", None, None, None),
        P(),
        P("labels"),
        P("groups", None),
        P("groups", None),
    )
    return jax.shard_map(
        per_device,
        mesh=mesh,
        in_specs=placed,
        out_specs=(P(("groups", "labels"), None), P("groups", None)),
        check_vma=False,
    )
```

```python
import functools
import math

import jax
import jax.numpy as jnp
from jax import lax
from jax.experimental import pallas as pl
from jax.experimental.pallas import tpu as pltpu
from jax.sharding import PartitionSpec as P

AXIS = "labels"
BF16 = jnp.bfloat16
F32 = jnp.float32
NT = (((1,), (1,)), ((), ()))
NN = (((1,), (0,)), ((), ()))
TN = (((0,), (0,)), ((), ()))
MIB = 1024 * 1024

OFF, ON = True, False


def dot(a, b, dims):
    return lax.dot_general(a, b, dims, preferred_element_type=F32)


def own_side(device, off):
    odd = device % 2
    return 1 - odd if off else odd


def partner_of(device, count, off):
    ahead = jnp.where(device == count - 1, 0, device + 1)
    behind = jnp.where(device == 0, count - 1, device - 1)
    return jnp.where(own_side(device, off) == 0, ahead, behind)


def own_list(lists, blocks, off):
    device = lax.axis_index(AXIS)
    side = own_side(device, off)
    return [lists[side, device * blocks + g] for g in range(blocks)]


def slots_of(lists, blocks, off):
    named = own_list(lists, blocks, off)
    least = functools.reduce(jnp.minimum, named)
    return [(value != least).astype(jnp.int32) for value in named]


def named_by_partner(lists, blocks, off):
    device = lax.axis_index(AXIS)
    partner = partner_of(device, lax.axis_size(AXIS), off)
    side = 1 - own_side(device, off)
    named = [lists[side, partner * blocks + g] for g in range(blocks)]
    return functools.reduce(jnp.minimum, named), functools.reduce(jnp.maximum, named)


def tile_side(off):
    return own_side(lax.axis_index(AXIS), off)


def block_rows(ref, index, block):
    return ref[pl.ds(pl.multiple_of(index * block, block), block), :]


def project_kernel(lists, queries, embeddings, out, left, right, table, sem, *, scale):
    rows, block = out.shape
    blocks = right.shape[0] // block
    fetches = [pltpu.make_async_copy(lists, table, sem.at[0]), pltpu.make_async_copy(queries, left, sem.at[1])]
    for g in range(blocks):
        place = pl.ds(g * block, block)
        fetches.append(pltpu.make_async_copy(embeddings.at[place, :], right.at[place, :], sem.at[2 + g]))
    for fetch in fetches:
        fetch.start()
    fetches[0].wait()
    first, _ = named_by_partner(table, blocks, OFF)
    fetches[1].wait()
    place = pl.ds(pl.multiple_of(first * block, block), block)
    pltpu.make_async_copy(embeddings.at[place, :], right.at[place, :], sem.at[2 + first]).wait()
    out[...] = (dot(left[...], right[place, :], NT) * scale).astype(BF16)
    for g in range(blocks):

        @pl.when(g != first)
        def _():
            fetches[2 + g].wait()


def spans_of(pieces, rows):
    spans = []
    begin = 0
    for piece in pieces:
        end = begin + piece.shape[0]
        for slot in range(2):
            low, high = max(begin, slot * rows), min(end, (slot + 1) * rows)
            if low < high:
                inside = slice(low - slot * rows, high - slot * rows)
                spans.append((piece, slice(low - begin, high - begin), slot, inside))
        begin = end
    return spans


def write_pieces(pieces, value):
    rows = sum(piece.shape[0] for piece in pieces) // 2
    for piece, place, slot, inside in spans_of(pieces, rows):
        piece[place, :] = value(slot, inside).astype(BF16)


def gather_pieces(pieces, whole):
    for piece, place, slot, inside in spans_of(pieces, whole.shape[1]):
        whole[slot, inside] = piece[place, :]


def own_kernel(lists, queries, embeddings, own, off, *on, scale):
    blocks, _, block = own.shape
    for g in range(blocks):
        own[g] = dot(queries[...], embeddings[g * block : (g + 1) * block, :], NT) * scale
    _, second = named_by_partner(lists, blocks, OFF)
    off[...] = own[second].astype(BF16)
    first, second = named_by_partner(lists, blocks, ON)
    write_pieces(on, lambda slot, rows: own[(first, second)[slot], rows])


def hits_kernel(positives, tiles, out, kept, sem):
    fetch = pltpu.make_async_copy(tiles, kept, sem)
    fetch.start()
    blocks, rows, block = out.shape
    first = lax.axis_index(AXIS) * blocks * block
    ids = lax.broadcasted_iota(jnp.int32, (rows, block), 1)
    columns = jnp.transpose(positives[...]) - first
    for g in range(blocks):
        hits = jnp.zeros((rows, block), jnp.bool_)
        for column in range(positives.shape[0]):
            hits = jnp.logical_or(hits, ids + g * block == columns[:, column : column + 1])
        out[g] = jnp.where(hits, 1.0, 0.0).astype(BF16)
    fetch.wait()


def base_kernel(lists, own, tiles, *rest):
    *pieces, out, received = rest
    gather_pieces(pieces, received)
    blocks = out.shape[0]
    side = tile_side(ON)
    for g, slot in enumerate(slots_of(lists, blocks, ON)):
        out[g] = own[g] + dot(received[slot], tiles[g, side], NT)


def signal_kernel(lists, base, hits, propensity, received, tiles, *rest, slot):
    signal, push, total = rest[-3:]
    blocks, _, block = base.shape
    side = tile_side(OFF)
    total[...] = jnp.zeros_like(total)
    for g, taken in enumerate(slots_of(lists, blocks, OFF)):

        @pl.when(taken == slot)
        def _():
            scores = base[g] + dot(received[...], tiles[g, side], NT)
            inverse = 1.0 / propensity[:, g * block : (g + 1) * block]
            value = (jax.nn.sigmoid(scores) - hits[g].astype(F32) * inverse).astype(BF16)
            signal[g] = value
            total[...] += dot(value, tiles[g, side], NN)

    push[...] = total[...].astype(BF16)


def push_kernel(lists, signal, tiles, *rest):
    *pieces, total = rest
    blocks = signal.shape[0]
    side = tile_side(ON)
    total[...] = jnp.zeros_like(total)
    for g, slot in enumerate(slots_of(lists, blocks, ON)):
        total[slot] += dot(signal[g], tiles[g, side], NN)
    write_pieces(pieces, lambda slot, rows: total[slot, rows])


def query_kernel(signal, embeddings, out):
    blocks, _, block = signal.shape
    total = dot(signal[0], embeddings[0:block, :], NN)
    for g in range(1, blocks):
        total += dot(signal[g], embeddings[g * block : (g + 1) * block, :], NN)
    out[...] = total


def query_half_kernel(lists, part, received, embeddings, out, *, blocks):
    first, _ = named_by_partner(lists, blocks, OFF)
    out[...] = part[...] + dot(received[...], block_rows(embeddings, first, received.shape[1]), NN)


def query_on_kernel(lists, part, embeddings, *rest, blocks):
    *pieces, out, received = rest
    gather_pieces(pieces, received)
    block = received.shape[2]
    first, second = named_by_partner(lists, blocks, ON)
    out[...] = (
        part[...]
        + dot(received[0], block_rows(embeddings, first, block), NN)
        + dot(received[1], block_rows(embeddings, second, block), NN)
    )


def query_end_kernel(lists, part, received, embeddings, after, out, *, blocks, own):
    del after
    _, second = named_by_partner(lists, blocks, OFF)
    rows = out.shape[0]
    core = lax.axis_index(AXIS) % 2
    half = core if own else 1 - core
    place = pl.ds(pl.multiple_of(half * rows, rows), rows)
    right = block_rows(embeddings, second, received.shape[1])
    out[...] = (part[place, :] + dot(received[place, :], right, NN)).astype(out.dtype)


def embed_kernel(lists, signal, on, off_a, queries, *rest, blocks, turn, scale):
    last = turn == blocks - 1
    off = [off_a]
    if last:
        off.append(rest[0])
        rest = rest[1:]
    if turn == 0:
        ready, token, total = rest
    else:
        before = rest[0]
        out, ready, token, total, sem = rest[-5:]
    rows, block = total.shape
    writes = []

    def write(source, index, slot):
        place = out.at[pl.ds(pl.multiple_of(index * block, block), block), :]
        writes.append(pltpu.make_async_copy(source, place, sem.at[slot]))
        writes[-1].start()

    named = named_by_partner(lists, blocks, ON) + named_by_partner(lists, blocks, OFF)
    g = (named[3] + 1 + turn) % blocks
    if turn > 0:
        write(before, (named[3] + turn) % blocks, 0)
    token[...] = jnp.zeros_like(token)
    total[...] = signal[g].astype(F32)
    for received, index in zip([on.at[0], on.at[1], *off], named):

        @pl.when(index == g)
        def _():
            total[...] += received[...].astype(F32)

    ready[...] = (dot(total[...].astype(BF16), queries[...], TN) * scale).astype(BF16)
    if last:
        write(ready, g, 1)
    for copy in writes:
        copy.wait()


VMEM = pl.BlockSpec(memory_space=pltpu.VMEM)
SMEM = pl.BlockSpec(memory_space=pltpu.SMEM)
ANY = pl.BlockSpec(memory_space=pl.ANY)
HBM = pl.BlockSpec(memory_space=pltpu.HBM)


def call(kernel, name, in_specs, out_shape, out_specs=None, scratch=(), aliases=None, vmem=12, flops=0):
    if out_specs is None:
        out_specs = jax.tree.map(lambda _: VMEM, out_shape)
    return pl.pallas_call(
        kernel,
        in_specs=in_specs,
        out_specs=out_specs,
        out_shape=out_shape,
        scratch_shapes=scratch,
        input_output_aliases=aliases or {},
        name=name,
        cost_estimate=pl.CostEstimate(flops=flops, bytes_accessed=0, transcendentals=0),
        compiler_params=pltpu.CompilerParams(vmem_limit_bytes=vmem * MIB),
    )


def exchange(value, mask):
    count = lax.axis_size(AXIS)
    return lax.ppermute(value, AXIS, [(i, i ^ mask) for i in range(count)])


def in_vmem(shape, dtype):
    return pltpu.VMEM(shape, dtype)


def digit_of(bit):
    return (lax.axis_index(AXIS) // bit) % 2


def halve_kernel(held, got, *outs):
    total = held[...] + got[...].astype(F32)
    rows = outs[0].shape[0]
    for chain, out in enumerate(outs):
        out[...] = total[chain * rows : (chain + 1) * rows, :].astype(BF16)


def add_kernel(held, got, *rest, scale):
    rest[-1][...] = ((held[...].astype(F32) + got[...].astype(F32)) * scale).astype(BF16)


def place_kernel(*refs, places):
    out, wide, sem = refs[-3:]
    rows = refs[0].shape[0]
    core = lax.axis_index(AXIS) % 2
    copies = []
    for k, (chain, own) in enumerate(places):
        wide[k] = refs[k][...].astype(F32)
        half = core if own else 1 - core
        begin = pl.multiple_of((2 * half + chain) * rows, rows)
        copies.append(pltpu.make_async_copy(wide.at[k], out.at[pl.ds(begin, rows), :], sem.at[k]))
        copies[-1].start()
    for copy in copies:
        copy.wait()


def sum_queries(kept, sent, beside, scale):
    count = lax.axis_size(AXIS)
    rows, width = kept.shape
    got = exchange(sent, 1)
    if count & (count - 1) or count < 8:
        half = kept + got.astype(F32)
        half = lax.psum(half, AXIS, axis_index_groups=[list(range(c, count, 2)) for c in range(2)])
        both = jnp.stack([half, exchange(half, 1)])
        both = jnp.where(lax.axis_index(AXIS) % 2 == 0, both, both[::-1])
        return both.reshape(2 * rows, width) * scale
    bits = [1 << k for k in range(1, count.bit_length() - 1)]
    orders = [[bits[0], *bits[2:], bits[1]], [bits[1], bits[0], *bits[2:]]]
    piece = in_vmem((rows // 2, width), BF16)
    held = list(call(halve_kernel, "halve", [VMEM] * 2, [piece, piece])(kept, got))
    swapped = []
    for k in range(len(bits)):
        last = k == len(bits) - 1
        got = [exchange(value, order[k]) for value, order in zip(held, orders)]
        for chain in range(2):
            after = beside[k : k + 1] if chain == 0 else []
            held[chain] = call(
                functools.partial(add_kernel, scale=scale if last else 1.0),
                "add",
                [VMEM] * 2 + [ANY] * len(after),
                piece,
                flops=2 * 10**8 if last else 0,
            )(held[chain], got[chain], *after)
    swapped = [exchange(value, 1) for value in held]

    def place(values, places, *begun):
        return call(
            functools.partial(place_kernel, places=places),
            "place",
            [VMEM] * len(values) + [ANY] * len(begun),
            jax.ShapeDtypeStruct((2 * rows, width), F32),
            out_specs=ANY,
            scratch=[
                pltpu.VMEM((len(values), rows // 2, width), F32),
                pltpu.SemaphoreType.DMA((len(values),)),
            ],
            aliases={len(values): 0} if begun else None,
        )(*values, *begun)

    early = place([held[0], held[1], swapped[0]], [(0, True), (1, True), (0, False)])
    return place([swapped[1]], [(1, False)], early)


def per_device(embeddings, edge_tiles, neighbour, propensity, queries, positives):
    count = lax.axis_size(AXIS)
    blocks, _, block, _ = edge_tiles.shape
    labels_dev, width = embeddings.shape
    rows = queries.shape[0]
    lists = neighbour.T
    odd = range(1, count, 2)
    off_route = [(i, (i + 1) % count) for i in odd] + [((i + 1) % count, i) for i in odd]

    def off_swap(value):
        return lax.ppermute(value, AXIS, off_route)

    def on_swap(value):
        return exchange(value, 1)

    one = in_vmem((rows, block), BF16)
    pair = in_vmem((2, rows, block), BF16)
    third = -(-2 * rows // 48) * 16
    thirds = [in_vmem((size, block), BF16) for size in (third, third, 2 * rows - 2 * third)]
    full = (blocks, rows, block)
    scale = 1.0 / math.sqrt(width)

    off_a, queries, embeddings = call(
        functools.partial(project_kernel, scale=scale),
        "project",
        [HBM] * 3,
        [one, in_vmem(queries.shape, BF16), in_vmem(embeddings.shape, BF16)],
        scratch=[pltpu.SMEM(lists.shape, jnp.int32), pltpu.SemaphoreType.DMA((2 + blocks,))],
    )(*(pltpu.with_memory_space_constraint(x, pltpu.HBM) for x in (lists, queries, embeddings)))
    from_off_a = off_swap(off_a)
    own, off_b, *for_on = call(
        functools.partial(own_kernel, scale=scale),
        "own",
        [SMEM, VMEM, VMEM],
        [in_vmem(full, F32), one] + thirds,
    )(lists, queries, embeddings)
    from_on = [on_swap(piece) for piece in for_on]
    hits, tiles = call(
        hits_kernel,
        "hits",
        [VMEM, HBM],
        [in_vmem(full, BF16), in_vmem(edge_tiles.shape, BF16)],
        scratch=[pltpu.SemaphoreType.DMA],
    )(positives.T, pltpu.with_memory_space_constraint(edge_tiles, pltpu.HBM))
    from_off_b = off_swap(off_b)
    base = call(
        base_kernel,
        "base",
        [SMEM] + [VMEM] * 5,
        in_vmem(full, F32),
        scratch=[pltpu.VMEM((2, rows, block), BF16)],
    )(lists, own, tiles, *from_on)
    propensity = propensity.reshape(1, labels_dev)

    def signal_of(received, slot, *begun):
        return call(
            functools.partial(signal_kernel, slot=slot),
            "signal",
            [SMEM] + [VMEM] * (5 + len(begun)),
            [in_vmem(full, BF16), one],
            scratch=[pltpu.VMEM((rows, block), F32)],
            aliases={6: 0} if begun else None,
            flops=0 if begun else 2 * 10**9,
        )(lists, base, hits, propensity, received, tiles, *begun)

    signal, push_a = signal_of(from_off_a, 0)
    back_a = off_swap(push_a)
    signal, push_b = signal_of(from_off_b, 1, signal)
    back_b = off_swap(push_b)
    push_on = call(
        push_kernel,
        "push",
        [SMEM, VMEM, VMEM],
        thirds,
        scratch=[pltpu.VMEM((2, rows, block), F32)],
    )(lists, signal, tiles)
    back_on = [on_swap(piece) for piece in push_on]

    whole = in_vmem((rows, width), F32)
    part = call(query_kernel, "query", [VMEM] * 2, whole)(signal, embeddings)
    part = call(
        functools.partial(query_half_kernel, blocks=blocks),
        "query_half",
        [SMEM] + [VMEM] * 3,
        whole,
        flops=10**9,
    )(lists, part, back_a, embeddings)
    part, on = call(
        functools.partial(query_on_kernel, blocks=blocks), "query_on", [SMEM] + [VMEM] * 5, [whole, pair]
    )(lists, part, embeddings, *back_on)
    ready = in_vmem((block, width), BF16)
    written = jax.ShapeDtypeStruct((labels_dev, width), BF16)

    def embed(turn, outs):
        values = [lists, signal, on, back_a, queries] + ([back_b] if turn == blocks - 1 else []) + outs[::-1]
        return call(
            functools.partial(embed_kernel, blocks=blocks, turn=turn, scale=1.0 / math.sqrt(rows)),
            "embed",
            [SMEM] + [VMEM] * (len(values) - 1 - (turn > 1)) + [ANY] * (turn > 1),
            ([written] if turn else []) + [ready, in_vmem((8, 128), F32)],
            out_specs=([ANY] if turn else []) + [VMEM] * 2,
            scratch=[pltpu.VMEM((rows, block), F32)] + ([pltpu.SemaphoreType.DMA((2,))] if turn else []),
            aliases={len(values) - 1: 0} if turn > 1 else None,
        )(*values)

    *outs, token = embed(0, [])
    tokens = [token]

    def query_end(own, kind):
        return call(
            functools.partial(query_end_kernel, blocks=blocks, own=own),
            "query_end",
            [SMEM] + [VMEM] * 3 + [ANY],
            in_vmem((rows // 2, width), kind),
        )(lists, part, back_b, embeddings, tokens[0])

    sent, kept = query_end(False, BF16), query_end(True, F32)
    for turn in range(1, blocks):
        *outs, token = embed(turn, outs)
        tokens.append(token)
    grad_embed = outs[0]
    grad_queries = sum_queries(kept, sent, tokens[1:], 1.0 / math.sqrt(labels_dev * count))
    return (grad_embed, grad_queries)


def solution(mesh):
    placed = (
        P("labels", None),
        P("labels", None, None, None),
        P(),
        P("labels"),
        P("groups", None),
        P("groups", None),
    )
    return jax.shard_map(
        per_device,
        mesh=mesh,
        in_specs=placed,
        out_specs=(P(("groups", "labels"), None), P("groups", None)),
        check_vma=False,
    )
```

```python
import functools
import math

import jax
import jax.numpy as jnp
from jax import lax
from jax.experimental import pallas as pl
from jax.experimental.pallas import tpu as pltpu
from jax.sharding import PartitionSpec as P

AXIS = "labels"
BF16 = jnp.bfloat16
F32 = jnp.float32
NT = (((1,), (1,)), ((), ()))
NN = (((1,), (0,)), ((), ()))
TN = (((0,), (0,)), ((), ()))
MIB = 1024 * 1024

OFF, ON = True, False


def dot(a, b, dims):
    return lax.dot_general(a, b, dims, preferred_element_type=F32)


def own_side(device, off):
    odd = device % 2
    return 1 - odd if off else odd


def partner_of(device, count, off):
    ahead = jnp.where(device == count - 1, 0, device + 1)
    behind = jnp.where(device == 0, count - 1, device - 1)
    return jnp.where(own_side(device, off) == 0, ahead, behind)


def own_list(lists, blocks, off):
    device = lax.axis_index(AXIS)
    side = own_side(device, off)
    return [lists[side, device * blocks + g] for g in range(blocks)]


def slots_of(lists, blocks, off):
    named = own_list(lists, blocks, off)
    least = functools.reduce(jnp.minimum, named)
    return [(value != least).astype(jnp.int32) for value in named]


def named_by_partner(lists, blocks, off):
    device = lax.axis_index(AXIS)
    partner = partner_of(device, lax.axis_size(AXIS), off)
    side = 1 - own_side(device, off)
    named = [lists[side, partner * blocks + g] for g in range(blocks)]
    return functools.reduce(jnp.minimum, named), functools.reduce(jnp.maximum, named)


def tile_side(off):
    return own_side(lax.axis_index(AXIS), off)


def block_rows(ref, index, block):
    return ref[pl.ds(pl.multiple_of(index * block, block), block), :]


def project_kernel(lists, queries, embeddings, out, left, right, table, sem, *, scale):
    rows, block = out.shape
    blocks = right.shape[0] // block
    fetches = [pltpu.make_async_copy(lists, table, sem.at[0]), pltpu.make_async_copy(queries, left, sem.at[1])]
    for g in range(blocks):
        place = pl.ds(g * block, block)
        fetches.append(pltpu.make_async_copy(embeddings.at[place, :], right.at[place, :], sem.at[2 + g]))
    for fetch in fetches:
        fetch.start()
    fetches[0].wait()
    first, _ = named_by_partner(table, blocks, OFF)
    fetches[1].wait()
    place = pl.ds(pl.multiple_of(first * block, block), block)
    pltpu.make_async_copy(embeddings.at[place, :], right.at[place, :], sem.at[2 + first]).wait()
    out[...] = (dot(left[...], right[place, :], NT) * scale).astype(BF16)
    for g in range(blocks):

        @pl.when(g != first)
        def _():
            fetches[2 + g].wait()


def spans_of(pieces, rows):
    spans = []
    begin = 0
    for piece in pieces:
        end = begin + piece.shape[0]
        for slot in range(2):
            low, high = max(begin, slot * rows), min(end, (slot + 1) * rows)
            if low < high:
                inside = slice(low - slot * rows, high - slot * rows)
                spans.append((piece, slice(low - begin, high - begin), slot, inside))
        begin = end
    return spans


def write_pieces(pieces, value):
    rows = sum(piece.shape[0] for piece in pieces) // 2
    for piece, place, slot, inside in spans_of(pieces, rows):
        piece[place, :] = value(slot, inside).astype(BF16)


def gather_pieces(pieces, whole):
    for piece, place, slot, inside in spans_of(pieces, whole.shape[1]):
        whole[slot, inside] = piece[place, :]


def own_kernel(lists, queries, embeddings, own, off, *on, scale):
    blocks, _, block = own.shape
    for g in range(blocks):
        own[g] = dot(queries[...], embeddings[g * block : (g + 1) * block, :], NT) * scale
    _, second = named_by_partner(lists, blocks, OFF)
    off[...] = own[second].astype(BF16)
    first, second = named_by_partner(lists, blocks, ON)
    write_pieces(on, lambda slot, rows: own[(first, second)[slot], rows])


def hits_kernel(positives, tiles, out, kept, sem):
    fetch = pltpu.make_async_copy(tiles, kept, sem)
    fetch.start()
    blocks, rows, block = out.shape
    first = lax.axis_index(AXIS) * blocks * block
    ids = lax.broadcasted_iota(jnp.int32, (rows, block), 1)
    columns = jnp.transpose(positives[...]) - first
    for g in range(blocks):
        hits = jnp.zeros((rows, block), jnp.bool_)
        for column in range(positives.shape[0]):
            hits = jnp.logical_or(hits, ids + g * block == columns[:, column : column + 1])
        out[g] = jnp.where(hits, 1.0, 0.0).astype(BF16)
    fetch.wait()


def base_kernel(lists, own, tiles, *rest):
    *pieces, out, received = rest
    gather_pieces(pieces, received)
    blocks = out.shape[0]
    side = tile_side(ON)
    for g, slot in enumerate(slots_of(lists, blocks, ON)):
        out[g] = own[g] + dot(received[slot], tiles[g, side], NT)


def signal_kernel(lists, base, hits, propensity, received, tiles, *rest, slot):
    signal, push, total = rest[-3:]
    blocks, _, block = base.shape
    side = tile_side(OFF)
    total[...] = jnp.zeros_like(total)
    for g, taken in enumerate(slots_of(lists, blocks, OFF)):

        @pl.when(taken == slot)
        def _():
            scores = base[g] + dot(received[...], tiles[g, side], NT)
            inverse = 1.0 / propensity[:, g * block : (g + 1) * block]
            value = (jax.nn.sigmoid(scores) - hits[g].astype(F32) * inverse).astype(BF16)
            signal[g] = value
            total[...] += dot(value, tiles[g, side], NN)

    push[...] = total[...].astype(BF16)


def push_kernel(lists, signal, tiles, *rest):
    *pieces, total = rest
    blocks = signal.shape[0]
    side = tile_side(ON)
    total[...] = jnp.zeros_like(total)
    for g, slot in enumerate(slots_of(lists, blocks, ON)):
        total[slot] += dot(signal[g], tiles[g, side], NN)
    write_pieces(pieces, lambda slot, rows: total[slot, rows])


def query_kernel(signal, embeddings, out):
    blocks, _, block = signal.shape
    total = dot(signal[0], embeddings[0:block, :], NN)
    for g in range(1, blocks):
        total += dot(signal[g], embeddings[g * block : (g + 1) * block, :], NN)
    out[...] = total


def query_half_kernel(lists, part, received, embeddings, out, *, blocks):
    first, _ = named_by_partner(lists, blocks, OFF)
    out[...] = part[...] + dot(received[...], block_rows(embeddings, first, received.shape[1]), NN)


def query_on_kernel(lists, part, embeddings, *rest, blocks):
    *pieces, out, received = rest
    gather_pieces(pieces, received)
    block = received.shape[2]
    first, second = named_by_partner(lists, blocks, ON)
    out[...] = (
        part[...]
        + dot(received[0], block_rows(embeddings, first, block), NN)
        + dot(received[1], block_rows(embeddings, second, block), NN)
    )


def query_end_kernel(lists, part, received, embeddings, after, out, *, blocks, own):
    del after
    _, second = named_by_partner(lists, blocks, OFF)
    rows = out.shape[0]
    core = lax.axis_index(AXIS) % 2
    half = core if own else 1 - core
    place = pl.ds(pl.multiple_of(half * rows, rows), rows)
    right = block_rows(embeddings, second, received.shape[1])
    out[...] = (part[place, :] + dot(received[place, :], right, NN)).astype(out.dtype)


def embed_kernel(lists, signal, on, off_a, queries, *rest, blocks, turn, scale):
    last = turn == blocks - 1
    off = [off_a]
    if last:
        off.append(rest[0])
        rest = rest[1:]
    if turn == 0:
        ready, token, total = rest
    else:
        before = rest[0]
        out, ready, token, total, sem = rest[-5:]
    rows, block = total.shape
    writes = []

    def write(source, index, slot):
        place = out.at[pl.ds(pl.multiple_of(index * block, block), block), :]
        writes.append(pltpu.make_async_copy(source, place, sem.at[slot]))
        writes[-1].start()

    named = named_by_partner(lists, blocks, ON) + named_by_partner(lists, blocks, OFF)
    g = (named[3] + 1 + turn) % blocks
    if turn > 0:
        write(before, (named[3] + turn) % blocks, 0)
    token[...] = jnp.zeros_like(token)
    total[...] = signal[g].astype(F32)
    for received, index in zip([on.at[0], on.at[1], *off], named):

        @pl.when(index == g)
        def _():
            total[...] += received[...].astype(F32)

    ready[...] = (dot(total[...].astype(BF16), queries[...], TN) * scale).astype(BF16)
    if last:
        write(ready, g, 1)
    for copy in writes:
        copy.wait()


VMEM = pl.BlockSpec(memory_space=pltpu.VMEM)
SMEM = pl.BlockSpec(memory_space=pltpu.SMEM)
ANY = pl.BlockSpec(memory_space=pl.ANY)
HBM = pl.BlockSpec(memory_space=pltpu.HBM)


def call(kernel, name, in_specs, out_shape, out_specs=None, scratch=(), aliases=None, vmem=12, flops=0):
    if out_specs is None:
        out_specs = jax.tree.map(lambda _: VMEM, out_shape)
    return pl.pallas_call(
        kernel,
        in_specs=in_specs,
        out_specs=out_specs,
        out_shape=out_shape,
        scratch_shapes=scratch,
        input_output_aliases=aliases or {},
        name=name,
        cost_estimate=pl.CostEstimate(flops=flops, bytes_accessed=0, transcendentals=0),
        compiler_params=pltpu.CompilerParams(vmem_limit_bytes=vmem * MIB),
    )


def exchange(value, mask):
    count = lax.axis_size(AXIS)
    return lax.ppermute(value, AXIS, [(i, i ^ mask) for i in range(count)])


def in_vmem(shape, dtype):
    return pltpu.VMEM(shape, dtype)


def digit_of(bit):
    return (lax.axis_index(AXIS) // bit) % 2


def halve_kernel(held, got, *outs):
    total = held[...] + got[...].astype(F32)
    rows = outs[0].shape[0]
    for chain, out in enumerate(outs):
        out[...] = total[chain * rows : (chain + 1) * rows, :].astype(BF16)


def add_kernel(held, got, *rest, scale):
    rest[-1][...] = ((held[...].astype(F32) + got[...].astype(F32)) * scale).astype(BF16)


def place_kernel(*refs, places):
    out, wide, sem = refs[-3:]
    rows = refs[0].shape[0]
    core = lax.axis_index(AXIS) % 2
    copies = []
    for k, (chain, own) in enumerate(places):
        wide[k] = refs[k][...].astype(F32)
        half = core if own else 1 - core
        begin = pl.multiple_of((2 * half + chain) * rows, rows)
        copies.append(pltpu.make_async_copy(wide.at[k], out.at[pl.ds(begin, rows), :], sem.at[k]))
        copies[-1].start()
    for copy in copies:
        copy.wait()


def sum_queries(kept, sent, beside, scale):
    count = lax.axis_size(AXIS)
    rows, width = kept.shape
    got = exchange(sent, 1)
    if count & (count - 1) or count < 8:
        half = kept + got.astype(F32)
        half = lax.psum(half, AXIS, axis_index_groups=[list(range(c, count, 2)) for c in range(2)])
        both = jnp.stack([half, exchange(half, 1)])
        both = jnp.where(lax.axis_index(AXIS) % 2 == 0, both, both[::-1])
        return both.reshape(2 * rows, width) * scale
    bits = [1 << k for k in range(1, count.bit_length() - 1)]
    orders = [[bits[0], *bits[2:], bits[1]], [bits[1], bits[0], *bits[2:]]]
    piece = in_vmem((rows // 2, width), BF16)
    held = list(call(halve_kernel, "halve", [VMEM] * 2, [piece, piece])(kept, got))
    swapped = []
    for k in range(len(bits)):
        last = k == len(bits) - 1
        got = [exchange(value, order[k]) for value, order in zip(held, orders)]
        for chain in range(2):
            after = beside[k : k + 1] if chain == 0 else []
            held[chain] = call(
                functools.partial(add_kernel, scale=scale if last else 1.0),
                "add",
                [VMEM] * 2 + [ANY] * len(after),
                piece,
                flops=2 * 10**8 if last else 0,
            )(held[chain], got[chain], *after)
    swapped = [exchange(value, 1) for value in held]

    def place(values, places, *begun):
        return call(
            functools.partial(place_kernel, places=places),
            "place",
            [VMEM] * len(values) + [ANY] * len(begun),
            jax.ShapeDtypeStruct((2 * rows, width), F32),
            out_specs=ANY,
            scratch=[
                pltpu.VMEM((len(values), rows // 2, width), F32),
                pltpu.SemaphoreType.DMA((len(values),)),
            ],
            aliases={len(values): 0} if begun else None,
        )(*values, *begun)

    early = place([held[0], held[1], swapped[0]], [(0, True), (1, True), (0, False)])
    return place([swapped[1]], [(1, False)], early)


def per_device(embeddings, edge_tiles, neighbour, propensity, queries, positives):
    count = lax.axis_size(AXIS)
    blocks, _, block, _ = edge_tiles.shape
    labels_dev, width = embeddings.shape
    rows = queries.shape[0]
    lists = neighbour.T
    odd = range(1, count, 2)
    off_route = [(i, (i + 1) % count) for i in odd] + [((i + 1) % count, i) for i in odd]

    def off_swap(value):
        return lax.ppermute(value, AXIS, off_route)

    def on_swap(value):
        return exchange(value, 1)

    one = in_vmem((rows, block), BF16)
    pair = in_vmem((2, rows, block), BF16)
    third = -(-2 * rows // 48) * 16
    thirds = [in_vmem((size, block), BF16) for size in (third, third, 2 * rows - 2 * third)]
    full = (blocks, rows, block)
    scale = 1.0 / math.sqrt(width)

    off_a, queries, embeddings, lists = call(
        functools.partial(project_kernel, scale=scale),
        "project",
        [HBM] * 3,
        [
            one,
            in_vmem(queries.shape, BF16),
            in_vmem(embeddings.shape, BF16),
            pltpu.SMEM(lists.shape, jnp.int32),
        ],
        out_specs=[VMEM] * 3 + [SMEM],
        scratch=[pltpu.SemaphoreType.DMA((2 + blocks,))],
    )(*(pltpu.with_memory_space_constraint(x, pltpu.HBM) for x in (lists, queries, embeddings)))
    from_off_a = off_swap(off_a)
    own, off_b, *for_on = call(
        functools.partial(own_kernel, scale=scale),
        "own",
        [SMEM, VMEM, VMEM],
        [in_vmem(full, F32), one] + thirds,
    )(lists, queries, embeddings)
    from_on = [on_swap(piece) for piece in for_on]
    hits, tiles = call(
        hits_kernel,
        "hits",
        [VMEM, HBM],
        [in_vmem(full, BF16), in_vmem(edge_tiles.shape, BF16)],
        scratch=[pltpu.SemaphoreType.DMA],
    )(positives.T, pltpu.with_memory_space_constraint(edge_tiles, pltpu.HBM))
    from_off_b = off_swap(off_b)
    base = call(
        base_kernel,
        "base",
        [SMEM] + [VMEM] * 5,
        in_vmem(full, F32),
        scratch=[pltpu.VMEM((2, rows, block), BF16)],
    )(lists, own, tiles, *from_on)
    propensity = propensity.reshape(1, labels_dev)

    def signal_of(received, slot, *begun):
        return call(
            functools.partial(signal_kernel, slot=slot),
            "signal",
            [SMEM] + [VMEM] * (5 + len(begun)),
            [in_vmem(full, BF16), one],
            scratch=[pltpu.VMEM((rows, block), F32)],
            aliases={6: 0} if begun else None,
            flops=0 if begun else 2 * 10**9,
        )(lists, base, hits, propensity, received, tiles, *begun)

    signal, push_a = signal_of(from_off_a, 0)
    back_a = off_swap(push_a)
    signal, push_b = signal_of(from_off_b, 1, signal)
    back_b = off_swap(push_b)
    push_on = call(
        push_kernel,
        "push",
        [SMEM, VMEM, VMEM],
        thirds,
        scratch=[pltpu.VMEM((2, rows, block), F32)],
    )(lists, signal, tiles)
    back_on = [on_swap(piece) for piece in push_on]

    whole = in_vmem((rows, width), F32)
    part = call(query_kernel, "query", [VMEM] * 2, whole)(signal, embeddings)
    part = call(
        functools.partial(query_half_kernel, blocks=blocks),
        "query_half",
        [SMEM] + [VMEM] * 3,
        whole,
        flops=10**9,
    )(lists, part, back_a, embeddings)
    part, on = call(
        functools.partial(query_on_kernel, blocks=blocks), "query_on", [SMEM] + [VMEM] * 5, [whole, pair]
    )(lists, part, embeddings, *back_on)
    ready = in_vmem((block, width), BF16)
    written = jax.ShapeDtypeStruct((labels_dev, width), BF16)

    def embed(turn, outs):
        values = [lists, signal, on, back_a, queries] + ([back_b] if turn == blocks - 1 else []) + outs[::-1]
        return call(
            functools.partial(embed_kernel, blocks=blocks, turn=turn, scale=1.0 / math.sqrt(rows)),
            "embed",
            [SMEM] + [VMEM] * (len(values) - 1 - (turn > 1)) + [ANY] * (turn > 1),
            ([written] if turn else []) + [ready, in_vmem((8, 128), F32)],
            out_specs=([ANY] if turn else []) + [VMEM] * 2,
            scratch=[pltpu.VMEM((rows, block), F32)] + ([pltpu.SemaphoreType.DMA((2,))] if turn else []),
            aliases={len(values) - 1: 0} if turn > 1 else None,
        )(*values)

    *outs, token = embed(0, [])
    tokens = [token]

    def query_end(own, kind):
        return call(
            functools.partial(query_end_kernel, blocks=blocks, own=own),
            "query_end",
            [SMEM] + [VMEM] * 3 + [ANY],
            in_vmem((rows // 2, width), kind),
        )(lists, part, back_b, embeddings, tokens[0])

    sent, kept = query_end(False, BF16), query_end(True, F32)
    for turn in range(1, blocks):
        *outs, token = embed(turn, outs)
        tokens.append(token)
    grad_embed = outs[0]
    grad_queries = sum_queries(kept, sent, tokens[1:], 1.0 / math.sqrt(labels_dev * count))
    return (grad_embed, grad_queries)


def solution(mesh):
    placed = (
        P("labels", None),
        P("labels", None, None, None),
        P(),
        P("labels"),
        P("groups", None),
        P("groups", None),
    )
    return jax.shard_map(
        per_device,
        mesh=mesh,
        in_specs=placed,
        out_specs=(P(("groups", "labels"), None), P("groups", None)),
        check_vma=False,
    )
```

```python
import functools
import math

import jax
import jax.numpy as jnp
from jax import lax
from jax.experimental import pallas as pl
from jax.experimental.pallas import tpu as pltpu
from jax.sharding import PartitionSpec as P

AXIS = "labels"
BF16 = jnp.bfloat16
F32 = jnp.float32
NT = (((1,), (1,)), ((), ()))
NN = (((1,), (0,)), ((), ()))
TN = (((0,), (0,)), ((), ()))
MIB = 1024 * 1024

OFF, ON = True, False


def dot(a, b, dims):
    return lax.dot_general(a, b, dims, preferred_element_type=F32)


def own_side(device, off):
    odd = device % 2
    return 1 - odd if off else odd


def partner_of(device, count, off):
    ahead = jnp.where(device == count - 1, 0, device + 1)
    behind = jnp.where(device == 0, count - 1, device - 1)
    return jnp.where(own_side(device, off) == 0, ahead, behind)


def own_list(lists, blocks, off):
    device = lax.axis_index(AXIS)
    side = own_side(device, off)
    return [lists[side, device * blocks + g] for g in range(blocks)]


def slots_of(lists, blocks, off):
    named = own_list(lists, blocks, off)
    least = functools.reduce(jnp.minimum, named)
    return [(value != least).astype(jnp.int32) for value in named]


def named_by_partner(lists, blocks, off):
    device = lax.axis_index(AXIS)
    partner = partner_of(device, lax.axis_size(AXIS), off)
    side = 1 - own_side(device, off)
    named = [lists[side, partner * blocks + g] for g in range(blocks)]
    return functools.reduce(jnp.minimum, named), functools.reduce(jnp.maximum, named)


def tile_side(off):
    return own_side(lax.axis_index(AXIS), off)


def block_rows(ref, index, block):
    return ref[pl.ds(pl.multiple_of(index * block, block), block), :]


def project_kernel(lists, queries, embeddings, out, left, right, table, sem, *, scale):
    rows, block = out.shape
    blocks = right.shape[0] // block
    fetches = [pltpu.make_async_copy(lists, table, sem.at[0]), pltpu.make_async_copy(queries, left, sem.at[1])]
    for g in range(blocks):
        place = pl.ds(g * block, block)
        fetches.append(pltpu.make_async_copy(embeddings.at[place, :], right.at[place, :], sem.at[2 + g]))
    for fetch in fetches:
        fetch.start()
    fetches[0].wait()
    first, _ = named_by_partner(table, blocks, OFF)
    fetches[1].wait()
    place = pl.ds(pl.multiple_of(first * block, block), block)
    pltpu.make_async_copy(embeddings.at[place, :], right.at[place, :], sem.at[2 + first]).wait()
    out[...] = (dot(left[...], right[place, :], NT) * scale).astype(BF16)
    for g in range(blocks):

        @pl.when(g != first)
        def _():
            fetches[2 + g].wait()


def spans_of(pieces, rows):
    spans = []
    begin = 0
    for piece in pieces:
        end = begin + piece.shape[0]
        for slot in range(2):
            low, high = max(begin, slot * rows), min(end, (slot + 1) * rows)
            if low < high:
                inside = slice(low - slot * rows, high - slot * rows)
                spans.append((piece, slice(low - begin, high - begin), slot, inside))
        begin = end
    return spans


def write_pieces(pieces, value):
    rows = sum(piece.shape[0] for piece in pieces) // 2
    for piece, place, slot, inside in spans_of(pieces, rows):
        piece[place, :] = value(slot, inside).astype(BF16)


def gather_pieces(pieces, whole):
    for piece, place, slot, inside in spans_of(pieces, whole.shape[1]):
        whole[slot, inside] = piece[place, :]


def own_kernel(lists, queries, embeddings, own, off, *on, scale):
    blocks, _, block = own.shape
    for g in range(blocks):
        own[g] = dot(queries[...], embeddings[g * block : (g + 1) * block, :], NT) * scale
    _, second = named_by_partner(lists, blocks, OFF)
    off[...] = own[second].astype(BF16)
    first, second = named_by_partner(lists, blocks, ON)
    write_pieces(on, lambda slot, rows: own[(first, second)[slot], rows])


def hits_kernel(positives, tiles, out, kept, sem):
    fetch = pltpu.make_async_copy(tiles, kept, sem)
    fetch.start()
    blocks, rows, block = out.shape
    first = lax.axis_index(AXIS) * blocks * block
    ids = lax.broadcasted_iota(jnp.int32, (rows, block), 1)
    columns = jnp.transpose(positives[...]) - first
    for g in range(blocks):
        hits = jnp.zeros((rows, block), jnp.bool_)
        for column in range(positives.shape[0]):
            hits = jnp.logical_or(hits, ids + g * block == columns[:, column : column + 1])
        out[g] = jnp.where(hits, 1.0, 0.0).astype(BF16)
    fetch.wait()


def base_kernel(lists, own, tiles, *rest):
    *pieces, out, received = rest
    gather_pieces(pieces, received)
    blocks = out.shape[0]
    side = tile_side(ON)
    for g, slot in enumerate(slots_of(lists, blocks, ON)):
        out[g] = own[g] + dot(received[slot], tiles[g, side], NT)


def signal_kernel(lists, base, hits, propensity, received, tiles, *rest, slot):
    signal, push, total = rest[-3:]
    blocks, _, block = base.shape
    side = tile_side(OFF)
    total[...] = jnp.zeros_like(total)
    for g, taken in enumerate(slots_of(lists, blocks, OFF)):

        @pl.when(taken == slot)
        def _():
            scores = base[g] + dot(received[...], tiles[g, side], NT)
            inverse = 1.0 / propensity[:, g * block : (g + 1) * block]
            value = (jax.nn.sigmoid(scores) - hits[g].astype(F32) * inverse).astype(BF16)
            signal[g] = value
            total[...] += dot(value, tiles[g, side], NN)

    push[...] = total[...].astype(BF16)


def push_kernel(lists, signal, tiles, *rest):
    *pieces, total = rest
    blocks = signal.shape[0]
    side = tile_side(ON)
    total[...] = jnp.zeros_like(total)
    for g, slot in enumerate(slots_of(lists, blocks, ON)):
        total[slot] += dot(signal[g], tiles[g, side], NN)
    write_pieces(pieces, lambda slot, rows: total[slot, rows])


def query_kernel(signal, embeddings, out):
    blocks, _, block = signal.shape
    total = dot(signal[0], embeddings[0:block, :], NN)
    for g in range(1, blocks):
        total += dot(signal[g], embeddings[g * block : (g + 1) * block, :], NN)
    out[...] = total


def query_half_kernel(lists, part, received, embeddings, out, *, blocks):
    first, _ = named_by_partner(lists, blocks, OFF)
    out[...] = part[...] + dot(received[...], block_rows(embeddings, first, received.shape[1]), NN)


def query_on_kernel(lists, part, embeddings, *rest, blocks):
    *pieces, out, received = rest
    gather_pieces(pieces, received)
    block = received.shape[2]
    first, second = named_by_partner(lists, blocks, ON)
    out[...] = (
        part[...]
        + dot(received[0], block_rows(embeddings, first, block), NN)
        + dot(received[1], block_rows(embeddings, second, block), NN)
    )


def query_end_kernel(lists, part, received, embeddings, after, out, *, blocks, own):
    del after
    _, second = named_by_partner(lists, blocks, OFF)
    rows = out.shape[0]
    core = lax.axis_index(AXIS) % 2
    half = core if own else 1 - core
    place = pl.ds(pl.multiple_of(half * rows, rows), rows)
    right = block_rows(embeddings, second, received.shape[1])
    out[...] = (part[place, :] + dot(received[place, :], right, NN)).astype(out.dtype)


def embed_kernel(lists, signal, on, off_a, queries, *rest, blocks, turn, scale):
    last = turn == blocks - 1
    off = [off_a]
    if last:
        off.append(rest[0])
        rest = rest[1:]
    if turn == 0:
        ready, token, total = rest
    else:
        before = rest[0]
        out, ready, token, total, sem = rest[-5:]
    rows, block = total.shape
    writes = []

    def write(source, index, slot):
        place = out.at[pl.ds(pl.multiple_of(index * block, block), block), :]
        writes.append(pltpu.make_async_copy(source, place, sem.at[slot]))
        writes[-1].start()

    named = named_by_partner(lists, blocks, ON) + named_by_partner(lists, blocks, OFF)
    g = (named[3] + 1 + turn) % blocks
    if turn > 0:
        write(before, (named[3] + turn) % blocks, 0)
    token[...] = jnp.zeros_like(token)
    total[...] = signal[g].astype(F32)
    for received, index in zip([on.at[0], on.at[1], *off], named):

        @pl.when(index == g)
        def _():
            total[...] += received[...].astype(F32)

    ready[...] = (dot(total[...].astype(BF16), queries[...], TN) * scale).astype(BF16)
    if last:
        write(ready, g, 1)
    for copy in writes:
        copy.wait()


VMEM = pl.BlockSpec(memory_space=pltpu.VMEM)
SMEM = pl.BlockSpec(memory_space=pltpu.SMEM)
ANY = pl.BlockSpec(memory_space=pl.ANY)
HBM = pl.BlockSpec(memory_space=pltpu.HBM)


def call(kernel, name, in_specs, out_shape, out_specs=None, scratch=(), aliases=None, vmem=12, flops=0):
    if out_specs is None:
        out_specs = jax.tree.map(lambda _: VMEM, out_shape)
    return pl.pallas_call(
        kernel,
        in_specs=in_specs,
        out_specs=out_specs,
        out_shape=out_shape,
        scratch_shapes=scratch,
        input_output_aliases=aliases or {},
        name=name,
        cost_estimate=pl.CostEstimate(flops=flops, bytes_accessed=0, transcendentals=0),
        compiler_params=pltpu.CompilerParams(vmem_limit_bytes=vmem * MIB),
    )


def exchange(value, mask):
    count = lax.axis_size(AXIS)
    return lax.ppermute(value, AXIS, [(i, i ^ mask) for i in range(count)])


def in_vmem(shape, dtype):
    return pltpu.VMEM(shape, dtype)


def digit_of(bit):
    return (lax.axis_index(AXIS) // bit) % 2


def halve_kernel(held, got, *outs):
    total = held[...] + got[...].astype(F32)
    rows = outs[0].shape[0]
    for chain, out in enumerate(outs):
        out[...] = total[chain * rows : (chain + 1) * rows, :].astype(BF16)


def add_kernel(held, got, *rest, scale):
    rest[-1][...] = ((held[...].astype(F32) + got[...].astype(F32)) * scale).astype(BF16)


def place_kernel(*refs, places):
    out, wide, sem = refs[-3:]
    rows = refs[0].shape[0]
    core = lax.axis_index(AXIS) % 2
    copies = []
    for k, (chain, own) in enumerate(places):
        wide[k] = refs[k][...].astype(F32)
        half = core if own else 1 - core
        begin = pl.multiple_of((2 * half + chain) * rows, rows)
        copies.append(pltpu.make_async_copy(wide.at[k], out.at[pl.ds(begin, rows), :], sem.at[k]))
        copies[-1].start()
    for copy in copies:
        copy.wait()


def sum_queries(kept, sent, beside, scale):
    count = lax.axis_size(AXIS)
    rows, width = kept.shape
    got = exchange(sent, 1)
    if count & (count - 1) or count < 8:
        half = kept + got.astype(F32)
        half = lax.psum(half, AXIS, axis_index_groups=[list(range(c, count, 2)) for c in range(2)])
        both = jnp.stack([half, exchange(half, 1)])
        both = jnp.where(lax.axis_index(AXIS) % 2 == 0, both, both[::-1])
        return both.reshape(2 * rows, width) * scale
    bits = [1 << k for k in range(1, count.bit_length() - 1)]
    orders = [bits, bits[-1:] + bits[:-1]]
    piece = in_vmem((rows // 2, width), BF16)
    held = list(call(halve_kernel, "halve", [VMEM] * 2, [piece, piece])(kept, got))
    swapped = []
    for k in range(len(bits)):
        last = k == len(bits) - 1
        got = [exchange(value, order[k]) for value, order in zip(held, orders)]
        for chain in range(2):
            after = beside[k : k + 1] if chain == 0 else []
            held[chain] = call(
                functools.partial(add_kernel, scale=scale if last else 1.0),
                "add",
                [VMEM] * 2 + [ANY] * len(after),
                piece,
                flops=2 * 10**8 if last else 0,
            )(held[chain], got[chain], *after)
    swapped = [exchange(value, 1) for value in held]

    def place(values, places, *begun):
        return call(
            functools.partial(place_kernel, places=places),
            "place",
            [VMEM] * len(values) + [ANY] * len(begun),
            jax.ShapeDtypeStruct((2 * rows, width), F32),
            out_specs=ANY,
            scratch=[
                pltpu.VMEM((len(values), rows // 2, width), F32),
                pltpu.SemaphoreType.DMA((len(values),)),
            ],
            aliases={len(values): 0} if begun else None,
        )(*values, *begun)

    early = place([held[0], held[1], swapped[0]], [(0, True), (1, True), (0, False)])
    return place([swapped[1]], [(1, False)], early)


def per_device(embeddings, edge_tiles, neighbour, propensity, queries, positives):
    count = lax.axis_size(AXIS)
    blocks, _, block, _ = edge_tiles.shape
    labels_dev, width = embeddings.shape
    rows = queries.shape[0]
    lists = neighbour.T
    odd = range(1, count, 2)
    off_route = [(i, (i + 1) % count) for i in odd] + [((i + 1) % count, i) for i in odd]

    def off_swap(value):
        return lax.ppermute(value, AXIS, off_route)

    def on_swap(value):
        return exchange(value, 1)

    one = in_vmem((rows, block), BF16)
    pair = in_vmem((2, rows, block), BF16)
    third = -(-2 * rows // 48) * 16
    thirds = [in_vmem((size, block), BF16) for size in (third, third, 2 * rows - 2 * third)]
    full = (blocks, rows, block)
    scale = 1.0 / math.sqrt(width)

    off_a, queries, embeddings, lists = call(
        functools.partial(project_kernel, scale=scale),
        "project",
        [HBM] * 3,
        [
            one,
            in_vmem(queries.shape, BF16),
            in_vmem(embeddings.shape, BF16),
            pltpu.SMEM(lists.shape, jnp.int32),
        ],
        out_specs=[VMEM] * 3 + [SMEM],
        scratch=[pltpu.SemaphoreType.DMA((2 + blocks,))],
    )(*(pltpu.with_memory_space_constraint(x, pltpu.HBM) for x in (lists, queries, embeddings)))
    from_off_a = off_swap(off_a)
    own, off_b, *for_on = call(
        functools.partial(own_kernel, scale=scale),
        "own",
        [SMEM, VMEM, VMEM],
        [in_vmem(full, F32), one] + thirds,
    )(lists, queries, embeddings)
    from_on = [on_swap(piece) for piece in for_on]
    hits, tiles = call(
        hits_kernel,
        "hits",
        [VMEM, HBM],
        [in_vmem(full, BF16), in_vmem(edge_tiles.shape, BF16)],
        scratch=[pltpu.SemaphoreType.DMA],
    )(positives.T, pltpu.with_memory_space_constraint(edge_tiles, pltpu.HBM))
    from_off_b = off_swap(off_b)
    base = call(
        base_kernel,
        "base",
        [SMEM] + [VMEM] * 5,
        in_vmem(full, F32),
        scratch=[pltpu.VMEM((2, rows, block), BF16)],
    )(lists, own, tiles, *from_on)
    propensity = propensity.reshape(1, labels_dev)

    def signal_of(received, slot, *begun):
        return call(
            functools.partial(signal_kernel, slot=slot),
            "signal",
            [SMEM] + [VMEM] * (5 + len(begun)),
            [in_vmem(full, BF16), one],
            scratch=[pltpu.VMEM((rows, block), F32)],
            aliases={6: 0} if begun else None,
            flops=0 if begun else 2 * 10**9,
        )(lists, base, hits, propensity, received, tiles, *begun)

    signal, push_a = signal_of(from_off_a, 0)
    back_a = off_swap(push_a)
    signal, push_b = signal_of(from_off_b, 1, signal)
    back_b = off_swap(push_b)
    push_on = call(
        push_kernel,
        "push",
        [SMEM, VMEM, VMEM],
        thirds,
        scratch=[pltpu.VMEM((2, rows, block), F32)],
    )(lists, signal, tiles)
    back_on = [on_swap(piece) for piece in push_on]

    whole = in_vmem((rows, width), F32)
    part = call(query_kernel, "query", [VMEM] * 2, whole)(signal, embeddings)
    part = call(
        functools.partial(query_half_kernel, blocks=blocks),
        "query_half",
        [SMEM] + [VMEM] * 3,
        whole,
        flops=10**9,
    )(lists, part, back_a, embeddings)
    part, on = call(
        functools.partial(query_on_kernel, blocks=blocks), "query_on", [SMEM] + [VMEM] * 5, [whole, pair]
    )(lists, part, embeddings, *back_on)
    ready = in_vmem((block, width), BF16)
    written = jax.ShapeDtypeStruct((labels_dev, width), BF16)

    def embed(turn, outs):
        values = [lists, signal, on, back_a, queries] + ([back_b] if turn == blocks - 1 else []) + outs[::-1]
        return call(
            functools.partial(embed_kernel, blocks=blocks, turn=turn, scale=1.0 / math.sqrt(rows)),
            "embed",
            [SMEM] + [VMEM] * (len(values) - 1 - (turn > 1)) + [ANY] * (turn > 1),
            ([written] if turn else []) + [ready, in_vmem((8, 128), F32)],
            out_specs=([ANY] if turn else []) + [VMEM] * 2,
            scratch=[pltpu.VMEM((rows, block), F32)] + ([pltpu.SemaphoreType.DMA((2,))] if turn else []),
            aliases={len(values) - 1: 0} if turn > 1 else None,
        )(*values)

    *outs, token = embed(0, [])
    tokens = [token]

    def query_end(own, kind):
        return call(
            functools.partial(query_end_kernel, blocks=blocks, own=own),
            "query_end",
            [SMEM] + [VMEM] * 3 + [ANY],
            in_vmem((rows // 2, width), kind),
        )(lists, part, back_b, embeddings, tokens[0])

    sent, kept = query_end(False, BF16), query_end(True, F32)
    for turn in range(1, blocks):
        *outs, token = embed(turn, outs)
        tokens.append(token)
    grad_embed = outs[0]
    grad_queries = sum_queries(kept, sent, tokens[1:], 1.0 / math.sqrt(labels_dev * count))
    return (grad_embed, grad_queries)


def solution(mesh):
    placed = (
        P("labels", None),
        P("labels", None, None, None),
        P(),
        P("labels"),
        P("groups", None),
        P("groups", None),
    )
    return jax.shard_map(
        per_device,
        mesh=mesh,
        in_specs=placed,
        out_specs=(P(("groups", "labels"), None), P("groups", None)),
        check_vma=False,
    )
```

```python
import functools
import math

import jax
import jax.numpy as jnp
from jax import lax
from jax.experimental import pallas as pl
from jax.experimental.pallas import tpu as pltpu
from jax.sharding import PartitionSpec as P

AXIS = "labels"
BF16 = jnp.bfloat16
F32 = jnp.float32
NT = (((1,), (1,)), ((), ()))
NN = (((1,), (0,)), ((), ()))
TN = (((0,), (0,)), ((), ()))
MIB = 1024 * 1024

OFF, ON = True, False


def dot(a, b, dims):
    return lax.dot_general(a, b, dims, preferred_element_type=F32)


def own_side(device, off):
    odd = device % 2
    return 1 - odd if off else odd


def partner_of(device, count, off):
    ahead = jnp.where(device == count - 1, 0, device + 1)
    behind = jnp.where(device == 0, count - 1, device - 1)
    return jnp.where(own_side(device, off) == 0, ahead, behind)


def own_list(lists, blocks, off):
    device = lax.axis_index(AXIS)
    side = own_side(device, off)
    return [lists[side, device * blocks + g] for g in range(blocks)]


def slots_of(lists, blocks, off):
    named = own_list(lists, blocks, off)
    least = functools.reduce(jnp.minimum, named)
    return [(value != least).astype(jnp.int32) for value in named]


def named_by_partner(lists, blocks, off):
    device = lax.axis_index(AXIS)
    partner = partner_of(device, lax.axis_size(AXIS), off)
    side = 1 - own_side(device, off)
    named = [lists[side, partner * blocks + g] for g in range(blocks)]
    return functools.reduce(jnp.minimum, named), functools.reduce(jnp.maximum, named)


def tile_side(off):
    return own_side(lax.axis_index(AXIS), off)


def block_rows(ref, index, block):
    return ref[pl.ds(pl.multiple_of(index * block, block), block), :]


def project_kernel(lists, queries, embeddings, out, left, table, right, sem, *, scale):
    block = out.shape[1]
    fetch_lists = pltpu.make_async_copy(lists, table, sem.at[0])
    fetch_queries = pltpu.make_async_copy(queries, left, sem.at[1])
    fetch_lists.start()
    fetch_queries.start()
    fetch_lists.wait()
    first, _ = named_by_partner(table, embeddings.shape[0] // block, OFF)
    place = pl.ds(pl.multiple_of(first * block, block), block)
    fetch = pltpu.make_async_copy(embeddings.at[place, :], right, sem.at[2])
    fetch.start()
    fetch_queries.wait()
    fetch.wait()
    out[...] = (dot(left[...], right[...], NT) * scale).astype(BF16)


def spans_of(pieces, rows):
    spans = []
    begin = 0
    for piece in pieces:
        end = begin + piece.shape[0]
        for slot in range(2):
            low, high = max(begin, slot * rows), min(end, (slot + 1) * rows)
            if low < high:
                inside = slice(low - slot * rows, high - slot * rows)
                spans.append((piece, slice(low - begin, high - begin), slot, inside))
        begin = end
    return spans


def write_pieces(pieces, value):
    rows = sum(piece.shape[0] for piece in pieces) // 2
    for piece, place, slot, inside in spans_of(pieces, rows):
        piece[place, :] = value(slot, inside).astype(BF16)


def gather_pieces(pieces, whole):
    for piece, place, slot, inside in spans_of(pieces, whole.shape[1]):
        whole[slot, inside] = piece[place, :]


def own_kernel(lists, queries, embeddings, own, off, right, *rest, scale):
    *on, sem = rest
    blocks, _, block = own.shape
    fetches = []
    for g in range(blocks):
        rows = pl.ds(g * block, block)
        fetches.append(pltpu.make_async_copy(embeddings.at[rows, :], right.at[rows, :], sem.at[g]))
        fetches[-1].start()
    for g in range(blocks):
        fetches[g].wait()
        own[g] = dot(queries[...], right[g * block : (g + 1) * block, :], NT) * scale
    _, second = named_by_partner(lists, blocks, OFF)
    off[...] = own[second].astype(BF16)
    first, second = named_by_partner(lists, blocks, ON)
    write_pieces(on, lambda slot, rows: own[(first, second)[slot], rows])


def hits_kernel(positives, tiles, out, kept, sem):
    fetch = pltpu.make_async_copy(tiles, kept, sem)
    fetch.start()
    blocks, rows, block = out.shape
    first = lax.axis_index(AXIS) * blocks * block
    ids = lax.broadcasted_iota(jnp.int32, (rows, block), 1)
    columns = jnp.transpose(positives[...]) - first
    for g in range(blocks):
        hits = jnp.zeros((rows, block), jnp.bool_)
        for column in range(positives.shape[0]):
            hits = jnp.logical_or(hits, ids + g * block == columns[:, column : column + 1])
        out[g] = jnp.where(hits, 1.0, 0.0).astype(BF16)
    fetch.wait()


def base_kernel(lists, own, tiles, *rest):
    *pieces, out, received = rest
    gather_pieces(pieces, received)
    blocks = out.shape[0]
    side = tile_side(ON)
    for g, slot in enumerate(slots_of(lists, blocks, ON)):
        out[g] = own[g] + dot(received[slot], tiles[g, side], NT)


def signal_kernel(lists, base, hits, propensity, received, tiles, *rest, slot):
    signal, push, total = rest[-3:]
    blocks, _, block = base.shape
    side = tile_side(OFF)
    total[...] = jnp.zeros_like(total)
    for g, taken in enumerate(slots_of(lists, blocks, OFF)):

        @pl.when(taken == slot)
        def _():
            scores = base[g] + dot(received[...], tiles[g, side], NT)
            inverse = 1.0 / propensity[:, g * block : (g + 1) * block]
            value = (jax.nn.sigmoid(scores) - hits[g].astype(F32) * inverse).astype(BF16)
            signal[g] = value
            total[...] += dot(value, tiles[g, side], NN)

    push[...] = total[...].astype(BF16)


def push_kernel(lists, signal, tiles, *rest):
    *pieces, total = rest
    blocks = signal.shape[0]
    side = tile_side(ON)
    total[...] = jnp.zeros_like(total)
    for g, slot in enumerate(slots_of(lists, blocks, ON)):
        total[slot] += dot(signal[g], tiles[g, side], NN)
    write_pieces(pieces, lambda slot, rows: total[slot, rows])


def query_kernel(signal, embeddings, out):
    blocks, _, block = signal.shape
    total = dot(signal[0], embeddings[0:block, :], NN)
    for g in range(1, blocks):
        total += dot(signal[g], embeddings[g * block : (g + 1) * block, :], NN)
    out[...] = total


def query_half_kernel(lists, part, received, embeddings, out, *, blocks):
    first, _ = named_by_partner(lists, blocks, OFF)
    out[...] = part[...] + dot(received[...], block_rows(embeddings, first, received.shape[1]), NN)


def query_on_kernel(lists, part, embeddings, *rest, blocks):
    *pieces, out, received = rest
    gather_pieces(pieces, received)
    block = received.shape[2]
    first, second = named_by_partner(lists, blocks, ON)
    out[...] = (
        part[...]
        + dot(received[0], block_rows(embeddings, first, block), NN)
        + dot(received[1], block_rows(embeddings, second, block), NN)
    )


def query_end_kernel(lists, part, received, embeddings, after, out, *, blocks, own):
    del after
    _, second = named_by_partner(lists, blocks, OFF)
    rows = out.shape[0]
    core = lax.axis_index(AXIS) % 2
    half = core if own else 1 - core
    place = pl.ds(pl.multiple_of(half * rows, rows), rows)
    right = block_rows(embeddings, second, received.shape[1])
    out[...] = (part[place, :] + dot(received[place, :], right, NN)).astype(out.dtype)


def embed_kernel(lists, signal, on, off_a, queries, *rest, blocks, turn, scale):
    last = turn == blocks - 1
    off = [off_a]
    if last:
        off.append(rest[0])
        rest = rest[1:]
    if turn == 0:
        ready, token, total = rest
    else:
        before = rest[0]
        out, ready, token, total, sem = rest[-5:]
    rows, block = total.shape
    writes = []

    def write(source, index, slot):
        place = out.at[pl.ds(pl.multiple_of(index * block, block), block), :]
        writes.append(pltpu.make_async_copy(source, place, sem.at[slot]))
        writes[-1].start()

    named = named_by_partner(lists, blocks, ON) + named_by_partner(lists, blocks, OFF)
    g = (named[3] + 1 + turn) % blocks
    if turn > 0:
        write(before, (named[3] + turn) % blocks, 0)
    token[...] = jnp.zeros_like(token)
    total[...] = signal[g].astype(F32)
    for received, index in zip([on.at[0], on.at[1], *off], named):

        @pl.when(index == g)
        def _():
            total[...] += received[...].astype(F32)

    ready[...] = (dot(total[...].astype(BF16), queries[...], TN) * scale).astype(BF16)
    if last:
        write(ready, g, 1)
    for copy in writes:
        copy.wait()


VMEM = pl.BlockSpec(memory_space=pltpu.VMEM)
SMEM = pl.BlockSpec(memory_space=pltpu.SMEM)
ANY = pl.BlockSpec(memory_space=pl.ANY)
HBM = pl.BlockSpec(memory_space=pltpu.HBM)


def call(kernel, name, in_specs, out_shape, out_specs=None, scratch=(), aliases=None, vmem=12, flops=0):
    if out_specs is None:
        out_specs = jax.tree.map(lambda _: VMEM, out_shape)
    return pl.pallas_call(
        kernel,
        in_specs=in_specs,
        out_specs=out_specs,
        out_shape=out_shape,
        scratch_shapes=scratch,
        input_output_aliases=aliases or {},
        name=name,
        cost_estimate=pl.CostEstimate(flops=flops, bytes_accessed=0, transcendentals=0),
        compiler_params=pltpu.CompilerParams(vmem_limit_bytes=vmem * MIB),
    )


def exchange(value, mask):
    count = lax.axis_size(AXIS)
    return lax.ppermute(value, AXIS, [(i, i ^ mask) for i in range(count)])


def in_vmem(shape, dtype):
    return pltpu.VMEM(shape, dtype)


def digit_of(bit):
    return (lax.axis_index(AXIS) // bit) % 2


def halve_kernel(held, got, *outs):
    total = held[...] + got[...].astype(F32)
    rows = outs[0].shape[0]
    for chain, out in enumerate(outs):
        out[...] = total[chain * rows : (chain + 1) * rows, :].astype(BF16)


def add_kernel(held, got, *rest, scale):
    rest[-1][...] = ((held[...].astype(F32) + got[...].astype(F32)) * scale).astype(BF16)


def place_kernel(*refs, places):
    out, wide, sem = refs[-3:]
    rows = refs[0].shape[0]
    core = lax.axis_index(AXIS) % 2
    copies = []
    for k, (chain, own) in enumerate(places):
        wide[k] = refs[k][...].astype(F32)
        half = core if own else 1 - core
        begin = pl.multiple_of((2 * half + chain) * rows, rows)
        copies.append(pltpu.make_async_copy(wide.at[k], out.at[pl.ds(begin, rows), :], sem.at[k]))
        copies[-1].start()
    for copy in copies:
        copy.wait()


def sum_queries(kept, sent, beside, scale):
    count = lax.axis_size(AXIS)
    rows, width = kept.shape
    got = exchange(sent, 1)
    if count & (count - 1) or count < 8:
        half = kept + got.astype(F32)
        half = lax.psum(half, AXIS, axis_index_groups=[list(range(c, count, 2)) for c in range(2)])
        both = jnp.stack([half, exchange(half, 1)])
        both = jnp.where(lax.axis_index(AXIS) % 2 == 0, both, both[::-1])
        return both.reshape(2 * rows, width) * scale
    bits = [1 << k for k in range(1, count.bit_length() - 1)]
    orders = [bits, bits[-1:] + bits[:-1]]
    piece = in_vmem((rows // 2, width), BF16)
    held = list(call(halve_kernel, "halve", [VMEM] * 2, [piece, piece])(kept, got))
    swapped = []
    for k in range(len(bits)):
        last = k == len(bits) - 1
        got = [exchange(value, order[k]) for value, order in zip(held, orders)]
        for chain in range(2):
            after = beside[k : k + 1] if chain == 0 else []
            held[chain] = call(
                functools.partial(add_kernel, scale=scale if last else 1.0),
                "add",
                [VMEM] * 2 + [ANY] * len(after),
                piece,
                flops=2 * 10**8 if last else 0,
            )(held[chain], got[chain], *after)
    swapped = [exchange(value, 1) for value in held]

    def place(values, places, *begun):
        return call(
            functools.partial(place_kernel, places=places),
            "place",
            [VMEM] * len(values) + [ANY] * len(begun),
            jax.ShapeDtypeStruct((2 * rows, width), F32),
            out_specs=ANY,
            scratch=[
                pltpu.VMEM((len(values), rows // 2, width), F32),
                pltpu.SemaphoreType.DMA((len(values),)),
            ],
            aliases={len(values): 0} if begun else None,
        )(*values, *begun)

    early = place(held, [(0, True), (1, True)])
    return place(swapped, [(0, False), (1, False)], early)


def per_device(embeddings, edge_tiles, neighbour, propensity, queries, positives):
    count = lax.axis_size(AXIS)
    blocks, _, block, _ = edge_tiles.shape
    labels_dev, width = embeddings.shape
    rows = queries.shape[0]
    lists = neighbour.T
    odd = range(1, count, 2)
    off_route = [(i, (i + 1) % count) for i in odd] + [((i + 1) % count, i) for i in odd]

    def off_swap(value):
        return lax.ppermute(value, AXIS, off_route)

    def on_swap(value):
        return exchange(value, 1)

    one = in_vmem((rows, block), BF16)
    pair = in_vmem((2, rows, block), BF16)
    third = -(-2 * rows // 48) * 16
    thirds = [in_vmem((size, block), BF16) for size in (third, third, 2 * rows - 2 * third)]
    full = (blocks, rows, block)
    scale = 1.0 / math.sqrt(width)

    lists, narrow, stored = (pltpu.with_memory_space_constraint(x, pltpu.HBM) for x in (lists, queries, embeddings))
    off_a, queries, lists = call(
        functools.partial(project_kernel, scale=scale),
        "project",
        [HBM] * 3,
        [one, in_vmem(queries.shape, BF16), pltpu.SMEM(lists.shape, jnp.int32)],
        out_specs=[VMEM] * 2 + [SMEM],
        scratch=[pltpu.VMEM((block, width), BF16), pltpu.SemaphoreType.DMA((3,))],
    )(lists, narrow, stored)
    from_off_a = off_swap(off_a)
    own, off_b, embeddings, *for_on = call(
        functools.partial(own_kernel, scale=scale),
        "own",
        [SMEM, VMEM, HBM],
        [in_vmem(full, F32), one, in_vmem(embeddings.shape, BF16)] + thirds,
        scratch=[pltpu.SemaphoreType.DMA((blocks,))],
    )(lists, queries, stored)
    from_off_b = off_swap(off_b)
    from_on = [on_swap(piece) for piece in for_on]
    hits, tiles = call(
        hits_kernel,
        "hits",
        [VMEM, HBM],
        [in_vmem(full, BF16), in_vmem(edge_tiles.shape, BF16)],
        scratch=[pltpu.SemaphoreType.DMA],
    )(positives.T, pltpu.with_memory_space_constraint(edge_tiles, pltpu.HBM))
    base = call(
        base_kernel,
        "base",
        [SMEM] + [VMEM] * 5,
        in_vmem(full, F32),
        scratch=[pltpu.VMEM((2, rows, block), BF16)],
    )(lists, own, tiles, *from_on)
    propensity = propensity.reshape(1, labels_dev)

    def signal_of(received, slot, *begun):
        return call(
            functools.partial(signal_kernel, slot=slot),
            "signal",
            [SMEM] + [VMEM] * (5 + len(begun)),
            [in_vmem(full, BF16), one],
            scratch=[pltpu.VMEM((rows, block), F32)],
            aliases={6: 0} if begun else None,
            flops=0 if begun else 2 * 10**9,
        )(lists, base, hits, propensity, received, tiles, *begun)

    signal, push_a = signal_of(from_off_a, 0)
    back_a = off_swap(push_a)
    signal, push_b = signal_of(from_off_b, 1, signal)
    back_b = off_swap(push_b)
    push_on = call(
        push_kernel,
        "push",
        [SMEM, VMEM, VMEM],
        thirds,
        scratch=[pltpu.VMEM((2, rows, block), F32)],
    )(lists, signal, tiles)
    back_on = [on_swap(piece) for piece in push_on]

    whole = in_vmem((rows, width), F32)
    part = call(query_kernel, "query", [VMEM] * 2, whole)(signal, embeddings)
    part = call(
        functools.partial(query_half_kernel, blocks=blocks),
        "query_half",
        [SMEM] + [VMEM] * 3,
        whole,
        flops=10**9,
    )(lists, part, back_a, embeddings)
    part, on = call(
        functools.partial(query_on_kernel, blocks=blocks), "query_on", [SMEM] + [VMEM] * 5, [whole, pair]
    )(lists, part, embeddings, *back_on)
    ready = in_vmem((block, width), BF16)
    written = jax.ShapeDtypeStruct((labels_dev, width), BF16)

    def embed(turn, outs):
        values = [lists, signal, on, back_a, queries] + ([back_b] if turn == blocks - 1 else []) + outs[::-1]
        return call(
            functools.partial(embed_kernel, blocks=blocks, turn=turn, scale=1.0 / math.sqrt(rows)),
            "embed",
            [SMEM] + [VMEM] * (len(values) - 1 - (turn > 1)) + [ANY] * (turn > 1),
            ([written] if turn else []) + [ready, in_vmem((8, 128), F32)],
            out_specs=([ANY] if turn else []) + [VMEM] * 2,
            scratch=[pltpu.VMEM((rows, block), F32)] + ([pltpu.SemaphoreType.DMA((2,))] if turn else []),
            aliases={len(values) - 1: 0} if turn > 1 else None,
        )(*values)

    *outs, token = embed(0, [])
    tokens = [token]

    def query_end(own, kind):
        return call(
            functools.partial(query_end_kernel, blocks=blocks, own=own),
            "query_end",
            [SMEM] + [VMEM] * 3 + [ANY],
            in_vmem((rows // 2, width), kind),
        )(lists, part, back_b, embeddings, tokens[0])

    sent, kept = query_end(False, BF16), query_end(True, F32)
    for turn in range(1, blocks):
        *outs, token = embed(turn, outs)
        tokens.append(token)
    grad_embed = outs[0]
    grad_queries = sum_queries(kept, sent, tokens[1:], 1.0 / math.sqrt(labels_dev * count))
    return (grad_embed, grad_queries)


def solution(mesh):
    placed = (
        P("labels", None),
        P("labels", None, None, None),
        P(),
        P("labels"),
        P("groups", None),
        P("groups", None),
    )
    return jax.shard_map(
        per_device,
        mesh=mesh,
        in_specs=placed,
        out_specs=(P(("groups", "labels"), None), P("groups", None)),
        check_vma=False,
    )
```

```python
import functools
import math

import jax
import jax.numpy as jnp
from jax import lax
from jax.experimental import pallas as pl
from jax.experimental.pallas import tpu as pltpu
from jax.sharding import PartitionSpec as P

AXIS = "labels"
BF16 = jnp.bfloat16
F32 = jnp.float32
NT = (((1,), (1,)), ((), ()))
NN = (((1,), (0,)), ((), ()))
TN = (((0,), (0,)), ((), ()))
MIB = 1024 * 1024

OFF, ON = True, False


def dot(a, b, dims):
    return lax.dot_general(a, b, dims, preferred_element_type=F32)


def own_side(device, off):
    odd = device % 2
    return 1 - odd if off else odd


def partner_of(device, count, off):
    ahead = jnp.where(device == count - 1, 0, device + 1)
    behind = jnp.where(device == 0, count - 1, device - 1)
    return jnp.where(own_side(device, off) == 0, ahead, behind)


def own_list(lists, blocks, off):
    device = lax.axis_index(AXIS)
    side = own_side(device, off)
    return [lists[side, device * blocks + g] for g in range(blocks)]


def slots_of(lists, blocks, off):
    named = own_list(lists, blocks, off)
    least = functools.reduce(jnp.minimum, named)
    return [(value != least).astype(jnp.int32) for value in named]


def named_by_partner(lists, blocks, off):
    device = lax.axis_index(AXIS)
    partner = partner_of(device, lax.axis_size(AXIS), off)
    side = 1 - own_side(device, off)
    named = [lists[side, partner * blocks + g] for g in range(blocks)]
    return functools.reduce(jnp.minimum, named), functools.reduce(jnp.maximum, named)


def tile_side(off):
    return own_side(lax.axis_index(AXIS), off)


def block_rows(ref, index, block):
    return ref[pl.ds(pl.multiple_of(index * block, block), block), :]


def project_kernel(lists, queries, embeddings, out, left, right, table, sem, list_sem, *, scale):
    rows, block = out.shape
    blocks = right.shape[0] // block
    parts = sem.shape[0] // (blocks + 1)

    def fetches_of(source, target, begin, size, slot):
        copies = []
        for part in range(parts):
            place = pl.ds(pl.multiple_of(begin + part * size // parts, size // parts), size // parts)
            copies.append(pltpu.make_async_copy(source.at[place, :], target.at[place, :], sem.at[slot * parts + part]))
        return copies

    def wait_all(copies):
        for copy in copies:
            copy.wait()

    fetch_lists = pltpu.make_async_copy(lists, table, list_sem)
    fetch_lists.start()
    fetch_queries = fetches_of(queries, left, 0, rows, blocks)
    fetch_blocks = [fetches_of(embeddings, right, g * block, block, g) for g in range(blocks)]
    for copies in [fetch_queries, *fetch_blocks]:
        for copy in copies:
            copy.start()
    fetch_lists.wait()
    first, _ = named_by_partner(table, blocks, OFF)
    wait_all(fetch_queries)
    wait_all(fetches_of(embeddings, right, first * block, block, first))
    out[...] = (dot(left[...], block_rows(right, first, block), NT) * scale).astype(BF16)
    for g in range(blocks):

        @pl.when(g != first)
        def _():
            wait_all(fetch_blocks[g])


def spans_of(pieces, rows):
    spans = []
    begin = 0
    for piece in pieces:
        end = begin + piece.shape[0]
        for slot in range(2):
            low, high = max(begin, slot * rows), min(end, (slot + 1) * rows)
            if low < high:
                inside = slice(low - slot * rows, high - slot * rows)
                spans.append((piece, slice(low - begin, high - begin), slot, inside))
        begin = end
    return spans


def write_pieces(pieces, value):
    rows = sum(piece.shape[0] for piece in pieces) // 2
    for piece, place, slot, inside in spans_of(pieces, rows):
        piece[place, :] = value(slot, inside).astype(BF16)


def gather_pieces(pieces, whole):
    for piece, place, slot, inside in spans_of(pieces, whole.shape[1]):
        whole[slot, inside] = piece[place, :]


def own_kernel(lists, queries, embeddings, own, off, *on, scale):
    blocks, _, block = own.shape
    for g in range(blocks):
        own[g] = dot(queries[...], embeddings[g * block : (g + 1) * block, :], NT) * scale
    _, second = named_by_partner(lists, blocks, OFF)
    off[...] = own[second].astype(BF16)
    first, second = named_by_partner(lists, blocks, ON)
    write_pieces(on, lambda slot, rows: own[(first, second)[slot], rows])


def hits_kernel(positives, tiles, out, kept, sem):
    fetch = pltpu.make_async_copy(tiles, kept, sem)
    fetch.start()
    blocks, rows, block = out.shape
    first = lax.axis_index(AXIS) * blocks * block
    ids = lax.broadcasted_iota(jnp.int32, (rows, block), 1)
    columns = jnp.transpose(positives[...]) - first
    for g in range(blocks):
        hits = jnp.zeros((rows, block), jnp.bool_)
        for column in range(positives.shape[0]):
            hits = jnp.logical_or(hits, ids + g * block == columns[:, column : column + 1])
        out[g] = jnp.where(hits, 1.0, 0.0).astype(BF16)
    fetch.wait()


def base_kernel(lists, own, tiles, *rest):
    *pieces, out, received = rest
    gather_pieces(pieces, received)
    blocks = out.shape[0]
    side = tile_side(ON)
    for g, slot in enumerate(slots_of(lists, blocks, ON)):
        out[g] = own[g] + dot(received[slot], tiles[g, side], NT)


def signal_kernel(lists, base, hits, propensity, received, tiles, *rest, slot):
    signal, push, total = rest[-3:]
    blocks, _, block = base.shape
    side = tile_side(OFF)
    total[...] = jnp.zeros_like(total)
    for g, taken in enumerate(slots_of(lists, blocks, OFF)):

        @pl.when(taken == slot)
        def _():
            scores = base[g] + dot(received[...], tiles[g, side], NT)
            inverse = 1.0 / propensity[:, g * block : (g + 1) * block]
            value = (jax.nn.sigmoid(scores) - hits[g].astype(F32) * inverse).astype(BF16)
            signal[g] = value
            total[...] += dot(value, tiles[g, side], NN)

    push[...] = total[...].astype(BF16)


def push_kernel(lists, signal, tiles, *rest):
    *pieces, total = rest
    blocks = signal.shape[0]
    side = tile_side(ON)
    total[...] = jnp.zeros_like(total)
    for g, slot in enumerate(slots_of(lists, blocks, ON)):
        total[slot] += dot(signal[g], tiles[g, side], NN)
    write_pieces(pieces, lambda slot, rows: total[slot, rows])


def query_kernel(signal, embeddings, out):
    blocks, _, block = signal.shape
    total = dot(signal[0], embeddings[0:block, :], NN)
    for g in range(1, blocks):
        total += dot(signal[g], embeddings[g * block : (g + 1) * block, :], NN)
    out[...] = total


def query_half_kernel(lists, part, received, embeddings, out, *, blocks):
    first, _ = named_by_partner(lists, blocks, OFF)
    out[...] = part[...] + dot(received[...], block_rows(embeddings, first, received.shape[1]), NN)


def query_on_kernel(lists, part, embeddings, *rest, blocks):
    *pieces, out, received = rest
    gather_pieces(pieces, received)
    block = received.shape[2]
    first, second = named_by_partner(lists, blocks, ON)
    out[...] = (
        part[...]
        + dot(received[0], block_rows(embeddings, first, block), NN)
        + dot(received[1], block_rows(embeddings, second, block), NN)
    )


def query_end_kernel(lists, part, received, embeddings, after, out, *, blocks, own):
    del after
    _, second = named_by_partner(lists, blocks, OFF)
    rows = out.shape[0]
    core = lax.axis_index(AXIS) % 2
    half = core if own else 1 - core
    place = pl.ds(pl.multiple_of(half * rows, rows), rows)
    right = block_rows(embeddings, second, received.shape[1])
    out[...] = (part[place, :] + dot(received[place, :], right, NN)).astype(out.dtype)


def embed_kernel(lists, signal, on, off_a, queries, *rest, blocks, turn, scale):
    last = turn == blocks - 1
    off = [off_a]
    if last:
        off.append(rest[0])
        rest = rest[1:]
    if turn == 0:
        ready, token, total = rest
    else:
        before = rest[0]
        out, ready, token, total, sem = rest[-5:]
    rows, block = total.shape
    writes = []

    def write(source, index, slot):
        place = out.at[pl.ds(pl.multiple_of(index * block, block), block), :]
        writes.append(pltpu.make_async_copy(source, place, sem.at[slot]))
        writes[-1].start()

    named = named_by_partner(lists, blocks, ON) + named_by_partner(lists, blocks, OFF)
    g = (named[3] + 1 + turn) % blocks
    if turn > 0:
        write(before, (named[3] + turn) % blocks, 0)
    token[...] = jnp.zeros_like(token)
    total[...] = signal[g].astype(F32)
    for received, index in zip([on.at[0], on.at[1], *off], named):

        @pl.when(index == g)
        def _():
            total[...] += received[...].astype(F32)

    ready[...] = (dot(total[...].astype(BF16), queries[...], TN) * scale).astype(BF16)
    if last:
        write(ready, g, 1)
    for copy in writes:
        copy.wait()


VMEM = pl.BlockSpec(memory_space=pltpu.VMEM)
SMEM = pl.BlockSpec(memory_space=pltpu.SMEM)
ANY = pl.BlockSpec(memory_space=pl.ANY)
HBM = pl.BlockSpec(memory_space=pltpu.HBM)


def call(kernel, name, in_specs, out_shape, out_specs=None, scratch=(), aliases=None, vmem=12, flops=0):
    if out_specs is None:
        out_specs = jax.tree.map(lambda _: VMEM, out_shape)
    return pl.pallas_call(
        kernel,
        in_specs=in_specs,
        out_specs=out_specs,
        out_shape=out_shape,
        scratch_shapes=scratch,
        input_output_aliases=aliases or {},
        name=name,
        cost_estimate=pl.CostEstimate(flops=flops, bytes_accessed=0, transcendentals=0),
        compiler_params=pltpu.CompilerParams(vmem_limit_bytes=vmem * MIB),
    )


def exchange(value, mask):
    count = lax.axis_size(AXIS)
    return lax.ppermute(value, AXIS, [(i, i ^ mask) for i in range(count)])


def in_vmem(shape, dtype):
    return pltpu.VMEM(shape, dtype)


def digit_of(bit):
    return (lax.axis_index(AXIS) // bit) % 2


def halve_kernel(held, got, *outs):
    total = held[...] + got[...].astype(F32)
    rows = outs[0].shape[0]
    for chain, out in enumerate(outs):
        out[...] = total[chain * rows : (chain + 1) * rows, :].astype(BF16)


def add_kernel(held, got, *rest, scale):
    rest[-1][...] = ((held[...].astype(F32) + got[...].astype(F32)) * scale).astype(BF16)


def place_kernel(*refs, places):
    out, wide, sem = refs[-3:]
    rows = refs[0].shape[0]
    core = lax.axis_index(AXIS) % 2
    copies = []
    for k, (chain, own) in enumerate(places):
        wide[k] = refs[k][...].astype(F32)
        half = core if own else 1 - core
        begin = pl.multiple_of((2 * half + chain) * rows, rows)
        copies.append(pltpu.make_async_copy(wide.at[k], out.at[pl.ds(begin, rows), :], sem.at[k]))
        copies[-1].start()
    for copy in copies:
        copy.wait()


def sum_queries(kept, sent, beside, scale):
    count = lax.axis_size(AXIS)
    rows, width = kept.shape
    got = exchange(sent, 1)
    if count & (count - 1) or count < 8:
        half = kept + got.astype(F32)
        half = lax.psum(half, AXIS, axis_index_groups=[list(range(c, count, 2)) for c in range(2)])
        both = jnp.stack([half, exchange(half, 1)])
        both = jnp.where(lax.axis_index(AXIS) % 2 == 0, both, both[::-1])
        return both.reshape(2 * rows, width) * scale
    bits = [1 << k for k in range(1, count.bit_length() - 1)]
    orders = [bits, bits[-1:] + bits[:-1]]
    piece = in_vmem((rows // 2, width), BF16)
    held = list(call(halve_kernel, "halve", [VMEM] * 2, [piece, piece])(kept, got))
    swapped = []
    for k in range(len(bits)):
        last = k == len(bits) - 1
        got = [exchange(value, order[k]) for value, order in zip(held, orders)]
        for chain in range(2):
            after = beside[k : k + 1] if chain == 0 else []
            held[chain] = call(
                functools.partial(add_kernel, scale=scale if last else 1.0),
                "add",
                [VMEM] * 2 + [ANY] * len(after),
                piece,
                flops=2 * 10**8 if last else 0,
            )(held[chain], got[chain], *after)
    swapped = [exchange(value, 1) for value in held]

    def place(values, places, *begun):
        return call(
            functools.partial(place_kernel, places=places),
            "place",
            [VMEM] * len(values) + [ANY] * len(begun),
            jax.ShapeDtypeStruct((2 * rows, width), F32),
            out_specs=ANY,
            scratch=[
                pltpu.VMEM((len(values), rows // 2, width), F32),
                pltpu.SemaphoreType.DMA((len(values),)),
            ],
            aliases={len(values): 0} if begun else None,
        )(*values, *begun)

    early = place([held[0], held[1], swapped[0]], [(0, True), (1, True), (0, False)])
    return place([swapped[1]], [(1, False)], early)


def per_device(embeddings, edge_tiles, neighbour, propensity, queries, positives):
    count = lax.axis_size(AXIS)
    blocks, _, block, _ = edge_tiles.shape
    labels_dev, width = embeddings.shape
    rows = queries.shape[0]
    lists = neighbour.T
    odd = range(1, count, 2)
    off_route = [(i, (i + 1) % count) for i in odd] + [((i + 1) % count, i) for i in odd]

    def off_swap(value):
        return lax.ppermute(value, AXIS, off_route)

    def on_swap(value):
        return exchange(value, 1)

    one = in_vmem((rows, block), BF16)
    pair = in_vmem((2, rows, block), BF16)
    third = -(-2 * rows // 48) * 16
    thirds = [in_vmem((size, block), BF16) for size in (third, third, 2 * rows - 2 * third)]
    full = (blocks, rows, block)
    scale = 1.0 / math.sqrt(width)

    off_a, queries, embeddings, lists = call(
        functools.partial(project_kernel, scale=scale),
        "project",
        [HBM] * 3,
        [
            one,
            in_vmem(queries.shape, BF16),
            in_vmem(embeddings.shape, BF16),
            pltpu.SMEM(lists.shape, jnp.int32),
        ],
        out_specs=[VMEM] * 3 + [SMEM],
        scratch=[pltpu.SemaphoreType.DMA((4 * (blocks + 1),)), pltpu.SemaphoreType.DMA],
    )(*(pltpu.with_memory_space_constraint(x, pltpu.HBM) for x in (lists, queries, embeddings)))
    from_off_a = off_swap(off_a)
    own, off_b, *for_on = call(
        functools.partial(own_kernel, scale=scale),
        "own",
        [SMEM, VMEM, VMEM],
        [in_vmem(full, F32), one] + thirds,
    )(lists, queries, embeddings)
    from_on = [on_swap(piece) for piece in for_on]
    hits, tiles = call(
        hits_kernel,
        "hits",
        [VMEM, HBM],
        [in_vmem(full, BF16), in_vmem(edge_tiles.shape, BF16)],
        scratch=[pltpu.SemaphoreType.DMA],
    )(positives.T, pltpu.with_memory_space_constraint(edge_tiles, pltpu.HBM))
    from_off_b = off_swap(off_b)
    base = call(
        base_kernel,
        "base",
        [SMEM] + [VMEM] * 5,
        in_vmem(full, F32),
        scratch=[pltpu.VMEM((2, rows, block), BF16)],
    )(lists, own, tiles, *from_on)
    propensity = propensity.reshape(1, labels_dev)

    def signal_of(received, slot, *begun):
        return call(
            functools.partial(signal_kernel, slot=slot),
            "signal",
            [SMEM] + [VMEM] * (5 + len(begun)),
            [in_vmem(full, BF16), one],
            scratch=[pltpu.VMEM((rows, block), F32)],
            aliases={6: 0} if begun else None,
            flops=0 if begun else 2 * 10**9,
        )(lists, base, hits, propensity, received, tiles, *begun)

    signal, push_a = signal_of(from_off_a, 0)
    back_a = off_swap(push_a)
    signal, push_b = signal_of(from_off_b, 1, signal)
    back_b = off_swap(push_b)
    push_on = call(
        push_kernel,
        "push",
        [SMEM, VMEM, VMEM],
        thirds,
        scratch=[pltpu.VMEM((2, rows, block), F32)],
    )(lists, signal, tiles)
    back_on = [on_swap(piece) for piece in push_on]

    whole = in_vmem((rows, width), F32)
    part = call(query_kernel, "query", [VMEM] * 2, whole)(signal, embeddings)
    part = call(
        functools.partial(query_half_kernel, blocks=blocks),
        "query_half",
        [SMEM] + [VMEM] * 3,
        whole,
        flops=10**9,
    )(lists, part, back_a, embeddings)
    part, on = call(
        functools.partial(query_on_kernel, blocks=blocks), "query_on", [SMEM] + [VMEM] * 5, [whole, pair]
    )(lists, part, embeddings, *back_on)
    ready = in_vmem((block, width), BF16)
    written = jax.ShapeDtypeStruct((labels_dev, width), BF16)

    def embed(turn, outs):
        values = [lists, signal, on, back_a, queries] + ([back_b] if turn == blocks - 1 else []) + outs[::-1]
        return call(
            functools.partial(embed_kernel, blocks=blocks, turn=turn, scale=1.0 / math.sqrt(rows)),
            "embed",
            [SMEM] + [VMEM] * (len(values) - 1 - (turn > 1)) + [ANY] * (turn > 1),
            ([written] if turn else []) + [ready, in_vmem((8, 128), F32)],
            out_specs=([ANY] if turn else []) + [VMEM] * 2,
            scratch=[pltpu.VMEM((rows, block), F32)] + ([pltpu.SemaphoreType.DMA((2,))] if turn else []),
            aliases={len(values) - 1: 0} if turn > 1 else None,
        )(*values)

    *outs, token = embed(0, [])
    tokens = [token]

    def query_end(own, kind):
        return call(
            functools.partial(query_end_kernel, blocks=blocks, own=own),
            "query_end",
            [SMEM] + [VMEM] * 3 + [ANY],
            in_vmem((rows // 2, width), kind),
        )(lists, part, back_b, embeddings, tokens[0])

    sent, kept = query_end(False, BF16), query_end(True, F32)
    for turn in range(1, blocks):
        *outs, token = embed(turn, outs)
        tokens.append(token)
    grad_embed = outs[0]
    grad_queries = sum_queries(kept, sent, tokens[1:], 1.0 / math.sqrt(labels_dev * count))
    return (grad_embed, grad_queries)


def solution(mesh):
    placed = (
        P("labels", None),
        P("labels", None, None, None),
        P(),
        P("labels"),
        P("groups", None),
        P("groups", None),
    )
    return jax.shard_map(
        per_device,
        mesh=mesh,
        in_specs=placed,
        out_specs=(P(("groups", "labels"), None), P("groups", None)),
        check_vma=False,
    )
```

```python
import functools
import math

import jax
import jax.numpy as jnp
from jax import lax
from jax.experimental import pallas as pl
from jax.experimental.pallas import tpu as pltpu
from jax.sharding import PartitionSpec as P

AXIS = "labels"
BF16 = jnp.bfloat16
F32 = jnp.float32
NT = (((1,), (1,)), ((), ()))
NN = (((1,), (0,)), ((), ()))
TN = (((0,), (0,)), ((), ()))
MIB = 1024 * 1024

OFF, ON = True, False


def dot(a, b, dims):
    return lax.dot_general(a, b, dims, preferred_element_type=F32)


def own_side(device, off):
    odd = device % 2
    return 1 - odd if off else odd


def partner_of(device, count, off):
    ahead = jnp.where(device == count - 1, 0, device + 1)
    behind = jnp.where(device == 0, count - 1, device - 1)
    return jnp.where(own_side(device, off) == 0, ahead, behind)


def own_list(lists, blocks, off):
    device = lax.axis_index(AXIS)
    side = own_side(device, off)
    return [lists[side, device * blocks + g] for g in range(blocks)]


def slots_of(lists, blocks, off):
    named = own_list(lists, blocks, off)
    least = functools.reduce(jnp.minimum, named)
    return [(value != least).astype(jnp.int32) for value in named]


def named_by_partner(lists, blocks, off):
    device = lax.axis_index(AXIS)
    partner = partner_of(device, lax.axis_size(AXIS), off)
    side = 1 - own_side(device, off)
    named = [lists[side, partner * blocks + g] for g in range(blocks)]
    return functools.reduce(jnp.minimum, named), functools.reduce(jnp.maximum, named)


def tile_side(off):
    return own_side(lax.axis_index(AXIS), off)


def block_rows(ref, index, block):
    return ref[pl.ds(pl.multiple_of(index * block, block), block), :]


def project_kernel(lists, queries, embeddings, out, left, right, table, sem, *, scale):
    rows, block = out.shape
    blocks = right.shape[0] // block
    fetches = [pltpu.make_async_copy(lists, table, sem.at[0]), pltpu.make_async_copy(queries, left, sem.at[1])]
    for g in range(blocks):
        place = pl.ds(g * block, block)
        fetches.append(pltpu.make_async_copy(embeddings.at[place, :], right.at[place, :], sem.at[2 + g]))
    for fetch in fetches:
        fetch.start()
    fetches[0].wait()
    first, _ = named_by_partner(table, blocks, OFF)
    fetches[1].wait()
    place = pl.ds(pl.multiple_of(first * block, block), block)
    pltpu.make_async_copy(embeddings.at[place, :], right.at[place, :], sem.at[2 + first]).wait()
    out[...] = (dot(left[...], right[place, :], NT) * scale).astype(BF16)
    for g in range(blocks):

        @pl.when(g != first)
        def _():
            fetches[2 + g].wait()


def spans_of(pieces, rows):
    spans = []
    begin = 0
    for piece in pieces:
        end = begin + piece.shape[0]
        for slot in range(2):
            low, high = max(begin, slot * rows), min(end, (slot + 1) * rows)
            if low < high:
                inside = slice(low - slot * rows, high - slot * rows)
                spans.append((piece, slice(low - begin, high - begin), slot, inside))
        begin = end
    return spans


def write_pieces(pieces, value):
    rows = sum(piece.shape[0] for piece in pieces) // 2
    for piece, place, slot, inside in spans_of(pieces, rows):
        piece[place, :] = value(slot, inside).astype(BF16)


def gather_pieces(pieces, whole):
    for piece, place, slot, inside in spans_of(pieces, whole.shape[1]):
        whole[slot, inside] = piece[place, :]


def own_kernel(lists, queries, embeddings, own, off, *on, scale):
    blocks, _, block = own.shape
    for g in range(blocks):
        own[g] = dot(queries[...], embeddings[g * block : (g + 1) * block, :], NT) * scale
    _, second = named_by_partner(lists, blocks, OFF)
    off[...] = own[second].astype(BF16)
    first, second = named_by_partner(lists, blocks, ON)
    write_pieces(on, lambda slot, rows: own[(first, second)[slot], rows])


def hits_kernel(positives, tiles, out, kept, sem):
    fetch = pltpu.make_async_copy(tiles, kept, sem)
    fetch.start()
    blocks, rows, block = out.shape
    first = lax.axis_index(AXIS) * blocks * block
    ids = lax.broadcasted_iota(jnp.int32, (rows, block), 1)
    columns = jnp.transpose(positives[...]) - first
    for g in range(blocks):
        hits = jnp.zeros((rows, block), jnp.bool_)
        for column in range(positives.shape[0]):
            hits = jnp.logical_or(hits, ids + g * block == columns[:, column : column + 1])
        out[g] = jnp.where(hits, 1.0, 0.0).astype(BF16)
    fetch.wait()


def base_kernel(lists, own, tiles, *rest):
    *pieces, out, received = rest
    gather_pieces(pieces, received)
    blocks = out.shape[0]
    side = tile_side(ON)
    for g, slot in enumerate(slots_of(lists, blocks, ON)):
        out[g] = own[g] + dot(received[slot], tiles[g, side], NT)


def signal_kernel(lists, base, hits, propensity, received, tiles, *rest, slot):
    signal, push, total = rest[-3:]
    blocks, _, block = base.shape
    side = tile_side(OFF)
    total[...] = jnp.zeros_like(total)
    for g, taken in enumerate(slots_of(lists, blocks, OFF)):

        @pl.when(taken == slot)
        def _():
            scores = base[g] + dot(received[...], tiles[g, side], NT)
            inverse = 1.0 / propensity[:, g * block : (g + 1) * block]
            value = (jax.nn.sigmoid(scores) - hits[g].astype(F32) * inverse).astype(BF16)
            signal[g] = value
            total[...] += dot(value, tiles[g, side], NN)

    push[...] = total[...].astype(BF16)


def push_kernel(lists, signal, tiles, *rest):
    *pieces, total = rest
    blocks = signal.shape[0]
    side = tile_side(ON)
    total[...] = jnp.zeros_like(total)
    for g, slot in enumerate(slots_of(lists, blocks, ON)):
        total[slot] += dot(signal[g], tiles[g, side], NN)
    write_pieces(pieces, lambda slot, rows: total[slot, rows])


def query_kernel(signal, embeddings, out):
    blocks, _, block = signal.shape
    total = dot(signal[0], embeddings[0:block, :], NN)
    for g in range(1, blocks):
        total += dot(signal[g], embeddings[g * block : (g + 1) * block, :], NN)
    out[...] = total


def query_half_kernel(lists, part, received, embeddings, out, *, blocks):
    first, _ = named_by_partner(lists, blocks, OFF)
    out[...] = part[...] + dot(received[...], block_rows(embeddings, first, received.shape[1]), NN)


def query_on_kernel(lists, part, embeddings, *rest, blocks):
    *pieces, out, received = rest
    gather_pieces(pieces, received)
    block = received.shape[2]
    first, second = named_by_partner(lists, blocks, ON)
    out[...] = (
        part[...]
        + dot(received[0], block_rows(embeddings, first, block), NN)
        + dot(received[1], block_rows(embeddings, second, block), NN)
    )


def query_end_kernel(lists, part, received, embeddings, after, out, *, blocks, own):
    del after
    _, second = named_by_partner(lists, blocks, OFF)
    rows = out.shape[0]
    core = lax.axis_index(AXIS) % 2
    half = core if own else 1 - core
    place = pl.ds(pl.multiple_of(half * rows, rows), rows)
    right = block_rows(embeddings, second, received.shape[1])
    out[...] = (part[place, :] + dot(received[place, :], right, NN)).astype(out.dtype)


def embed_kernel(lists, signal, on, off_a, queries, *rest, blocks, turn, scale):
    last = turn == blocks - 1
    off = [off_a]
    if last:
        off.append(rest[0])
        rest = rest[1:]
    if turn == 0:
        ready, token, total = rest
    else:
        before = rest[0]
        out, ready, token, total, sem = rest[-5:]
    rows, block = total.shape
    writes = []

    def write(source, index, slot):
        place = out.at[pl.ds(pl.multiple_of(index * block, block), block), :]
        writes.append(pltpu.make_async_copy(source, place, sem.at[slot]))
        writes[-1].start()

    named = named_by_partner(lists, blocks, ON) + named_by_partner(lists, blocks, OFF)
    g = (named[3] + 1 + turn) % blocks
    if turn > 0:
        write(before, (named[3] + turn) % blocks, 0)
    token[...] = jnp.zeros_like(token)
    total[...] = signal[g].astype(F32)
    for received, index in zip([on.at[0], on.at[1], *off], named):

        @pl.when(index == g)
        def _():
            total[...] += received[...].astype(F32)

    ready[...] = (dot(total[...].astype(BF16), queries[...], TN) * scale).astype(BF16)
    if last:
        write(ready, g, 1)
    for copy in writes:
        copy.wait()


VMEM = pl.BlockSpec(memory_space=pltpu.VMEM)
SMEM = pl.BlockSpec(memory_space=pltpu.SMEM)
ANY = pl.BlockSpec(memory_space=pl.ANY)
HBM = pl.BlockSpec(memory_space=pltpu.HBM)


def call(kernel, name, in_specs, out_shape, out_specs=None, scratch=(), aliases=None, vmem=12, flops=0):
    if out_specs is None:
        out_specs = jax.tree.map(lambda _: VMEM, out_shape)
    return pl.pallas_call(
        kernel,
        in_specs=in_specs,
        out_specs=out_specs,
        out_shape=out_shape,
        scratch_shapes=scratch,
        input_output_aliases=aliases or {},
        name=name,
        cost_estimate=pl.CostEstimate(flops=flops, bytes_accessed=0, transcendentals=0),
        compiler_params=pltpu.CompilerParams(vmem_limit_bytes=vmem * MIB),
    )


def exchange(value, mask):
    count = lax.axis_size(AXIS)
    return lax.ppermute(value, AXIS, [(i, i ^ mask) for i in range(count)])


def in_vmem(shape, dtype):
    return pltpu.VMEM(shape, dtype)


def digit_of(bit):
    return (lax.axis_index(AXIS) // bit) % 2


def halve_kernel(held, got, *outs):
    total = held[...] + got[...].astype(F32)
    rows = outs[0].shape[0]
    for chain, out in enumerate(outs):
        out[...] = total[chain * rows : (chain + 1) * rows, :].astype(BF16)


def add_kernel(held, got, *rest, scale):
    rest[-1][...] = ((held[...].astype(F32) + got[...].astype(F32)) * scale).astype(BF16)


def place_kernel(*refs, places):
    out, wide, sem = refs[-3:]
    rows = refs[0].shape[0]
    core = lax.axis_index(AXIS) % 2
    copies = []
    for k, (chain, own) in enumerate(places):
        wide[k] = refs[k][...].astype(F32)
        half = core if own else 1 - core
        begin = pl.multiple_of((2 * half + chain) * rows, rows)
        copies.append(pltpu.make_async_copy(wide.at[k], out.at[pl.ds(begin, rows), :], sem.at[k]))
        copies[-1].start()
    for copy in copies:
        copy.wait()


def sum_queries(kept, sent, beside, scale):
    count = lax.axis_size(AXIS)
    rows, width = kept.shape
    got = exchange(sent, 1)
    if count & (count - 1) or count < 8:
        half = kept + got.astype(F32)
        half = lax.psum(half, AXIS, axis_index_groups=[list(range(c, count, 2)) for c in range(2)])
        both = jnp.stack([half, exchange(half, 1)])
        both = jnp.where(lax.axis_index(AXIS) % 2 == 0, both, both[::-1])
        return both.reshape(2 * rows, width) * scale
    bits = [1 << k for k in range(1, count.bit_length() - 1)]
    orders = [bits, bits[-1:] + bits[:-1]]
    piece = in_vmem((rows // 2, width), BF16)
    held = list(call(halve_kernel, "halve", [VMEM] * 2, [piece, piece])(kept, got))
    swapped = []
    for k in range(len(bits)):
        last = k == len(bits) - 1
        got = [exchange(value, order[k]) for value, order in zip(held, orders)]
        for chain in range(2):
            after = beside[k : k + 1] if chain == 0 else held[:1] if last else []
            held[chain] = call(
                functools.partial(add_kernel, scale=scale if last else 1.0),
                "add",
                [VMEM] * 2 + [ANY] * len(after),
                piece,
                flops=2 * 10**8 if last else 0,
            )(held[chain], got[chain], *after)
    swapped = [exchange(value, 1) for value in held]

    def place(values, places, *begun):
        return call(
            functools.partial(place_kernel, places=places),
            "place",
            [VMEM] * len(values) + [ANY] * len(begun),
            jax.ShapeDtypeStruct((2 * rows, width), F32),
            out_specs=ANY,
            scratch=[
                pltpu.VMEM((len(values), rows // 2, width), F32),
                pltpu.SemaphoreType.DMA((len(values),)),
            ],
            aliases={len(values): 0} if begun else None,
        )(*values, *begun)

    early = place(held, [(0, True), (1, True)])
    return place(swapped, [(0, False), (1, False)], early)


def per_device(embeddings, edge_tiles, neighbour, propensity, queries, positives):
    count = lax.axis_size(AXIS)
    blocks, _, block, _ = edge_tiles.shape
    labels_dev, width = embeddings.shape
    rows = queries.shape[0]
    lists = neighbour.T
    odd = range(1, count, 2)
    off_route = [(i, (i + 1) % count) for i in odd] + [((i + 1) % count, i) for i in odd]

    def off_swap(value):
        return lax.ppermute(value, AXIS, off_route)

    def on_swap(value):
        return exchange(value, 1)

    one = in_vmem((rows, block), BF16)
    pair = in_vmem((2, rows, block), BF16)
    third = -(-2 * rows // 48) * 16
    thirds = [in_vmem((size, block), BF16) for size in (third, third, 2 * rows - 2 * third)]
    full = (blocks, rows, block)
    scale = 1.0 / math.sqrt(width)

    off_a, queries, embeddings, lists = call(
        functools.partial(project_kernel, scale=scale),
        "project",
        [HBM] * 3,
        [
            one,
            in_vmem(queries.shape, BF16),
            in_vmem(embeddings.shape, BF16),
            pltpu.SMEM(lists.shape, jnp.int32),
        ],
        out_specs=[VMEM] * 3 + [SMEM],
        scratch=[pltpu.SemaphoreType.DMA((2 + blocks,))],
    )(*(pltpu.with_memory_space_constraint(x, pltpu.HBM) for x in (lists, queries, embeddings)))
    from_off_a = off_swap(off_a)
    own, off_b, *for_on = call(
        functools.partial(own_kernel, scale=scale),
        "own",
        [SMEM, VMEM, VMEM],
        [in_vmem(full, F32), one] + thirds,
    )(lists, queries, embeddings)
    from_on = [on_swap(piece) for piece in for_on]
    hits, tiles = call(
        hits_kernel,
        "hits",
        [VMEM, HBM],
        [in_vmem(full, BF16), in_vmem(edge_tiles.shape, BF16)],
        scratch=[pltpu.SemaphoreType.DMA],
    )(positives.T, pltpu.with_memory_space_constraint(edge_tiles, pltpu.HBM))
    from_off_b = off_swap(off_b)
    base = call(
        base_kernel,
        "base",
        [SMEM] + [VMEM] * 5,
        in_vmem(full, F32),
        scratch=[pltpu.VMEM((2, rows, block), BF16)],
    )(lists, own, tiles, *from_on)
    propensity = propensity.reshape(1, labels_dev)

    def signal_of(received, slot, *begun):
        return call(
            functools.partial(signal_kernel, slot=slot),
            "signal",
            [SMEM] + [VMEM] * (5 + len(begun)),
            [in_vmem(full, BF16), one],
            scratch=[pltpu.VMEM((rows, block), F32)],
            aliases={6: 0} if begun else None,
            flops=0 if begun else 2 * 10**9,
        )(lists, base, hits, propensity, received, tiles, *begun)

    signal, push_a = signal_of(from_off_a, 0)
    back_a = off_swap(push_a)
    signal, push_b = signal_of(from_off_b, 1, signal)
    back_b = off_swap(push_b)
    push_on = call(
        push_kernel,
        "push",
        [SMEM, VMEM, VMEM],
        thirds,
        scratch=[pltpu.VMEM((2, rows, block), F32)],
    )(lists, signal, tiles)
    back_on = [on_swap(piece) for piece in push_on]

    whole = in_vmem((rows, width), F32)
    part = call(query_kernel, "query", [VMEM] * 2, whole)(signal, embeddings)
    part = call(
        functools.partial(query_half_kernel, blocks=blocks),
        "query_half",
        [SMEM] + [VMEM] * 3,
        whole,
        flops=10**9,
    )(lists, part, back_a, embeddings)
    part, on = call(
        functools.partial(query_on_kernel, blocks=blocks), "query_on", [SMEM] + [VMEM] * 5, [whole, pair]
    )(lists, part, embeddings, *back_on)
    ready = in_vmem((block, width), BF16)
    written = jax.ShapeDtypeStruct((labels_dev, width), BF16)

    def embed(turn, outs):
        values = [lists, signal, on, back_a, queries] + ([back_b] if turn == blocks - 1 else []) + outs[::-1]
        return call(
            functools.partial(embed_kernel, blocks=blocks, turn=turn, scale=1.0 / math.sqrt(rows)),
            "embed",
            [SMEM] + [VMEM] * (len(values) - 1 - (turn > 1)) + [ANY] * (turn > 1),
            ([written] if turn else []) + [ready, in_vmem((8, 128), F32)],
            out_specs=([ANY] if turn else []) + [VMEM] * 2,
            scratch=[pltpu.VMEM((rows, block), F32)] + ([pltpu.SemaphoreType.DMA((2,))] if turn else []),
            aliases={len(values) - 1: 0} if turn > 1 else None,
        )(*values)

    *outs, token = embed(0, [])
    tokens = [token]

    def query_end(own, kind):
        return call(
            functools.partial(query_end_kernel, blocks=blocks, own=own),
            "query_end",
            [SMEM] + [VMEM] * 3 + [ANY],
            in_vmem((rows // 2, width), kind),
        )(lists, part, back_b, embeddings, tokens[0])

    sent, kept = query_end(False, BF16), query_end(True, F32)
    for turn in range(1, blocks):
        *outs, token = embed(turn, outs)
        tokens.append(token)
    grad_embed = outs[0]
    grad_queries = sum_queries(kept, sent, tokens[1:], 1.0 / math.sqrt(labels_dev * count))
    return (grad_embed, grad_queries)


def solution(mesh):
    placed = (
        P("labels", None),
        P("labels", None, None, None),
        P(),
        P("labels"),
        P("groups", None),
        P("groups", None),
    )
    return jax.shard_map(
        per_device,
        mesh=mesh,
        in_specs=placed,
        out_specs=(P(("groups", "labels"), None), P("groups", None)),
        check_vma=False,
    )
```

```python
import functools
import math

import jax
import jax.numpy as jnp
from jax import lax
from jax.experimental import pallas as pl
from jax.experimental.pallas import tpu as pltpu
from jax.sharding import PartitionSpec as P

AXIS = "labels"
BF16 = jnp.bfloat16
F32 = jnp.float32
NT = (((1,), (1,)), ((), ()))
NN = (((1,), (0,)), ((), ()))
TN = (((0,), (0,)), ((), ()))
MIB = 1024 * 1024

OFF, ON = True, False


def dot(a, b, dims):
    return lax.dot_general(a, b, dims, preferred_element_type=F32)


def own_side(device, off):
    odd = device % 2
    return 1 - odd if off else odd


def partner_of(device, count, off):
    ahead = jnp.where(device == count - 1, 0, device + 1)
    behind = jnp.where(device == 0, count - 1, device - 1)
    return jnp.where(own_side(device, off) == 0, ahead, behind)


def own_list(lists, blocks, off):
    device = lax.axis_index(AXIS)
    side = own_side(device, off)
    return [lists[side, device * blocks + g] for g in range(blocks)]


def slots_of(lists, blocks, off):
    named = own_list(lists, blocks, off)
    least = functools.reduce(jnp.minimum, named)
    return [(value != least).astype(jnp.int32) for value in named]


def named_by_partner(lists, blocks, off):
    device = lax.axis_index(AXIS)
    partner = partner_of(device, lax.axis_size(AXIS), off)
    side = 1 - own_side(device, off)
    named = [lists[side, partner * blocks + g] for g in range(blocks)]
    return functools.reduce(jnp.minimum, named), functools.reduce(jnp.maximum, named)


def tile_side(off):
    return own_side(lax.axis_index(AXIS), off)


def block_rows(ref, index, block):
    return ref[pl.ds(pl.multiple_of(index * block, block), block), :]


def project_kernel(lists, queries, embeddings, out, left, right, table, sem, *, scale):
    rows, block = out.shape
    blocks = right.shape[0] // block
    fetches = [pltpu.make_async_copy(lists, table, sem.at[0]), pltpu.make_async_copy(queries, left, sem.at[1])]
    for g in range(blocks):
        place = pl.ds(g * block, block)
        fetches.append(pltpu.make_async_copy(embeddings.at[place, :], right.at[place, :], sem.at[2 + g]))
    for fetch in fetches:
        fetch.start()
    fetches[0].wait()
    first, _ = named_by_partner(table, blocks, OFF)
    fetches[1].wait()
    place = pl.ds(pl.multiple_of(first * block, block), block)
    pltpu.make_async_copy(embeddings.at[place, :], right.at[place, :], sem.at[2 + first]).wait()
    out[...] = (dot(left[...], right[place, :], NT) * scale).astype(BF16)
    for g in range(blocks):

        @pl.when(g != first)
        def _():
            fetches[2 + g].wait()


def spans_of(pieces, rows):
    spans = []
    begin = 0
    for piece in pieces:
        end = begin + piece.shape[0]
        for slot in range(2):
            low, high = max(begin, slot * rows), min(end, (slot + 1) * rows)
            if low < high:
                inside = slice(low - slot * rows, high - slot * rows)
                spans.append((piece, slice(low - begin, high - begin), slot, inside))
        begin = end
    return spans


def write_pieces(pieces, value):
    rows = sum(piece.shape[0] for piece in pieces) // 2
    for piece, place, slot, inside in spans_of(pieces, rows):
        piece[place, :] = value(slot, inside).astype(BF16)


def gather_pieces(pieces, whole):
    for piece, place, slot, inside in spans_of(pieces, whole.shape[1]):
        whole[slot, inside] = piece[place, :]


def own_kernel(lists, queries, embeddings, own, off, *on, scale):
    blocks, _, block = own.shape
    for g in range(blocks):
        own[g] = dot(queries[...], embeddings[g * block : (g + 1) * block, :], NT) * scale
    _, second = named_by_partner(lists, blocks, OFF)
    off[...] = own[second].astype(BF16)
    first, second = named_by_partner(lists, blocks, ON)
    write_pieces(on, lambda slot, rows: own[(first, second)[slot], rows])


def hits_kernel(positives, tiles, out, kept, sem):
    fetch = pltpu.make_async_copy(tiles, kept, sem)
    fetch.start()
    blocks, rows, block = out.shape
    first = lax.axis_index(AXIS) * blocks * block
    ids = lax.broadcasted_iota(jnp.int32, (rows, block), 1)
    columns = jnp.transpose(positives[...]) - first
    for g in range(blocks):
        hits = jnp.zeros((rows, block), jnp.bool_)
        for column in range(positives.shape[0]):
            hits = jnp.logical_or(hits, ids + g * block == columns[:, column : column + 1])
        out[g] = jnp.where(hits, 1.0, 0.0).astype(BF16)
    fetch.wait()


def base_kernel(lists, own, tiles, *rest):
    *pieces, out, received = rest
    gather_pieces(pieces, received)
    blocks = out.shape[0]
    side = tile_side(ON)
    for g, slot in enumerate(slots_of(lists, blocks, ON)):
        out[g] = own[g] + dot(received[slot], tiles[g, side], NT)


def signal_kernel(lists, base, hits, propensity, received, tiles, *rest, slot):
    signal, push, total = rest[-3:]
    blocks, _, block = base.shape
    side = tile_side(OFF)
    total[...] = jnp.zeros_like(total)
    for g, taken in enumerate(slots_of(lists, blocks, OFF)):

        @pl.when(taken == slot)
        def _():
            scores = base[g] + dot(received[...], tiles[g, side], NT)
            inverse = 1.0 / propensity[:, g * block : (g + 1) * block]
            value = (jax.nn.sigmoid(scores) - hits[g].astype(F32) * inverse).astype(BF16)
            signal[g] = value
            total[...] += dot(value, tiles[g, side], NN)

    push[...] = total[...].astype(BF16)


def push_kernel(lists, signal, tiles, *rest):
    *pieces, total = rest
    blocks = signal.shape[0]
    side = tile_side(ON)
    total[...] = jnp.zeros_like(total)
    for g, slot in enumerate(slots_of(lists, blocks, ON)):
        total[slot] += dot(signal[g], tiles[g, side], NN)
    write_pieces(pieces, lambda slot, rows: total[slot, rows])


def query_kernel(signal, embeddings, out):
    blocks, _, block = signal.shape
    total = dot(signal[0], embeddings[0:block, :], NN)
    for g in range(1, blocks):
        total += dot(signal[g], embeddings[g * block : (g + 1) * block, :], NN)
    out[...] = total


def query_half_kernel(lists, part, received, embeddings, out, *, blocks):
    first, _ = named_by_partner(lists, blocks, OFF)
    out[...] = part[...] + dot(received[...], block_rows(embeddings, first, received.shape[1]), NN)


def query_on_kernel(lists, part, embeddings, *rest, blocks):
    *pieces, out, received = rest
    gather_pieces(pieces, received)
    block = received.shape[2]
    first, second = named_by_partner(lists, blocks, ON)
    out[...] = (
        part[...]
        + dot(received[0], block_rows(embeddings, first, block), NN)
        + dot(received[1], block_rows(embeddings, second, block), NN)
    )


def query_end_kernel(lists, part, received, embeddings, after, out, *, blocks, own):
    del after
    _, second = named_by_partner(lists, blocks, OFF)
    rows = out.shape[0]
    core = lax.axis_index(AXIS) % 2
    half = core if own else 1 - core
    place = pl.ds(pl.multiple_of(half * rows, rows), rows)
    right = block_rows(embeddings, second, received.shape[1])
    out[...] = (part[place, :] + dot(received[place, :], right, NN)).astype(out.dtype)


def embed_kernel(lists, signal, on, off_a, queries, *rest, blocks, turn, scale):
    last = turn == blocks - 1
    off = [off_a]
    if last:
        off.append(rest[0])
        rest = rest[1:]
    if turn == 0:
        ready, token, total = rest
    else:
        before = rest[0]
        out, ready, token, total, sem = rest[-5:]
    rows, block = total.shape
    writes = []

    def write(source, index, slot):
        place = out.at[pl.ds(pl.multiple_of(index * block, block), block), :]
        writes.append(pltpu.make_async_copy(source, place, sem.at[slot]))
        writes[-1].start()

    named = named_by_partner(lists, blocks, ON) + named_by_partner(lists, blocks, OFF)
    g = (named[3] + 1 + turn) % blocks
    if turn > 0:
        write(before, (named[3] + turn) % blocks, 0)
    token[...] = jnp.zeros_like(token)
    total[...] = signal[g].astype(F32)
    for received, index in zip([on.at[0], on.at[1], *off], named):

        @pl.when(index == g)
        def _():
            total[...] += received[...].astype(F32)

    ready[...] = (dot(total[...].astype(BF16), queries[...], TN) * scale).astype(BF16)
    if last:
        write(ready, g, 1)
    for copy in writes:
        copy.wait()


VMEM = pl.BlockSpec(memory_space=pltpu.VMEM)
SMEM = pl.BlockSpec(memory_space=pltpu.SMEM)
ANY = pl.BlockSpec(memory_space=pl.ANY)
HBM = pl.BlockSpec(memory_space=pltpu.HBM)


def call(kernel, name, in_specs, out_shape, out_specs=None, scratch=(), aliases=None, vmem=12, flops=0):
    if out_specs is None:
        out_specs = jax.tree.map(lambda _: VMEM, out_shape)
    return pl.pallas_call(
        kernel,
        in_specs=in_specs,
        out_specs=out_specs,
        out_shape=out_shape,
        scratch_shapes=scratch,
        input_output_aliases=aliases or {},
        name=name,
        cost_estimate=pl.CostEstimate(flops=flops, bytes_accessed=0, transcendentals=0),
        compiler_params=pltpu.CompilerParams(vmem_limit_bytes=vmem * MIB),
    )


def exchange(value, mask):
    count = lax.axis_size(AXIS)
    return lax.ppermute(value, AXIS, [(i, i ^ mask) for i in range(count)])


def in_vmem(shape, dtype):
    return pltpu.VMEM(shape, dtype)


def digit_of(bit):
    return (lax.axis_index(AXIS) // bit) % 2


def halve_kernel(held, got, *outs):
    total = held[...] + got[...].astype(F32)
    rows = outs[0].shape[0]
    for chain, out in enumerate(outs):
        out[...] = total[chain * rows : (chain + 1) * rows, :].astype(BF16)


def add_kernel(held, got, *rest, scale):
    rest[-1][...] = ((held[...].astype(F32) + got[...].astype(F32)) * scale).astype(BF16)


def end_kernel(held, got, before, out, *, scale):
    rows = held.shape[0]
    out[:rows, :] = before[...]
    out[rows:, :] = ((held[...].astype(F32) + got[...].astype(F32)) * scale).astype(BF16)


def place_kernel(held, *rest, own):
    out, wide, sem = rest[-3:]
    rows = held.shape[0]
    core = lax.axis_index(AXIS) % 2
    half = core if own else 1 - core
    wide[...] = held[...].astype(F32)
    copy = pltpu.make_async_copy(wide, out.at[pl.ds(pl.multiple_of(half * rows, rows), rows), :], sem)
    copy.start()
    copy.wait()


def sum_queries(kept, sent, beside, scale):
    count = lax.axis_size(AXIS)
    rows, width = kept.shape
    got = exchange(sent, 1)
    if count & (count - 1) or count < 8:
        half = kept + got.astype(F32)
        half = lax.psum(half, AXIS, axis_index_groups=[list(range(c, count, 2)) for c in range(2)])
        both = jnp.stack([half, exchange(half, 1)])
        both = jnp.where(lax.axis_index(AXIS) % 2 == 0, both, both[::-1])
        return both.reshape(2 * rows, width) * scale
    bits = [1 << k for k in range(1, count.bit_length() - 1)]
    orders = [bits, bits[-1:] + bits[:-1]]
    piece = in_vmem((rows // 2, width), BF16)
    held = list(call(halve_kernel, "halve", [VMEM] * 2, [piece, piece])(kept, got))
    swapped = []
    for k in range(len(bits)):
        last = k == len(bits) - 1
        got = [exchange(value, order[k]) for value, order in zip(held, orders)]
        for chain in range(2 - last):
            after = beside[k : k + 1] if chain == 0 else []
            held[chain] = call(
                functools.partial(add_kernel, scale=scale if last else 1.0),
                "add",
                [VMEM] * 2 + [ANY] * len(after),
                piece,
                flops=2 * 10**8 if last else 0,
            )(held[chain], got[chain], *after)
    mine = call(
        functools.partial(end_kernel, scale=scale),
        "end",
        [VMEM] * 3,
        in_vmem((rows, width), BF16),
        flops=2 * 10**8,
    )(held[1], got[1], held[0])
    other = exchange(mine, 1)

    def place(half, own, *begun):
        return call(
            functools.partial(place_kernel, own=own),
            "place",
            [VMEM] + [ANY] * len(begun),
            jax.ShapeDtypeStruct((2 * rows, width), F32),
            out_specs=ANY,
            scratch=[pltpu.VMEM((rows, width), F32), pltpu.SemaphoreType.DMA],
            aliases={1: 0} if begun else None,
        )(half, *begun)

    return place(other, False, place(mine, True))


def per_device(embeddings, edge_tiles, neighbour, propensity, queries, positives):
    count = lax.axis_size(AXIS)
    blocks, _, block, _ = edge_tiles.shape
    labels_dev, width = embeddings.shape
    rows = queries.shape[0]
    lists = neighbour.T
    odd = range(1, count, 2)
    off_route = [(i, (i + 1) % count) for i in odd] + [((i + 1) % count, i) for i in odd]

    def off_swap(value):
        return lax.ppermute(value, AXIS, off_route)

    def on_swap(value):
        return exchange(value, 1)

    one = in_vmem((rows, block), BF16)
    pair = in_vmem((2, rows, block), BF16)
    third = -(-2 * rows // 48) * 16
    thirds = [in_vmem((size, block), BF16) for size in (third, third, 2 * rows - 2 * third)]
    full = (blocks, rows, block)
    scale = 1.0 / math.sqrt(width)

    off_a, queries, embeddings, lists = call(
        functools.partial(project_kernel, scale=scale),
        "project",
        [HBM] * 3,
        [
            one,
            in_vmem(queries.shape, BF16),
            in_vmem(embeddings.shape, BF16),
            pltpu.SMEM(lists.shape, jnp.int32),
        ],
        out_specs=[VMEM] * 3 + [SMEM],
        scratch=[pltpu.SemaphoreType.DMA((2 + blocks,))],
    )(*(pltpu.with_memory_space_constraint(x, pltpu.HBM) for x in (lists, queries, embeddings)))
    from_off_a = off_swap(off_a)
    own, off_b, *for_on = call(
        functools.partial(own_kernel, scale=scale),
        "own",
        [SMEM, VMEM, VMEM],
        [in_vmem(full, F32), one] + thirds,
    )(lists, queries, embeddings)
    from_on = [on_swap(piece) for piece in for_on]
    hits, tiles = call(
        hits_kernel,
        "hits",
        [VMEM, HBM],
        [in_vmem(full, BF16), in_vmem(edge_tiles.shape, BF16)],
        scratch=[pltpu.SemaphoreType.DMA],
    )(positives.T, pltpu.with_memory_space_constraint(edge_tiles, pltpu.HBM))
    from_off_b = off_swap(off_b)
    base = call(
        base_kernel,
        "base",
        [SMEM] + [VMEM] * 5,
        in_vmem(full, F32),
        scratch=[pltpu.VMEM((2, rows, block), BF16)],
    )(lists, own, tiles, *from_on)
    propensity = propensity.reshape(1, labels_dev)

    def signal_of(received, slot, *begun):
        return call(
            functools.partial(signal_kernel, slot=slot),
            "signal",
            [SMEM] + [VMEM] * (5 + len(begun)),
            [in_vmem(full, BF16), one],
            scratch=[pltpu.VMEM((rows, block), F32)],
            aliases={6: 0} if begun else None,
            flops=0 if begun else 2 * 10**9,
        )(lists, base, hits, propensity, received, tiles, *begun)

    signal, push_a = signal_of(from_off_a, 0)
    back_a = off_swap(push_a)
    signal, push_b = signal_of(from_off_b, 1, signal)
    back_b = off_swap(push_b)
    push_on = call(
        push_kernel,
        "push",
        [SMEM, VMEM, VMEM],
        thirds,
        scratch=[pltpu.VMEM((2, rows, block), F32)],
    )(lists, signal, tiles)
    back_on = [on_swap(piece) for piece in push_on]

    whole = in_vmem((rows, width), F32)
    part = call(query_kernel, "query", [VMEM] * 2, whole)(signal, embeddings)
    part = call(
        functools.partial(query_half_kernel, blocks=blocks),
        "query_half",
        [SMEM] + [VMEM] * 3,
        whole,
        flops=10**9,
    )(lists, part, back_a, embeddings)
    part, on = call(
        functools.partial(query_on_kernel, blocks=blocks), "query_on", [SMEM] + [VMEM] * 5, [whole, pair]
    )(lists, part, embeddings, *back_on)
    ready = in_vmem((block, width), BF16)
    written = jax.ShapeDtypeStruct((labels_dev, width), BF16)

    def embed(turn, outs):
        values = [lists, signal, on, back_a, queries] + ([back_b] if turn == blocks - 1 else []) + outs[::-1]
        return call(
            functools.partial(embed_kernel, blocks=blocks, turn=turn, scale=1.0 / math.sqrt(rows)),
            "embed",
            [SMEM] + [VMEM] * (len(values) - 1 - (turn > 1)) + [ANY] * (turn > 1),
            ([written] if turn else []) + [ready, in_vmem((8, 128), F32)],
            out_specs=([ANY] if turn else []) + [VMEM] * 2,
            scratch=[pltpu.VMEM((rows, block), F32)] + ([pltpu.SemaphoreType.DMA((2,))] if turn else []),
            aliases={len(values) - 1: 0} if turn > 1 else None,
        )(*values)

    *outs, token = embed(0, [])
    tokens = [token]

    def query_end(own, kind):
        return call(
            functools.partial(query_end_kernel, blocks=blocks, own=own),
            "query_end",
            [SMEM] + [VMEM] * 3 + [ANY],
            in_vmem((rows // 2, width), kind),
        )(lists, part, back_b, embeddings, tokens[0])

    sent, kept = query_end(False, BF16), query_end(True, F32)
    for turn in range(1, blocks):
        *outs, token = embed(turn, outs)
        tokens.append(token)
    grad_embed = outs[0]
    grad_queries = sum_queries(kept, sent, tokens[1:], 1.0 / math.sqrt(labels_dev * count))
    return (grad_embed, grad_queries)


def solution(mesh):
    placed = (
        P("labels", None),
        P("labels", None, None, None),
        P(),
        P("labels"),
        P("groups", None),
        P("groups", None),
    )
    return jax.shard_map(
        per_device,
        mesh=mesh,
        in_specs=placed,
        out_specs=(P(("groups", "labels"), None), P("groups", None)),
        check_vma=False,
    )
```

```python
import functools
import math

import jax
import jax.numpy as jnp
from jax import lax
from jax.experimental import pallas as pl
from jax.experimental.pallas import tpu as pltpu
from jax.sharding import PartitionSpec as P

AXIS = "labels"
BF16 = jnp.bfloat16
F32 = jnp.float32
NT = (((1,), (1,)), ((), ()))
NN = (((1,), (0,)), ((), ()))
TN = (((0,), (0,)), ((), ()))
MIB = 1024 * 1024

OFF, ON = True, False


def dot(a, b, dims):
    return lax.dot_general(a, b, dims, preferred_element_type=F32)


def own_side(device, off):
    odd = device % 2
    return 1 - odd if off else odd


def partner_of(device, count, off):
    ahead = jnp.where(device == count - 1, 0, device + 1)
    behind = jnp.where(device == 0, count - 1, device - 1)
    return jnp.where(own_side(device, off) == 0, ahead, behind)


def own_list(lists, blocks, off):
    device = lax.axis_index(AXIS)
    side = own_side(device, off)
    return [lists[side, device * blocks + g] for g in range(blocks)]


def slots_of(lists, blocks, off):
    named = own_list(lists, blocks, off)
    least = functools.reduce(jnp.minimum, named)
    return [(value != least).astype(jnp.int32) for value in named]


def named_by_partner(lists, blocks, off):
    device = lax.axis_index(AXIS)
    partner = partner_of(device, lax.axis_size(AXIS), off)
    side = 1 - own_side(device, off)
    named = [lists[side, partner * blocks + g] for g in range(blocks)]
    return functools.reduce(jnp.minimum, named), functools.reduce(jnp.maximum, named)


def tile_side(off):
    return own_side(lax.axis_index(AXIS), off)


def block_rows(ref, index, block):
    return ref[pl.ds(pl.multiple_of(index * block, block), block), :]


def project_kernel(lists, queries, embeddings, out, left, right, table, sem, *, scale):
    rows, block = out.shape
    blocks = right.shape[0] // block
    fetches = [pltpu.make_async_copy(lists, table, sem.at[0]), pltpu.make_async_copy(queries, left, sem.at[1])]
    for g in range(blocks):
        place = pl.ds(g * block, block)
        fetches.append(pltpu.make_async_copy(embeddings.at[place, :], right.at[place, :], sem.at[2 + g]))
    for fetch in fetches:
        fetch.start()
    fetches[0].wait()
    first, _ = named_by_partner(table, blocks, OFF)
    fetches[1].wait()
    place = pl.ds(pl.multiple_of(first * block, block), block)
    pltpu.make_async_copy(embeddings.at[place, :], right.at[place, :], sem.at[2 + first]).wait()
    out[...] = (dot(left[...], right[place, :], NT) * scale).astype(BF16)
    for g in range(blocks):

        @pl.when(g != first)
        def _():
            fetches[2 + g].wait()


def spans_of(pieces, rows):
    spans = []
    begin = 0
    for piece in pieces:
        end = begin + piece.shape[0]
        for slot in range(2):
            low, high = max(begin, slot * rows), min(end, (slot + 1) * rows)
            if low < high:
                inside = slice(low - slot * rows, high - slot * rows)
                spans.append((piece, slice(low - begin, high - begin), slot, inside))
        begin = end
    return spans


def write_pieces(pieces, value):
    rows = sum(piece.shape[0] for piece in pieces) // 2
    for piece, place, slot, inside in spans_of(pieces, rows):
        piece[place, :] = value(slot, inside).astype(BF16)


def gather_pieces(pieces, whole):
    for piece, place, slot, inside in spans_of(pieces, whole.shape[1]):
        whole[slot, inside] = piece[place, :]


def own_kernel(lists, queries, embeddings, own, off, *on, scale):
    blocks, _, block = own.shape
    for g in range(blocks):
        own[g] = dot(queries[...], embeddings[g * block : (g + 1) * block, :], NT) * scale
    _, second = named_by_partner(lists, blocks, OFF)
    off[...] = own[second].astype(BF16)
    first, second = named_by_partner(lists, blocks, ON)
    write_pieces(on, lambda slot, rows: own[(first, second)[slot], rows])


def hits_kernel(positives, tiles, out, kept, sem):
    fetch = pltpu.make_async_copy(tiles, kept, sem)
    fetch.start()
    blocks, rows, block = out.shape
    first = lax.axis_index(AXIS) * blocks * block
    ids = lax.broadcasted_iota(jnp.int32, (rows, block), 1)
    columns = jnp.transpose(positives[...]) - first
    for g in range(blocks):
        hits = jnp.zeros((rows, block), jnp.bool_)
        for column in range(positives.shape[0]):
            hits = jnp.logical_or(hits, ids + g * block == columns[:, column : column + 1])
        out[g] = jnp.where(hits, 1.0, 0.0).astype(BF16)
    fetch.wait()


def base_kernel(lists, own, tiles, *rest):
    *pieces, out, received = rest
    gather_pieces(pieces, received)
    blocks = out.shape[0]
    side = tile_side(ON)
    for g, slot in enumerate(slots_of(lists, blocks, ON)):
        out[g] = own[g] + dot(received[slot], tiles[g, side], NT)


def signal_kernel(lists, base, hits, propensity, received, tiles, *rest, slot):
    signal, push, total = rest[-3:]
    blocks, _, block = base.shape
    side = tile_side(OFF)
    total[...] = jnp.zeros_like(total)
    for g, taken in enumerate(slots_of(lists, blocks, OFF)):

        @pl.when(taken == slot)
        def _():
            scores = base[g] + dot(received[...], tiles[g, side], NT)
            inverse = 1.0 / propensity[:, g * block : (g + 1) * block]
            value = (jax.nn.sigmoid(scores) - hits[g].astype(F32) * inverse).astype(BF16)
            signal[g] = value
            total[...] += dot(value, tiles[g, side], NN)

    push[...] = total[...].astype(BF16)


def push_kernel(lists, signal, tiles, *rest):
    *pieces, total = rest
    blocks = signal.shape[0]
    side = tile_side(ON)
    total[...] = jnp.zeros_like(total)
    for g, slot in enumerate(slots_of(lists, blocks, ON)):
        total[slot] += dot(signal[g], tiles[g, side], NN)
    write_pieces(pieces, lambda slot, rows: total[slot, rows])


def query_kernel(signal, embeddings, out):
    blocks, _, block = signal.shape
    total = dot(signal[0], embeddings[0:block, :], NN)
    for g in range(1, blocks):
        total += dot(signal[g], embeddings[g * block : (g + 1) * block, :], NN)
    out[...] = total


def query_half_kernel(lists, part, received, embeddings, out, *, blocks):
    first, _ = named_by_partner(lists, blocks, OFF)
    out[...] = part[...] + dot(received[...], block_rows(embeddings, first, received.shape[1]), NN)


def query_on_kernel(lists, part, embeddings, *rest, blocks):
    *pieces, out, received = rest
    gather_pieces(pieces, received)
    block = received.shape[2]
    first, second = named_by_partner(lists, blocks, ON)
    out[...] = (
        part[...]
        + dot(received[0], block_rows(embeddings, first, block), NN)
        + dot(received[1], block_rows(embeddings, second, block), NN)
    )


def query_end_kernel(lists, part, received, embeddings, after, out, *, blocks, own):
    del after
    _, second = named_by_partner(lists, blocks, OFF)
    rows = out.shape[0]
    core = lax.axis_index(AXIS) % 2
    half = core if own else 1 - core
    place = pl.ds(pl.multiple_of(half * rows, rows), rows)
    right = block_rows(embeddings, second, received.shape[1])
    out[...] = (part[place, :] + dot(received[place, :], right, NN)).astype(out.dtype)


def embed_kernel(lists, signal, on, off_a, queries, *rest, blocks, turn, scale):
    last = turn == blocks - 1
    off = [off_a]
    if last:
        off.append(rest[0])
        rest = rest[1:]
    if turn == 0:
        ready, token, total = rest
    else:
        before = rest[0]
        out, ready, token, total, sem = rest[-5:]
    rows, block = total.shape
    writes = []

    def write(source, index, slot):
        place = out.at[pl.ds(pl.multiple_of(index * block, block), block), :]
        writes.append(pltpu.make_async_copy(source, place, sem.at[slot]))
        writes[-1].start()

    named = named_by_partner(lists, blocks, ON) + named_by_partner(lists, blocks, OFF)
    g = (named[3] + 1 + turn) % blocks
    if turn > 0:
        write(before, (named[3] + turn) % blocks, 0)
    token[...] = jnp.zeros_like(token)
    total[...] = signal[g].astype(F32)
    for received, index in zip([on.at[0], on.at[1], *off], named):

        @pl.when(index == g)
        def _():
            total[...] += received[...].astype(F32)

    ready[...] = (dot(total[...].astype(BF16), queries[...], TN) * scale).astype(BF16)
    if last:
        write(ready, g, 1)
    for copy in writes:
        copy.wait()


VMEM = pl.BlockSpec(memory_space=pltpu.VMEM)
SMEM = pl.BlockSpec(memory_space=pltpu.SMEM)
ANY = pl.BlockSpec(memory_space=pl.ANY)
HBM = pl.BlockSpec(memory_space=pltpu.HBM)


def call(kernel, name, in_specs, out_shape, out_specs=None, scratch=(), aliases=None, vmem=12, flops=0):
    if out_specs is None:
        out_specs = jax.tree.map(lambda _: VMEM, out_shape)
    return pl.pallas_call(
        kernel,
        in_specs=in_specs,
        out_specs=out_specs,
        out_shape=out_shape,
        scratch_shapes=scratch,
        input_output_aliases=aliases or {},
        name=name,
        cost_estimate=pl.CostEstimate(flops=flops, bytes_accessed=0, transcendentals=0),
        compiler_params=pltpu.CompilerParams(vmem_limit_bytes=vmem * MIB),
    )


def exchange(value, mask):
    count = lax.axis_size(AXIS)
    return lax.ppermute(value, AXIS, [(i, i ^ mask) for i in range(count)])


def in_vmem(shape, dtype):
    return pltpu.VMEM(shape, dtype)


def digit_of(bit):
    return (lax.axis_index(AXIS) // bit) % 2


def halve_kernel(held, got, *outs):
    total = held[...] + got[...].astype(F32)
    rows = outs[0].shape[0]
    for chain, out in enumerate(outs):
        out[...] = total[chain * rows : (chain + 1) * rows, :].astype(BF16)


def add_kernel(held, got, *rest, scale):
    rest[-1][...] = ((held[...].astype(F32) + got[...].astype(F32)) * scale).astype(BF16)


def place_kernel(*refs, places):
    out, wide, sem = refs[-3:]
    rows = refs[0].shape[0]
    core = lax.axis_index(AXIS) % 2
    copies = []
    for k, (chain, own) in enumerate(places):
        wide[k] = refs[k][...].astype(F32)
        half = core if own else 1 - core
        begin = pl.multiple_of((2 * half + chain) * rows, rows)
        copies.append(pltpu.make_async_copy(wide.at[k], out.at[pl.ds(begin, rows), :], sem.at[k]))
        copies[-1].start()
    for copy in copies:
        copy.wait()


def sum_queries(kept, sent, beside, scale):
    count = lax.axis_size(AXIS)
    rows, width = kept.shape
    got = exchange(sent, 1)
    if count & (count - 1) or count < 8:
        half = kept + got.astype(F32)
        half = lax.psum(half, AXIS, axis_index_groups=[list(range(c, count, 2)) for c in range(2)])
        both = jnp.stack([half, exchange(half, 1)])
        both = jnp.where(lax.axis_index(AXIS) % 2 == 0, both, both[::-1])
        return both.reshape(2 * rows, width) * scale
    bits = [1 << k for k in range(1, count.bit_length() - 1)]
    orders = [bits, bits[-1:] + bits[:-1]]
    piece = in_vmem((rows // 2, width), BF16)
    held = list(call(halve_kernel, "halve", [VMEM] * 2, [piece, piece])(kept, got))
    swapped = []
    for k in range(len(bits)):
        last = k == len(bits) - 1
        got = [exchange(value, order[k]) for value, order in zip(held, orders)]
        for chain in range(2):
            after = beside[k : k + 1] if chain == 0 else held[:1] if last else []
            held[chain] = call(
                functools.partial(add_kernel, scale=scale if last else 1.0),
                "add",
                [VMEM] * 2 + [ANY] * len(after),
                piece,
                flops=2 * 10**8 if last else 0,
            )(held[chain], got[chain], *after)
    swapped = [exchange(value, 1) for value in held]

    def place(values, places, *begun):
        return call(
            functools.partial(place_kernel, places=places),
            "place",
            [VMEM] * len(values) + [ANY] * len(begun),
            jax.ShapeDtypeStruct((2 * rows, width), F32),
            out_specs=ANY,
            scratch=[
                pltpu.VMEM((len(values), rows // 2, width), F32),
                pltpu.SemaphoreType.DMA((len(values),)),
            ],
            aliases={len(values): 0} if begun else None,
        )(*values, *begun)

    early = place(held, [(0, True), (1, True)])
    return place(swapped, [(0, False), (1, False)], early)


def per_device(embeddings, edge_tiles, neighbour, propensity, queries, positives):
    count = lax.axis_size(AXIS)
    blocks, _, block, _ = edge_tiles.shape
    labels_dev, width = embeddings.shape
    rows = queries.shape[0]
    lists = neighbour.T
    odd = range(1, count, 2)
    off_route = [(i, (i + 1) % count) for i in odd] + [((i + 1) % count, i) for i in odd]

    def off_swap(value):
        return lax.ppermute(value, AXIS, off_route)

    def on_swap(value):
        return exchange(value, 1)

    one = in_vmem((rows, block), BF16)
    pair = in_vmem((2, rows, block), BF16)
    third = -(-2 * rows // 48) * 16
    thirds = [in_vmem((size, block), BF16) for size in (third, third, 2 * rows - 2 * third)]
    full = (blocks, rows, block)
    scale = 1.0 / math.sqrt(width)

    off_a, queries, embeddings, lists = call(
        functools.partial(project_kernel, scale=scale),
        "project",
        [HBM] * 3,
        [
            one,
            in_vmem(queries.shape, BF16),
            in_vmem(embeddings.shape, BF16),
            pltpu.SMEM(lists.shape, jnp.int32),
        ],
        out_specs=[VMEM] * 3 + [SMEM],
        scratch=[pltpu.SemaphoreType.DMA((2 + blocks,))],
    )(*(pltpu.with_memory_space_constraint(x, pltpu.HBM) for x in (lists, queries, embeddings)))
    from_off_a = off_swap(off_a)
    own, off_b, *for_on = call(
        functools.partial(own_kernel, scale=scale),
        "own",
        [SMEM, VMEM, VMEM],
        [in_vmem(full, F32), one] + thirds,
    )(lists, queries, embeddings)
    from_on = [on_swap(piece) for piece in for_on]
    hits, tiles = call(
        hits_kernel,
        "hits",
        [VMEM, HBM],
        [in_vmem(full, BF16), in_vmem(edge_tiles.shape, BF16)],
        scratch=[pltpu.SemaphoreType.DMA],
    )(positives.T, pltpu.with_memory_space_constraint(edge_tiles, pltpu.HBM))
    from_off_b = off_swap(off_b)
    base = call(
        base_kernel,
        "base",
        [SMEM] + [VMEM] * 5,
        in_vmem(full, F32),
        scratch=[pltpu.VMEM((2, rows, block), BF16)],
    )(lists, own, tiles, *from_on)
    propensity = propensity.reshape(1, labels_dev)

    def signal_of(received, slot, *begun):
        return call(
            functools.partial(signal_kernel, slot=slot),
            "signal",
            [SMEM] + [VMEM] * (5 + len(begun)),
            [in_vmem(full, BF16), one],
            scratch=[pltpu.VMEM((rows, block), F32)],
            aliases={6: 0} if begun else None,
            flops=0 if begun else 2 * 10**9,
        )(lists, base, hits, propensity, received, tiles, *begun)

    signal, push_a = signal_of(from_off_a, 0)
    back_a = off_swap(push_a)
    signal, push_b = signal_of(from_off_b, 1, signal)
    back_b = off_swap(push_b)
    push_on = call(
        push_kernel,
        "push",
        [SMEM, VMEM, VMEM],
        thirds,
        scratch=[pltpu.VMEM((2, rows, block), F32)],
    )(lists, signal, tiles)
    back_on = [on_swap(piece) for piece in push_on]

    whole = in_vmem((rows, width), F32)
    part = call(query_kernel, "query", [VMEM] * 2, whole)(signal, embeddings)
    part = call(
        functools.partial(query_half_kernel, blocks=blocks),
        "query_half",
        [SMEM] + [VMEM] * 3,
        whole,
        flops=10**9,
    )(lists, part, back_a, embeddings)
    part, on = call(
        functools.partial(query_on_kernel, blocks=blocks), "query_on", [SMEM] + [VMEM] * 5, [whole, pair]
    )(lists, part, embeddings, *back_on)
    ready = in_vmem((block, width), BF16)
    written = jax.ShapeDtypeStruct((labels_dev, width), BF16)

    def embed(turn, outs):
        values = [lists, signal, on, back_a, queries] + ([back_b] if turn == blocks - 1 else []) + outs[::-1]
        return call(
            functools.partial(embed_kernel, blocks=blocks, turn=turn, scale=1.0 / math.sqrt(rows)),
            "embed",
            [SMEM] + [VMEM] * (len(values) - 1 - (turn > 1)) + [ANY] * (turn > 1),
            ([written] if turn else []) + [ready, in_vmem((8, 128), F32)],
            out_specs=([ANY] if turn else []) + [VMEM] * 2,
            scratch=[pltpu.VMEM((rows, block), F32)] + ([pltpu.SemaphoreType.DMA((2,))] if turn else []),
            aliases={len(values) - 1: 0} if turn > 1 else None,
        )(*values)

    outs, tokens = [], []
    for turn in range(blocks // 2):
        *outs, token = embed(turn, outs)
        tokens.append(token)

    def query_end(own, kind):
        return call(
            functools.partial(query_end_kernel, blocks=blocks, own=own),
            "query_end",
            [SMEM] + [VMEM] * 3 + [ANY],
            in_vmem((rows // 2, width), kind),
        )(lists, part, back_b, embeddings, tokens[blocks // 2 - 1])

    sent, kept = query_end(False, BF16), query_end(True, F32)
    for turn in range(blocks // 2, blocks):
        *outs, token = embed(turn, outs)
        tokens.append(token)
    grad_embed = outs[0]
    grad_queries = sum_queries(kept, sent, tokens[blocks // 2 :], 1.0 / math.sqrt(labels_dev * count))
    return (grad_embed, grad_queries)


def solution(mesh):
    placed = (
        P("labels", None),
        P("labels", None, None, None),
        P(),
        P("labels"),
        P("groups", None),
        P("groups", None),
    )
    return jax.shard_map(
        per_device,
        mesh=mesh,
        in_specs=placed,
        out_specs=(P(("groups", "labels"), None), P("groups", None)),
        check_vma=False,
    )
```
